32 devices in a mesh: dp: 8 (over y, x, core), tensor: 4 (over z).
Axes of the slice: x: 2, y: 2, z: 4, core: 2. Of those that a mesh axis runs over, the one named last changes fastest.
Arguments:
- x_in: bfloat16 [8192, 1536], P(('dp', 'tensor')), may hold values from -6 to 6
- segments: int32 [8192], P('dp'), may hold values from 0 to 2, as said below
- norm_gain: float32 [2, 1536], replicated, may hold values from 0.5 to 1.5
- w_z: bfloat16 [2, 1536, 3072], P(None, 'dp', 'tensor'), may hold values from -0.15625 to 0.15625
- w_x: bfloat16 [2, 1536, 3072], P(None, 'dp', 'tensor'), may hold values from -0.15625 to 0.15625
- w_bc: bfloat16 [2, 1536, 256], P(None, 'dp'), may hold values from -0.15625 to 0.15625
- w_dt: bfloat16 [2, 1536, 48], P(None, 'dp', 'tensor'), may hold values from -0.15625 to 0.15625
- conv_x: float32 [2, 4, 3072], P(None, None, 'tensor'), may hold values from -3 to 3
- conv_x_bias: float32 [2, 3072], P(None, 'tensor'), may hold values from -0.5 to 0.5
- conv_bc: float32 [2, 4, 256], replicated, may hold values from -3 to 3
- conv_bc_bias: float32 [2, 256], replicated, may hold values from -0.5 to 0.5
- dt_bias: float32 [2, 48], P(None, 'tensor'), may hold values from -6 to -2
- a_log: float32 [2, 48], P(None, 'tensor'), may hold values from 0 to 2.7
- d_skip: float32 [2, 48], P(None, 'tensor'), may hold values from 0.5 to 1.5
- gate_gain: float32 [2, 3072], P(None, 'tensor'), may hold values from 0.5 to 1.5
- w_out: bfloat16 [2, 3072, 1536], P(None, 'tensor', 'dp'), may hold values from -0.109375 to 0.109375
- cotangent: float32 [8192, 1536], P(('dp', 'tensor')), may hold values from -6 to 6
Outputs:
- y_out: float32 [8192, 1536], P(('dp', 'tensor'))
- grad_in: float32 [8192, 1536], P(('dp', 'tensor'))
- g_norm_gain: float32 [2, 1536], replicated
- g_w_z: float32 [2, 1536, 3072], P(None, 'dp', 'tensor')
- g_w_x: float32 [2, 1536, 3072], P(None, 'dp', 'tensor')
- g_w_bc: float32 [2, 1536, 256], P(None, 'dp')
- g_w_dt: float32 [2, 1536, 48], P(None, 'dp', 'tensor')
- g_conv_x: float32 [2, 4, 3072], P(None, None, 'tensor')
- g_conv_x_bias: float32 [2, 3072], P(None, 'tensor')
- g_conv_bc: float32 [2, 4, 256], replicated
- g_conv_bc_bias: float32 [2, 256], replicated
- g_dt_bias: float32 [2, 48], P(None, 'tensor')
- g_a_log: float32 [2, 48], P(None, 'tensor')
- g_d_skip: float32 [2, 48], P(None, 'tensor')
- g_gate_gain: float32 [2, 3072], P(None, 'tensor')
- g_w_out: float32 [2, 3072, 1536], P(None, 'tensor', 'dp')
The draws below stay inside these ranges and needn't reach their ends.
Inputs may be any that keep to these rules, and one draw needn't show every extreme that they name: `segments`: each sequence of 1024 tokens holds three documents numbered 0, 1, 2 in order (the first and last cut by the packing, each non-empty); document 1 starts within the first 256 tokens, ends within the last 256 tokens and is at most 1000 / 1024 of 1024 tokens long.
All inputs are finite; a program needn't handle non-finite values.
Results may differ from the reference program's by a relative error of at most 0.034.
Values may be sent and summed in bfloat16 or wider, within the bound.
No kernel may reach another device: no remote copies, remote signals or barrier semaphores. Data moves between devices by JAX's collectives and lax.ppermute only.
A program may use at most 256 MiB of HBM per device.

```python
import jax
import jax.numpy as jnp
from jax import lax

D = 1536
INNER = 3072
HEADS = 48
HEADDIM = 64
STATE = 128
CONV = 4
STRETCH = 256
LAYERS = 2
SEQ_LEN = 1024
TOK_DEV = 256
TOKENS = 8192
N_TENSOR = 4


def draw_segments(key, part):
    key = jax.random.fold_in(key, 11)
    seq_count = TOKENS // SEQ_LEN
    length_key, start_key = jax.random.split(key)
    longest = min(SEQ_LEN * 1000 // 1024, SEQ_LEN - 2)
    doc_length = jax.random.randint(length_key, (seq_count, 1), SEQ_LEN - TOK_DEV + 1, longest + 1)
    start_lowest = jnp.maximum(1, SEQ_LEN - TOK_DEV + 1 - doc_length)
    start_highest = jnp.minimum(TOK_DEV - 1, SEQ_LEN - 1 - doc_length)
    first_start = jax.random.randint(start_key, (seq_count, 1), start_lowest, start_highest + 1)
    second_start = first_start + doc_length
    position = jnp.arange(SEQ_LEN, dtype=jnp.int32)[None, :]
    numbers = (position >= first_start).astype(jnp.int32) + (position >= second_start).astype(jnp.int32)
    return numbers.reshape(TOKENS)


def steps_of(key, dims, shards, smallest, high):
    def one(dim, parts):
        steps = jax.random.uniform(jax.random.fold_in(jax.random.fold_in(key, 6), dim), (parts,), jnp.float32, smallest / len(shards), high / len(shards))
        return jnp.repeat(jnp.exp(steps), dims[dim] // parts).reshape((-1,) + (1,) * (len(dims) - dim - 1))

    factor_of = one(*shards[0])
    for cut in shards[1:]:
        factor_of = factor_of * one(*cut)
    return factor_of


def normal_values(stream_key, extent, width, limit, pieces=(), kind=jnp.bfloat16):
    values = jax.random.normal(stream_key, extent, jnp.float32) * width
    if len(pieces) > 0:
        values = steps_of(stream_key, extent, pieces, -0.22, 0.18) * values
    return jnp.clip(values, min=-limit, max=limit).astype(kind)


def setup_inputs(seed: int = 0) -> dict:
    keys = jax.random.split(jax.random.key(seed), 18)
    x_in = normal_values(keys[0], (TOKENS, D), 1.0, 6.0, ((0, 32),))
    segments = draw_segments(jax.random.fold_in(keys[17], 71), 0)
    norm_gain = jnp.clip(1.0 + 0.1 * jax.random.normal(keys[2], (LAYERS, D), jnp.float32), 0.5, 1.5)
    w_z = normal_values(keys[3], (LAYERS, D, INNER), D ** -0.5, 0.15625, ((1, 8), (2, 4)))
    w_x = normal_values(keys[4], (LAYERS, D, INNER), D ** -0.5, 0.15625, ((1, 8), (2, 4)))
    w_bc = normal_values(keys[5], (LAYERS, D, 2 * STATE), D ** -0.5, 0.15625, ((1, 8),))
    w_dt = normal_values(keys[6], (LAYERS, D, HEADS), D ** -0.5, 0.15625, ((1, 8), (2, 4)))
    conv_x = normal_values(keys[7], (LAYERS, CONV, INNER), CONV ** -0.5, 3.0, ((2, 4),), jnp.float32)
    conv_x_bias = jnp.clip(jax.random.uniform(keys[8], (LAYERS, INNER), jnp.float32, -0.5, 0.5) * steps_of(keys[8], (LAYERS, INNER), ((1, 4),), -0.4, 0.0), -0.5, 0.5)
    conv_bc = normal_values(keys[9], (LAYERS, CONV, 2 * STATE), CONV ** -0.5, 3.0, (), jnp.float32)
    conv_bc_bias = jnp.clip(jax.random.uniform(keys[10], (LAYERS, 2 * STATE), jnp.float32, -0.5, 0.5), -0.5, 0.5)
    dt_bias = jnp.clip(-6.0 + 4.0 * jax.random.uniform(keys[11], (LAYERS, HEADS), jnp.float32) ** steps_of(keys[11], (LAYERS, HEADS), ((1, 4),), -0.2, 0.2), -6.0, -2.0)
    a_log = jnp.clip(2.7 * jax.random.uniform(keys[12], (LAYERS, HEADS), jnp.float32) ** steps_of(keys[12], (LAYERS, HEADS), ((1, 4),), -0.2, 0.2), 0.0, 2.7)
    d_skip = jnp.clip(0.5 + 1.0 * jax.random.uniform(keys[13], (LAYERS, HEADS), jnp.float32) ** steps_of(keys[13], (LAYERS, HEADS), ((1, 4),), -0.2, 0.2), 0.5, 1.5)
    gate_gain = jnp.clip(1.0 + 0.1 * jax.random.normal(keys[14], (LAYERS, INNER), jnp.float32), 0.5, 1.5)
    w_out = normal_values(keys[15], (LAYERS, INNER, D), INNER ** -0.5, 0.109375, ((1, 4), (2, 8)))
    cotangent = normal_values(keys[16], (TOKENS, D), 1.0, 6.0, ((0, 32),), jnp.float32)
    return {"x_in": x_in, "segments": segments, "norm_gain": norm_gain, "w_z": w_z, "w_x": w_x, "w_bc": w_bc, "w_dt": w_dt, "conv_x": conv_x, "conv_x_bias": conv_x_bias, "conv_bc": conv_bc, "conv_bc_bias": conv_bc_bias, "dt_bias": dt_bias, "a_log": a_log, "d_skip": d_skip, "gate_gain": gate_gain, "w_out": w_out, "cotangent": cotangent}


EPSILON = 1e-05
HIGH = lax.Precision.HIGHEST

@jax.custom_vjp
def low(v):
    return lax.optimization_barrier(v.astype(jnp.bfloat16)).astype(jnp.float32)

@jax.custom_vjp
def low_back(v):
    return v

def low_keep(v):
    return (low(v), None)

def low_pass(kept, grad):
    return (grad,)

def back_keep(v):
    return (v, None)

def back_low(kept, grad):
    return (low(grad),)
low.defvjp(low_keep, low_pass)
low_back.defvjp(back_keep, back_low)

def shifted_conv(values, kernel, offset, seg_rows):
    length = values.shape[0]
    width_taps = kernel.shape[0]
    summed = offset[None, :] + kernel[width_taps - 1][None, :] * values
    for lag_steps in range(1, width_taps):
        earlier = jnp.pad(values, ((lag_steps, 0), (0, 0)))[:length]
        earlier_seg = jnp.pad(seg_rows, (lag_steps, 0), constant_values=-1)[:length]
        allowed = (earlier_seg == seg_rows).astype(jnp.float32)[:, None]
        summed = summed + kernel[width_taps - 1 - lag_steps][None, :] * earlier * allowed
    return summed

def scan_state(x_heads, b_rows, c_rows, step_size, decay_rates, seg_rows):
    length, head_count, head_size = x_heads.shape
    block_count = length // STRETCH
    log_decay = -step_size * decay_rates[None, :]
    x_blocks = x_heads.reshape(block_count, STRETCH, head_count, head_size)
    b_blocks = b_rows.reshape(block_count, STRETCH, b_rows.shape[1])
    c_blocks = c_rows.reshape(block_count, STRETCH, c_rows.shape[1])
    step_blocks = step_size.reshape(block_count, STRETCH, head_count)
    seg_blocks = seg_rows.reshape(block_count, STRETCH)
    cumulative = jnp.cumsum(log_decay.reshape(block_count, STRETCH, head_count), axis=1)
    position = jnp.arange(STRETCH)
    allowed = (seg_blocks[:, :, None] == seg_blocks[:, None, :]) & (position[:, None] >= position[None, :])[None]
    spread = cumulative[:, :, None, :] - cumulative[:, None, :, :]
    decays = jnp.exp(jnp.where(allowed[..., None], spread, -1e+30))
    scores = jnp.einsum('ktn,ksn->kts', c_blocks, b_blocks, precision=HIGH)
    weights = scores[..., None] * decays * step_blocks[:, None, :, :]
    within = jnp.einsum('ktsh,kshp->kthp', weights, x_blocks, precision=HIGH)
    block_end = cumulative[:, -1, :]
    end_seg = seg_blocks[:, -1]
    tail_keep = (seg_blocks == end_seg[:, None]).astype(jnp.float32)
    state_gain = jnp.exp(block_end[:, None, :] - cumulative) * step_blocks * tail_keep[:, :, None]
    states = jnp.einsum('ksh,ksn,kshp->khnp', state_gain, b_blocks, x_blocks, precision=HIGH)
    before_seg = jnp.concatenate([jnp.full((1,), -1, jnp.int32), end_seg[:-1].astype(jnp.int32)])
    carry_link = jnp.exp(block_end) * (end_seg == before_seg).astype(jnp.float32)[:, None]

    def advance(running, element):
        link_now, state_now = element
        return (link_now[:, None, None] * running + state_now, running)
    start_state = jnp.zeros(states.shape[1:], jnp.float32)
    incoming = lax.scan(advance, start_state, (carry_link, states))[1]
    entry_gain = jnp.exp(cumulative) * (seg_blocks == before_seg[:, None]).astype(jnp.float32)[:, :, None]
    carried = jnp.einsum('kth,ktn,khnp->kthp', entry_gain, c_blocks, incoming, precision=HIGH)
    return (within + carried).reshape(length, head_count, head_size)

def mixer_core(x_rows, bc_rows, step_size, a_log_row, skip_row, seg_rows):
    length, inner_dev = x_rows.shape
    x_heads = x_rows.reshape(length, inner_dev // HEADDIM, HEADDIM)
    mixed_heads = scan_state(x_heads, bc_rows[:, :STATE], bc_rows[:, STATE:], step_size, jnp.exp(a_log_row), seg_rows)
    return (mixed_heads + skip_row[None, :, None] * x_heads).reshape(length, inner_dev)

def front_part(raw_rows, layer_consts, seg_rows):
    conv_xw, conv_xb, conv_bcw, conv_bcb, bias_dt = layer_consts
    inner_dev = conv_xw.shape[1]
    x_rows = jax.nn.silu(shifted_conv(raw_rows[:, :inner_dev], conv_xw, conv_xb, seg_rows))
    bc_rows = jax.nn.silu(shifted_conv(raw_rows[:, inner_dev:inner_dev + 2 * STATE], conv_bcw, conv_bcb, seg_rows))
    step_size = jax.nn.softplus(raw_rows[:, inner_dev + 2 * STATE:] + bias_dt[None, :])
    return (x_rows, bc_rows, step_size)

def one_layer(residual, seg_rows, layer_params):
    gain_norm, wz_all, wx_all, wbc_all, wdt_all, convx_all, convxb_all, convbc_all, convbcb_all, dtb_all, alog_all, skip_all, gain_gate, wout_all = layer_params
    inv_rms = lax.rsqrt(lax.optimization_barrier(jnp.mean(residual * residual, axis=-1, keepdims=True)) + EPSILON)
    normed = low(residual * inv_rms * gain_norm[None, :])
    inner_dev = INNER // N_TENSOR
    head_span = HEADS // N_TENSOR
    gated_parts = []
    for group_index in range(N_TENSOR):
        columns = slice(group_index * inner_dev, (group_index + 1) * inner_dev)
        heads_here = slice(group_index * head_span, (group_index + 1) * head_span)
        in_weight = jnp.concatenate([wz_all[:, columns], wx_all[:, columns], wbc_all, wdt_all[:, heads_here]], axis=1)
        projected = low_back(jnp.dot(low_back(normed), in_weight, precision=HIGH))
        layer_consts = (convx_all[:, columns], convxb_all[columns], convbc_all, convbcb_all, dtb_all[heads_here])
        x_rows, bc_rows, step_size = front_part(projected[:, inner_dev:], layer_consts, seg_rows)
        core_out = low_back(mixer_core(low(x_rows), low(bc_rows), step_size, alog_all[heads_here], skip_all[heads_here], seg_rows))
        gated_parts.append(core_out * jax.nn.silu(projected[:, :inner_dev]))
    squares = lax.optimization_barrier(jnp.sum(gated_parts[0] * gated_parts[0], axis=-1))
    for group_index in range(1, N_TENSOR):
        squares = squares + lax.optimization_barrier(jnp.sum(gated_parts[group_index] * gated_parts[group_index], axis=-1))
    inv_gate = lax.rsqrt(squares / INNER + EPSILON)
    mixed_sum = jnp.zeros_like(residual)
    for group_index in range(N_TENSOR):
        columns = slice(group_index * inner_dev, (group_index + 1) * inner_dev)
        gnormed = low(gated_parts[group_index] * inv_gate[:, None] * gain_gate[columns][None, :])
        mixed_sum = mixed_sum + low(jnp.dot(gnormed, wout_all[columns], precision=HIGH))
    return residual + low_back(mixed_sum)

def reference(x_in, segments, norm_gain, w_z, w_x, w_bc, w_dt, conv_x, conv_x_bias, conv_bc, conv_bc_bias, dt_bias, a_log, d_skip, gate_gain, w_out, cotangent):
    parameters = tuple((array.astype(jnp.float32) for array in (norm_gain, w_z, w_x, w_bc, w_dt, conv_x, conv_x_bias, conv_bc, conv_bc_bias, dt_bias, a_log, d_skip, gate_gain, w_out)))
    seq_count = TOKENS // SEQ_LEN
    inputs = x_in.astype(jnp.float32).reshape(seq_count, SEQ_LEN, D)
    seg_all = segments.astype(jnp.int32).reshape(seq_count, SEQ_LEN)
    cot_all = cotangent.astype(jnp.float32).reshape(seq_count, SEQ_LEN, D)

    def forward(values, seg_rows, layer_params):
        for layer_index in range(LAYERS):
            values = one_layer(values, seg_rows, tuple((array[layer_index] for array in layer_params)))
        return values

    def per_sequence(totals, element):
        values, seg_rows, cot_rows = element
        result, pullback = jax.vjp(lambda first_arg, second_arg: forward(first_arg, seg_rows, second_arg), values, parameters)
        grad_values, grad_params = pullback(cot_rows)
        return (jax.tree.map(jnp.add, totals, grad_params), (result, grad_values))
    start_totals = jax.tree.map(jnp.zeros_like, parameters)
    totals, (results, grad_rows) = lax.scan(per_sequence, start_totals, (inputs, seg_all, cot_all))
    return (results.reshape(TOKENS, D), grad_rows.reshape(TOKENS, D), totals[0], totals[1], totals[2], totals[3], totals[4], totals[5], totals[6], totals[7], totals[8], totals[9], totals[10], totals[11], totals[12], totals[13])
```

```python
import functools

import jax
import jax.numpy as jnp
import numpy as np
from jax import lax
from jax.experimental import pallas as pl
from jax.experimental.pallas import tpu as pltpu
from jax.sharding import PartitionSpec as P

INNER = 3072
HEADDIM = 64
STATE = 128
LAYERS = 2
EPSILON = 1e-05
HALO = 16
CHUNK = 128
LANES = 128

BF = jnp.bfloat16
F32 = jnp.float32
EXACT = lax.Precision.HIGHEST
VMEM_BYTES = 50 * 1024 * 1024


def dot(left, right, dims=((1,), (0,)), precision=None):
    return lax.dot_general(
        left, right, (dims, ((), ())), preferred_element_type=F32, precision=precision
    )


def split(values):
    high = values.astype(BF)
    return high, (values - high.astype(F32)).astype(BF)


def spread(values, e2_ref):
    return dot(jnp.concatenate(split(values), axis=1), e2_ref[...])


def head_sum(values, hm_ref):
    high, low = split(values)
    return dot(high, hm_ref[...]) + dot(low, hm_ref[...])


def softplus(values):
    return jnp.maximum(values, 0.0) + jnp.log1p(jnp.exp(-jnp.abs(values)))


def triangle(size, lower):
    rows = lax.broadcasted_iota(jnp.int32, (size, size), 0)
    cols = lax.broadcasted_iota(jnp.int32, (size, size), 1)
    return rows >= cols if lower else rows <= cols


def convolve(window, marks, cw, lanes):
    size = window.shape[0] - 8
    total = cw[4:5, lanes] + cw[3:4, lanes] * window[8:]
    for lag in (1, 2, 3):
        earlier = window[8 - lag : 8 - lag + size]
        total = total + cw[3 - lag : 4 - lag, lanes] * (earlier * marks[:, lag - 1 : lag])
    return total


def front_kernel(
    raw_ref, cm_ref, lnk_ref, cw_ref, hp_ref, e2_ref,
    xb_ref, aux_ref, sloc_ref, send_ref, state_ref,
    *, inner,
):
    count = xb_ref.shape[0]
    lower = triangle(CHUNK, True).astype(F32)
    state_ref[...] = jnp.zeros_like(state_ref)

    def step_chunk(k, carry):
        base = pl.multiple_of(k * CHUNK, CHUNK)
        here = pl.ds(base, CHUNK)
        marks = cm_ref[pl.ds(base + HALO, CHUNK), :]
        for low in range(0, inner + 2 * STATE, STATE):
            lanes = slice(low, low + STATE)
            window = raw_ref[pl.ds(base + HALO - 8, CHUNK + 8), lanes]
            pre = convolve(window, marks, cw_ref, lanes)
            xb_ref[here, lanes] = (pre * jax.nn.sigmoid(pre)).astype(BF)
        raw_dt = raw_ref[pl.ds(base + HALO, CHUNK), inner + 2 * STATE :]
        step = softplus(raw_dt + hp_ref[0:1, :])
        cum = dot(lower, -hp_ref[1:2, :] * step, precision=EXACT)
        aux_ref[here, :LANES] = step
        aux_ref[here, LANES:] = cum
        end = cum[CHUNK - 1 :, :]
        gain = jnp.exp(end - cum) * marks[:, 3:4] * step
        scaled = (spread(gain, e2_ref) * xb_ref[here, :inner].astype(F32)).astype(BF)
        b_rows = xb_ref[here, inner : inner + STATE]
        local = dot(b_rows, scaled, ((0,), (0,)))
        keep = spread(jnp.exp(end) * lnk_ref[pl.ds(k * 8, 8), :], e2_ref)[0:1]
        sloc_ref[k] = state_ref[...]
        state_ref[...] = keep * state_ref[...] + local
        return carry

    lax.fori_loop(0, count // CHUNK, step_chunk, 0)
    send_ref[...] = state_ref[...].astype(BF)


def scan_kernel(
    xb_ref, aux_ref, sloc_ref, send_ref, sin_ref, z_ref, cm_ref, segr_ref, lnk_ref, gp_ref, e2_ref,
    core_ref, act_ref, ssq_ref, sst_ref, decay_ref,
    *, inner,
):
    count = xb_ref.shape[0]
    lower = triangle(CHUNK, True)
    first = lax.broadcasted_iota(jnp.int32, (CHUNK, STATE), 1) < HEADDIM
    decay_ref[...] = jnp.ones_like(decay_ref)

    def step_chunk(k, carry):
        base = pl.multiple_of(k * CHUNK, CHUNK)
        here = pl.ds(base, CHUNK)
        there = pl.ds(base + HALO, CHUNK)
        marks = cm_ref[there, :]
        incoming = (sloc_ref[k] + decay_ref[0:1, :] * sin_ref[...].astype(F32)).astype(BF)
        sst_ref[k] = incoming
        b_rows = xb_ref[here, inner : inner + STATE]
        c_rows = xb_ref[here, inner + STATE : inner + 2 * STATE]
        scores = dot(c_rows, b_rows, ((1,), (1,)))
        allowed = (marks[:, 5:6] == segr_ref[0:1, here]) & lower
        scores = jnp.where(allowed, scores, 0.0)
        step = aux_ref[here, :LANES]
        cum = aux_ref[here, LANES:]
        cum_t = jnp.transpose(cum)
        step_wide = spread(step, e2_ref)
        carried = spread(jnp.exp(cum) * marks[:, 4:5], e2_ref) * dot(c_rows, incoming)
        squares = jnp.zeros((CHUNK, STATE), F32)
        for pair in range(inner // STATE):
            lanes = slice(pair * STATE, (pair + 1) * STATE)
            x_rows = xb_ref[here, lanes].astype(F32)
            scaled = step_wide[:, lanes] * x_rows
            within = carried[:, lanes] + gp_ref[1:2, lanes] * x_rows
            for half in range(2):
                head = 2 * pair + half
                decay = jnp.exp(
                    jnp.minimum(cum[:, head : head + 1] - cum_t[head : head + 1, :], 0.0)
                )
                mine = first if half == 0 else ~first
                part = jnp.where(mine, scaled, 0.0).astype(BF)
                within = within + dot((scores * decay).astype(BF), part)
            core_ref[here, lanes] = within
            z_rows = z_ref[there, lanes]
            gated = within * (z_rows * jax.nn.sigmoid(z_rows))
            act_ref[here, lanes] = (gated * gp_ref[0:1, lanes]).astype(BF)
            squares = squares + gated * gated
        total = jnp.sum(jnp.transpose(squares), axis=0, keepdims=True)
        ssq_ref[:, here] = jnp.broadcast_to(total, (8, CHUNK))
        end = cum[CHUNK - 1 :, :]
        keep = spread(jnp.exp(end) * lnk_ref[pl.ds(k * 8, 8), :], e2_ref)
        decay_ref[...] = decay_ref[...] * keep
        return carry

    chunks = count // CHUNK
    lax.fori_loop(0, chunks, step_chunk, 0)
    last = send_ref[...].astype(F32) + decay_ref[0:1, :] * sin_ref[...].astype(F32)
    sst_ref[chunks] = last.astype(BF)


def gate_back_kernel(
    gg_ref, core_ref, z_ref, coef_ref, xb_ref, aux_ref, cm_ref, lnk_ref, gp_ref, e2_ref,
    gcore_ref, gz_ref, ggain_ref, dsin_ref, state_ref,
    *, inner,
):
    count = xb_ref.shape[0]
    chunks = count // CHUNK
    state_ref[...] = jnp.zeros_like(state_ref)
    ggain_ref[...] = jnp.zeros_like(ggain_ref)
    gz_ref[:HALO, :] = jnp.zeros((HALO, inner), BF)

    def step_chunk(turn, carry):
        k = chunks - 1 - turn
        base = pl.multiple_of(k * CHUNK, CHUNK)
        here = pl.ds(base, CHUNK)
        there = pl.ds(base + HALO, CHUNK)
        marks = cm_ref[there, :]
        coef = coef_ref[here, 0:1]
        cum = aux_ref[here, LANES:]
        entry = spread(jnp.exp(cum) * marks[:, 4:5], e2_ref)
        c_rows = xb_ref[here, inner + STATE : inner + 2 * STATE]
        end = cum[CHUNK - 1 :, :]
        keep = spread(jnp.exp(end) * lnk_ref[pl.ds(k * 8, 8), :], e2_ref)[0:1]
        for pair in range(inner // STATE):
            lanes = slice(pair * STATE, (pair + 1) * STATE)
            z_rows = z_ref[there, lanes]
            core = core_ref[here, lanes]
            grad = gg_ref[here, lanes]
            sig = jax.nn.sigmoid(z_rows)
            act = z_rows * sig
            gated = core * act
            ggain_ref[0:1, lanes] += jnp.sum(grad * gated, axis=0, keepdims=True)
            grad_gated = gp_ref[0:1, lanes] * grad - coef * gated
            gcore = (grad_gated * act).astype(BF)
            gcore_ref[here, lanes] = gcore
            gz_ref[there, lanes] = (
                grad_gated * core * (sig * (1.0 + z_rows * (1.0 - sig)))
            ).astype(BF)
            scaled = (entry[:, lanes] * gcore.astype(F32)).astype(BF)
            state_ref[:, lanes] = keep[:, lanes] * state_ref[:, lanes] + dot(
                c_rows, scaled, ((0,), (0,))
            )
        return carry

    lax.fori_loop(0, chunks, step_chunk, 0)
    dsin_ref[...] = state_ref[...].astype(BF)


def scan_back_kernel(
    gcore_ref, xb_ref, aux_ref, core_ref, sst_ref, dso_ref, raw_ref, cm_ref, segr_ref, lnk_ref,
    gp_ref, cw_ref, hp_ref, e2_ref, hm_ref,
    graw_ref, sgrad_ref, hgrad_ref, state_ref, dpre_ref, qv_ref, xd_ref,
    *, inner,
):
    count = xb_ref.shape[0]
    chunks = count // CHUNK
    wide = inner + 2 * STATE
    upper = triangle(CHUNK, False)
    first = lax.broadcasted_iota(jnp.int32, (CHUNK, STATE), 1) < HEADDIM
    state_ref[...] = dso_ref[...].astype(F32)
    sgrad_ref[...] = jnp.zeros_like(sgrad_ref)
    hgrad_ref[...] = jnp.zeros_like(hgrad_ref)
    dpre_ref[:HALO, :] = jnp.zeros((HALO, wide), F32)
    dpre_ref[HALO + count :, :] = jnp.zeros((HALO, wide), F32)
    graw_ref[:HALO, wide:] = jnp.zeros((HALO, LANES), BF)

    def step_chunk(turn, carry):
        k = chunks - 1 - turn
        base = pl.multiple_of(k * CHUNK, CHUNK)
        here = pl.ds(base, CHUNK)
        there = pl.ds(base + HALO, CHUNK)
        marks = cm_ref[there, :]
        step = aux_ref[here, :LANES]
        cum = aux_ref[here, LANES:]
        cum_t = jnp.transpose(cum)
        end = cum[CHUNK - 1 :, :]
        b_rows = xb_ref[here, inner : inner + STATE]
        c_rows = xb_ref[here, inner + STATE : wide]
        after = state_ref[...]
        after_low = after.astype(BF)
        product = jnp.sum(
            sst_ref[k + 1].astype(F32) * after_low.astype(F32), axis=0, keepdims=True
        )
        at_end = head_sum(jnp.broadcast_to(product, (8, inner)), hm_ref)[0:1]
        scores_t = dot(b_rows, c_rows, ((1,), (1,)))
        allowed = (marks[:, 5:6] == segr_ref[0:1, here]) & upper
        scores_t = jnp.where(allowed, scores_t, 0.0)
        gain = spread(jnp.exp(end - cum) * marks[:, 3:4], e2_ref)
        step_wide = spread(step, e2_ref)
        entry = spread(jnp.exp(cum) * marks[:, 4:5], e2_ref)
        keep = spread(jnp.exp(end) * lnk_ref[pl.ds(k * 8, 8), :], e2_ref)[0:1]
        outer = gain * dot(b_rows, after_low)
        scaled_grad = (entry * gcore_ref[here, :].astype(F32)).astype(BF)
        grad_c = dot(scaled_grad, sst_ref[k], ((1,), (1,)))
        scaled_x = (gain * (step_wide * xb_ref[here, :inner].astype(F32))).astype(BF)
        grad_b = dot(scaled_x, after_low, ((1,), (1,)))
        state_ref[...] = keep * after + dot(c_rows, scaled_grad, ((0,), (0,)))
        grad_scores = jnp.zeros((CHUNK, CHUNK), F32)
        for pair in range(inner // STATE):
            lanes = slice(pair * STATE, (pair + 1) * STATE)
            grad_low = gcore_ref[here, lanes]
            grad = grad_low.astype(F32)
            x_rows = xb_ref[here, lanes].astype(F32)
            wide_step = step_wide[:, lanes]
            scaled = wide_step * x_rows
            grad_u = outer[:, lanes]
            for half in range(2):
                head = 2 * pair + half
                decay = jnp.exp(
                    jnp.minimum(cum_t[head : head + 1, :] - cum[:, head : head + 1], 0.0)
                )
                mine = first if half == 0 else ~first
                part = jnp.where(mine, scaled, 0.0).astype(BF)
                grad_part = jnp.where(mine, grad, 0.0).astype(BF)
                grad_u = grad_u + dot((scores_t * decay).astype(BF), grad_part)
                grad_scores = grad_scores + dot(part, grad_low, ((1,), (1,))) * decay
            skip = gp_ref[1:2, lanes]
            qv_ref[:, lanes] = grad * (core_ref[here, lanes] - skip * x_rows) - (
                scaled.astype(BF).astype(F32) * grad_u
            )
            xd_ref[:, lanes] = x_rows * grad_u
            dpre_ref[there, lanes] = wide_step * grad_u + skip * grad
            sgrad_ref[5:6, lanes] += jnp.sum(grad * x_rows, axis=0, keepdims=True)
        grad_scores = jnp.where(allowed, grad_scores, 0.0).astype(BF)
        dpre_ref[there, inner : inner + STATE] = grad_b + dot(grad_scores, c_rows)
        dpre_ref[there, inner + STATE :] = grad_c + dot(grad_scores, b_rows, ((0,), (0,)))
        rate = hp_ref[1:2, :]
        grad_log = dot(upper.astype(F32), head_sum(qv_ref[...], hm_ref), precision=EXACT) + at_end
        grad_step = head_sum(xd_ref[...], hm_ref) - rate * grad_log
        raw_dt = raw_ref[there, wide:]
        grad_dt = grad_step * jax.nn.sigmoid(raw_dt + hp_ref[0:1, :])
        graw_ref[there, wide:] = grad_dt.astype(BF)
        hgrad_ref[0:1, :] += jnp.sum(grad_dt, axis=0, keepdims=True)
        hgrad_ref[1:2, :] -= rate * jnp.sum(step * grad_log, axis=0, keepdims=True)
        return carry

    lax.fori_loop(0, chunks, step_chunk, 0)

    def conv_chunk(k, carry):
        base = pl.multiple_of(k * CHUNK, CHUNK)
        there = pl.ds(base + HALO, CHUNK)
        marks = cm_ref[there, :]
        for low in range(0, wide, STATE):
            lanes = slice(low, low + STATE)
            window = raw_ref[pl.ds(base + HALO - 8, CHUNK + 8), lanes]
            pre = convolve(window, marks, cw_ref, lanes)
            sig = jax.nn.sigmoid(pre)
            grad = dpre_ref[there, lanes] * (sig * (1.0 + pre * (1.0 - sig)))
            dpre_ref[there, lanes] = grad
            sgrad_ref[4:5, lanes] += jnp.sum(grad, axis=0, keepdims=True)
            sgrad_ref[3:4, lanes] += jnp.sum(grad * window[8:], axis=0, keepdims=True)
            for lag in (1, 2, 3):
                earlier = window[8 - lag : 8 - lag + CHUNK]
                sgrad_ref[3 - lag : 4 - lag, lanes] += jnp.sum(
                    grad * (earlier * marks[:, lag - 1 : lag]), axis=0, keepdims=True
                )
        return carry

    lax.fori_loop(0, chunks, conv_chunk, 0)

    def transpose_rows(start, size):
        marks = cm_ref[pl.ds(start, size + 8), :]
        for low in range(0, wide, STATE):
            lanes = slice(low, low + STATE)
            window = dpre_ref[pl.ds(start, size + 8), lanes]
            total = cw_ref[3:4, lanes] * window[:size]
            for lag in (1, 2, 3):
                masked = window[lag : lag + size] * marks[lag : lag + size, lag - 1 : lag]
                total = total + cw_ref[3 - lag : 4 - lag, lanes] * masked
            graw_ref[pl.ds(start, size), lanes] = total.astype(BF)

    transpose_rows(0, HALO)

    def back_chunk(k, carry):
        transpose_rows(pl.multiple_of(k * CHUNK, CHUNK) + HALO, CHUNK)
        return carry

    lax.fori_loop(0, chunks, back_chunk, 0)


def run(kernel, operands, per_stream, outs, scratch, inner, flops):
    streams = 2

    def spec(shape, split_here):
        if split_here:
            return pl.BlockSpec((None,) + shape[1:], lambda s: (s,) + (0,) * (len(shape) - 1))
        return pl.BlockSpec(shape, lambda s: (0,) * len(shape))

    moved = sum(int(np.prod(v.shape)) * v.dtype.itemsize for v in operands)
    moved += sum(streams * int(np.prod(s)) * jnp.dtype(t).itemsize for s, t in outs)
    return pl.pallas_call(
        functools.partial(kernel, inner=inner),
        grid=(streams,),
        in_specs=[spec(v.shape, flag) for v, flag in zip(operands, per_stream)],
        out_specs=[spec((streams,) + s, True) for s, _ in outs],
        out_shape=[jax.ShapeDtypeStruct((streams,) + s, t) for s, t in outs],
        scratch_shapes=[pltpu.VMEM(s, t) for s, t in scratch],
        compiler_params=pltpu.CompilerParams(vmem_limit_bytes=VMEM_BYTES),
        cost_estimate=pl.CostEstimate(flops=flops, bytes_accessed=moved, transcendentals=0),
    )(*operands)


def build(n_dp, n_tensor):
    axes = ("dp", "tensor")
    half_size = n_tensor // 2
    planes = [[d for d in range(n_dp) if d % 2 == c] for c in range(2)]

    def pairs(route):
        found = []
        for d in range(n_dp):
            for t in range(n_tensor):
                goal = route(d, t)
                if goal is not None:
                    found.append((d * n_tensor + t, goal[0] * n_tensor + goal[1]))
        return found

    def send(value, route):
        return lax.ppermute(value, axes, pairs(route))

    def back(value, route):
        return lax.ppermute(value, axes, [(b, a) for a, b in pairs(route)])

    def to_core(d, t):
        return d ^ 1, t

    def to_piece(j):
        return lambda d, t: (d, (t // half_size) * half_size + ((t % half_size) ^ j))

    def to_later(d, t):
        return (d, t + half_size) if t < half_size else None

    def to_halo(j):
        return lambda d, t: (d, half_size + j) if t == half_size - 1 else None

    def to_group(turn):
        def route(d, t):
            return (d & ~1) | (t % 2), t // 2 + half_size * ((d & 1) ^ turn)

        return route

    def local(
        x_in, segments, norm_gain, w_z, w_x, w_bc, w_dt, conv_x, conv_x_bias, conv_bc, conv_bc_bias,
        dt_bias, a_log, d_skip, gate_gain, w_out, cotangent,
    ):
        inner = w_z.shape[2]
        heads = dt_bias.shape[1]
        piece, width = x_in.shape
        count = half_size * piece
        rows = count + HALO
        chunks = count // CHUNK
        shard = w_z.shape[1]
        wide = inner + 2 * STATE
        place = lax.axis_index("tensor")
        core = lax.axis_index("dp") % 2
        half = place // half_size
        mine = place % half_size

        def pad_lanes(value):
            return jnp.pad(value, ((0, 0), (0, LANES - value.shape[1])))

        def regroup(value):
            one, two = send(value, to_group(0)), send(value, to_group(1))
            return jnp.concatenate(
                [jnp.where(half == 0, one, two), jnp.where(half == 0, two, one)], axis=0
            )

        def over_plane(value):
            return lax.all_gather(value, "dp", axis=0, tiled=True, axis_index_groups=planes)

        def bc_rows(l):
            other = send(w_bc[l], to_core)
            return jnp.concatenate(
                [jnp.where(core == 0, w_bc[l], other), jnp.where(core == 0, other, w_bc[l])], axis=0
            )

        front_w, z_w, out_w = [], [], []
        for l in range(LAYERS):
            part = regroup(jnp.concatenate([w_x[l], pad_lanes(w_dt[l])], axis=1))
            front_w.append(
                over_plane(jnp.concatenate([part[:, :inner], bc_rows(l), part[:, inner:]], axis=1))
            )
            part = regroup(jnp.concatenate([w_z[l], w_out[l].T], axis=1))
            z_w.append(over_plane(part[:, :inner]))
            out_w.append(over_plane(part[:, inner:]))

        def row(value, size):
            return jnp.pad(value, ((0, 0), (0, size - value.shape[1])))[:, None]

        packed = jnp.concatenate(
            [conv_x, conv_x_bias[:, None], gate_gain[:, None]]
            + [jnp.concatenate([row(v, LANES) for v in (dt_bias, a_log, d_skip)], axis=2)
               if inner == 3 * LANES
               else jnp.pad(
                   jnp.concatenate([row(v, LANES) for v in (dt_bias, a_log, d_skip)], axis=2),
                   ((0, 0), (0, 0), (0, inner - 3 * LANES)))],
            axis=1,
        )
        packed = send(packed, to_group(0))
        taps, bias, gain_own = packed[:, :4], packed[:, 4:5], packed[:, 5:6]
        dt_own, a_own, skip_own = (packed[:, 6, i * LANES : (i + 1) * LANES] for i in range(3))
        head_ok = jnp.arange(LANES) < heads
        rate_own = jnp.where(head_ok, jnp.exp(a_own), 0.0)
        skip_wide = jnp.repeat(skip_own[:, :heads], HEADDIM, axis=1)
        conv_w = jnp.concatenate(
            [
                jnp.concatenate([taps, conv_bc], axis=2),
                jnp.concatenate([bias, conv_bc_bias[:, None]], axis=2),
                jnp.zeros((LAYERS, 3, wide), F32),
            ],
            axis=1,
        )
        gate_p = jnp.concatenate(
            [gain_own, skip_wide[:, None], jnp.zeros((LAYERS, 6, inner), F32)], axis=1
        )
        head_p = jnp.concatenate(
            [dt_own[:, None], rate_own[:, None], jnp.zeros((LAYERS, 6, LANES), F32)], axis=1
        )
        member = np.arange(inner)[None, :] // HEADDIM == np.arange(LANES)[:, None]
        e2 = jnp.asarray(np.concatenate([member, member], axis=0), BF)
        hm = jnp.asarray(member.T, BF)

        seg_own = jnp.concatenate([jnp.full((HALO,), -1.0, F32), segments.astype(F32)])
        seg_own = lax.dynamic_slice(seg_own, (half * count,), (rows,))
        seg = jnp.stack([seg_own, send(seg_own, to_core)])
        seg = jnp.where(
            (half == 0) & (jnp.arange(rows) < HALO)[None, :], -1.0, seg
        )
        tokens = seg[:, HALO:]
        lagged = [
            (tokens == seg[:, HALO - k : HALO - k + count]).astype(F32) for k in (1, 2, 3)
        ]
        by_chunk = tokens.reshape(2, chunks, CHUNK)
        last = by_chunk[:, :, -1]
        before = jnp.concatenate([seg[:, HALO - 1 : HALO], last[:, :-1]], axis=1)
        stays = (by_chunk == last[:, :, None]).astype(F32).reshape(2, count)
        enters = (by_chunk == before[:, :, None]).astype(F32).reshape(2, count)
        marks = jnp.stack(lagged + [stays, enters, tokens, tokens, tokens], axis=-1)
        marks = jnp.pad(marks, ((0, 0), (HALO, HALO), (0, 0)))
        seg_row = jnp.broadcast_to(tokens[:, None, :], (2, 8, count))
        links = (last == before).astype(F32)
        links = jnp.broadcast_to(links[:, :, None, None], (2, chunks, 8, LANES))
        links = links.reshape(2, chunks * 8, LANES)

        def gather(value, halo):
            offset = HALO if halo else 0
            block = jnp.zeros((offset + count,) + value.shape[1:], value.dtype)
            if halo:
                edge = value[piece - HALO :]
                came = send(edge, to_halo(0))
                for j in range(1, half_size):
                    came = came + send(edge, to_halo(j))
                block = lax.dynamic_update_slice(block, came, (0,) * value.ndim)
            rest = (0,) * (value.ndim - 1)
            parts = [value] + [send(value, to_piece(j)) for j in range(1, half_size)]
            for j, part in enumerate(parts):
                block = lax.dynamic_update_slice(
                    block, part, (offset + (mine ^ j) * piece,) + rest
                )
            return jnp.stack([block, send(block, to_core)])

        def scatter(own, other, halo):
            offset = HALO if halo else 0
            kind = own.dtype
            total = own.astype(F32) + send(other, to_core).astype(F32)
            rest = (0,) * (own.ndim - 1)
            size = (piece,) + own.shape[1:]

            def part_of(j):
                return lax.dynamic_slice(total, (offset + (mine ^ j) * piece,) + rest, size)

            result = part_of(0)
            for j in range(1, half_size):
                result = result + send(part_of(j).astype(kind), to_piece(j)).astype(F32)
            if halo:
                edge = total[:HALO].astype(kind)
                came = back(edge, to_halo(0)).astype(F32)
                for j in range(1, half_size):
                    came = came + back(edge, to_halo(j)).astype(F32)
                result = result.at[piece - HALO :].add(came)
            return result

        def matmul(left, right, dims):
            return lax.dot_general(left, right, (dims, ((), ())), preferred_element_type=F32)

        tok_flops = 2 * count

        residual = x_in.astype(F32)
        stored = []
        for l in range(LAYERS):
            inv_rms = lax.rsqrt(jnp.mean(residual * residual, axis=-1, keepdims=True) + EPSILON)
            normed = (residual * inv_rms * norm_gain[l][None, :]).astype(BF)
            toks = gather(normed, True)
            raw = matmul(toks, front_w[l], ((2,), (0,)))
            xb, aux, sloc, ends = run(
                front_kernel,
                [raw, marks, links, conv_w[l], head_p[l], e2],
                [True, True, True, False, False, False],
                [((count, wide), BF), ((count, 2 * LANES), F32),
                 ((chunks, STATE, inner), F32), ((STATE, inner), BF)],
                [((STATE, inner), F32)],
                inner,
                tok_flops * inner * STATE * 4,
            )
            begins = send(ends, to_later)
            z = matmul(toks, z_w[l], ((2,), (0,)))
            core_out, act, ssq, sst = run(
                scan_kernel,
                [xb, aux, sloc, ends, begins, z, marks, seg_row, links, gate_p[l], e2],
                [True, True, True, True, True, True, True, True, True, False, False],
                [((count, inner), F32), ((count, inner), BF), ((8, count), F32),
                 ((chunks + 1, STATE, inner), BF)],
                [((8, inner), F32)],
                inner,
                tok_flops * inner * STATE * 8,
            )
            part_other = matmul(act[1], out_w[l], ((1,), (1,))).astype(BF)
            part_own = matmul(act[0], out_w[l], ((1,), (1,))).astype(BF)
            squares = scatter(ssq[0, 0], ssq[1, 0], False)
            mixed = scatter(part_own, part_other, False)
            inv_gate = lax.rsqrt(squares / INNER + EPSILON)[:, None]
            stored.append(
                (residual, inv_rms, toks, raw, xb, aux, z, core_out, act, sst, mixed, inv_gate)
            )
            residual = residual + inv_gate * mixed
        output = residual

        def plane_sum(value):
            return lax.psum_scatter(
                value, "dp", scatter_dimension=0, tiled=True, axis_index_groups=planes
            )

        def ungroup(value):
            first_rows = lax.dynamic_slice(value, (half * shard, 0), (shard, value.shape[1]))
            other_rows = lax.dynamic_slice(value, ((1 - half) * shard, 0), (shard, value.shape[1]))
            one, two = back(first_rows, to_group(0)), back(other_rows, to_group(1))
            return one.astype(F32) + two.astype(F32)

        def over_tensor(value, kind):
            bit = 1
            while bit < n_tensor:
                value = value + send(value.astype(kind), lambda d, t: (d, t ^ bit)).astype(F32)
                bit *= 2
            return value

        gradient = cotangent
        found = [None] * LAYERS
        for l in reversed(range(LAYERS)):
            (residual, inv_rms, toks, raw, xb, aux, z, core_out, act, sst, mixed, inv_gate) = stored[l]
            scaled = (inv_gate * gradient).astype(BF)
            coef = inv_gate[:, 0] ** 2 * jnp.sum(scaled.astype(F32) * mixed, axis=-1) / INNER
            grows = gather(scaled, False)
            coefs = gather(coef, False)
            coefs = jnp.broadcast_to(coefs[:, :, None], (2, count, 8))
            gg = matmul(grows, out_w[l], ((2,), (0,)))
            gcore, gz, ggain, dsin = run(
                gate_back_kernel,
                [gg, core_out, z, coefs, xb, aux, marks, links, gate_p[l], e2],
                [True, True, True, True, True, True, True, True, False, False],
                [((count, inner), BF), ((rows, inner), BF), ((8, inner), F32),
                 ((STATE, inner), BF)],
                [((STATE, inner), F32)],
                inner,
                tok_flops * inner * STATE * 4,
            )
            dsout = back(dsin, to_later)
            g_out_w = matmul(grows, act, ((0, 1), (0, 1))).astype(BF)
            g_z_w = matmul(toks, gz, ((0, 1), (0, 1))).astype(BF)
            graw, sgrad, hgrad = run(
                scan_back_kernel,
                [gcore, xb, aux, core_out, sst, dsout, raw, marks, seg_row, links,
                 gate_p[l], conv_w[l], head_p[l], e2, hm],
                [True] * 10 + [False] * 5,
                [((rows, wide + LANES), BF), ((8, wide), F32), ((8, LANES), F32)],
                [((STATE, inner), F32), ((count + 2 * HALO, wide), F32),
                 ((CHUNK, inner), F32), ((CHUNK, inner), F32)],
                inner,
                tok_flops * inner * STATE * 16,
            )

            def normed_part(s):
                return (
                    matmul(gz[s], z_w[l], ((1,), (1,))) + matmul(graw[s], front_w[l], ((1,), (1,)))
                ).astype(BF)

            part_other = normed_part(1)
            part_own = normed_part(0)
            g_front_w = matmul(toks, graw, ((0, 1), (0, 1))).astype(BF)
            grad_normed = scatter(part_own, part_other, True)
            gain_vec = norm_gain[l][None, :]
            g_norm_gain = jnp.sum(grad_normed * residual * inv_rms, axis=0)
            inner_term = jnp.mean(grad_normed * gain_vec * residual, axis=-1, keepdims=True)
            gradient = (
                gradient + inv_rms * gain_vec * grad_normed
                - residual * (inv_rms * inv_rms * inv_rms) * inner_term
            )
            g_zo = ungroup(plane_sum(jnp.concatenate([g_z_w, g_out_w], axis=1)))
            g_front = plane_sum(g_front_w)
            g_xd = ungroup(jnp.concatenate([g_front[:, :inner], g_front[:, wide:]], axis=1))
            bc_part = g_front[:, inner:wide]
            keep_rows = lax.dynamic_slice(bc_part, (core * shard, 0), (shard, 2 * STATE))
            send_rows = lax.dynamic_slice(bc_part, ((1 - core) * shard, 0), (shard, 2 * STATE))
            g_bc = keep_rows.astype(F32) + send(send_rows, to_core).astype(F32)
            g_bc = over_tensor(g_bc, BF)
            found[l] = (g_zo, g_xd, g_bc, ggain, sgrad, hgrad, g_norm_gain)

        def small(l):
            _, _, _, ggain, sgrad, hgrad, g_norm_gain = found[l]
            sums = sgrad[0] + sgrad[1]
            head_rows = hgrad[0, :2] + hgrad[1, :2]
            skips = jnp.sum(sums[5, :inner].reshape(heads, HEADDIM), axis=1)
            last_row = jnp.concatenate(
                [head_rows[0], head_rows[1], jnp.pad(skips, (0, LANES - heads)),
                 jnp.zeros((inner - 3 * LANES,), F32)]
            )
            group = jnp.concatenate(
                [sums[:5, :inner], (ggain[0, :1] + ggain[1, :1]), last_row[None]], axis=0
            )
            shared = jnp.concatenate([sums[:5, inner:].reshape(-1), g_norm_gain])
            return group, shared

        group, shared = (jnp.stack(v) for v in zip(*[small(l) for l in range(LAYERS)]))
        group = back(group, to_group(0)) + back(group, to_group(1))
        shared = shared + send(shared, to_core)
        shared = over_tensor(shared, F32)
        everything = jnp.concatenate([group.reshape(-1), shared.reshape(-1)])
        bit = 2
        while bit < n_dp:
            everything = everything + send(everything, lambda d, t: (d ^ bit, t))
            bit *= 2
        group, shared = everything[: group.size].reshape(group.shape), everything[
            group.size :
        ].reshape(shared.shape)
        five = shared[:, : 5 * 2 * STATE].reshape(LAYERS, 5, 2 * STATE)
        head_grads = [group[:, 6, i * LANES : i * LANES + heads] for i in range(3)]

        def both(pick):
            return jnp.stack([pick(found[l]) for l in range(LAYERS)])

        return (
            output,
            gradient,
            shared[:, 5 * 2 * STATE :],
            both(lambda f: f[0][:, :inner]),
            both(lambda f: f[1][:, :inner]),
            both(lambda f: f[2]),
            both(lambda f: f[1][:, inner : inner + heads]),
            group[:, :4],
            group[:, 4],
            five[:, :4],
            five[:, 4],
            head_grads[0],
            head_grads[1],
            head_grads[2],
            group[:, 5],
            both(lambda f: f[0][:, inner:].T),
        )

    return local


def solution(mesh):
    n_dp, n_tensor = mesh.shape["dp"], mesh.shape["tensor"]
    tokens = P(("dp", "tensor"), None)
    columns = P(None, "dp", "tensor")
    placed = (
        tokens,
        P("dp"),
        P(),
        columns,
        columns,
        P(None, "dp", None),
        columns,
        P(None, None, "tensor"),
        P(None, "tensor"),
        P(),
        P(),
        P(None, "tensor"),
        P(None, "tensor"),
        P(None, "tensor"),
        P(None, "tensor"),
        P(None, "tensor", "dp"),
        tokens,
    )
    return jax.shard_map(
        build(n_dp, n_tensor),
        mesh=mesh,
        in_specs=placed,
        out_specs=(
            tokens,
            tokens,
            P(),
            columns,
            columns,
            P(None, "dp", None),
            columns,
            P(None, None, "tensor"),
            P(None, "tensor"),
            P(),
            P(),
            P(None, "tensor"),
            P(None, "tensor"),
            P(None, "tensor"),
            P(None, "tensor"),
            P(None, "tensor", "dp"),
        ),
        check_vma=False,
    )
```

```python
import functools

import jax
import jax.numpy as jnp
import numpy as np
from jax import lax
from jax.experimental import pallas as pl
from jax.experimental.pallas import tpu as pltpu
from jax.sharding import PartitionSpec as P

INNER = 3072
HEADDIM = 64
STATE = 128
LAYERS = 2
EPSILON = 1e-05
HALO = 16
CHUNK = 128
LANES = 128

BF = jnp.bfloat16
F32 = jnp.float32
EXACT = lax.Precision.HIGHEST


def dot(left, right, dims=((1,), (0,)), precision=None):
    return lax.dot_general(
        left, right, (dims, ((), ())), preferred_element_type=F32, precision=precision
    )


def split(values):
    high = values.astype(BF)
    return high, (values - high.astype(F32)).astype(BF)


def spread(values, e2_ref):
    return dot(jnp.concatenate(split(values), axis=1), e2_ref[...])


def head_sum(values, hm_ref):
    high, low = split(values)
    return dot(high, hm_ref[...]) + dot(low, hm_ref[...])


def softplus(values):
    return jnp.maximum(values, 0.0) + jnp.log1p(jnp.exp(-jnp.abs(values)))


def triangle(size, lower):
    rows = lax.broadcasted_iota(jnp.int32, (size, size), 0)
    cols = lax.broadcasted_iota(jnp.int32, (size, size), 1)
    return rows >= cols if lower else rows <= cols


def convolve(window, marks, cw, lanes):
    size = window.shape[0] - 8
    total = cw[4:5, lanes] + cw[3:4, lanes] * window[8:]
    for lag in (1, 2, 3):
        earlier = window[8 - lag : 8 - lag + size]
        total = total + cw[3 - lag : 4 - lag, lanes] * (earlier * marks[:, lag - 1 : lag])
    return total


def place(at_ref, j, side, piece, block):
    return pl.multiple_of((at_ref[0] ^ j) * piece + side * block, block)


def fetch_front(at_ref, pieces, w_ref, sems):
    size = pieces[0].shape[0]
    copies = []
    for j, piece in enumerate(pieces):
        row = pl.multiple_of((at_ref[2] ^ j) * size, size) if len(pieces) > 1 else 0
        copies.append(pltpu.make_async_copy(piece, w_ref.at[pl.ds(row, size), :], sems.at[j]))
    for copy in copies:
        copy.start()
    return copies


def start_copy(source, target, sem):
    copy = pltpu.make_async_copy(source, target, sem)
    copy.start()
    return copy


def fetch_rest(rest_ref, low, w_ref, sem):
    copy = pltpu.make_async_copy(rest_ref.at[:, pl.ds(low, w_ref.shape[1])], w_ref, sem)
    copy.start()
    return copy


def front_kernel(*refs, inner, half_size, chips, ready):
    at_ref, refs = refs[0], refs[1:]
    ours, theirs, refs = refs[:half_size], refs[half_size : 2 * half_size], refs[2 * half_size :]
    pieces, refs = refs[:chips], refs[chips:]
    cm_ref, lnk_ref, cw_ref, hp_ref, e2_ref = refs[:5]
    (far_toks_ref, far_raw_ref, head_ref, xb_ref, aux_ref, sloc_ref, tail_ref, edge_ref, send_ref,
     state_ref, raw_ref, w_ref, toks_ref, rawl_ref, sems) = refs[-15:]
    copies = fetch_front(at_ref, pieces, w_ref, sems)
    count = xb_ref.shape[0]
    wide = inner + 2 * STATE
    block = ours[0].shape[0]
    core = at_ref[1]
    toks_ref[:HALO, :] = jnp.zeros((HALO, toks_ref.shape[1]), BF)
    for j in range(half_size):
        for part, side in ((ours[j], core), (theirs[j], 1 - core)):
            row = place(at_ref, j, side, 2 * block, block) + HALO
            toks_ref[pl.ds(pl.multiple_of(row, HALO), block), :] = part[...]
    leaving = [start_copy(toks_ref, far_toks_ref, sems.at[chips])]
    for copy in copies:
        copy.wait()
    for low in range(0, wide + LANES, 2 * LANES):
        lanes = slice(low, min(low + 2 * LANES, wide + LANES))
        raw_ref[:, lanes] = dot(toks_ref[...], w_ref[:, lanes])
        rawl_ref[:, lanes] = raw_ref[:, lanes].astype(BF)
    leaving.append(start_copy(rawl_ref, far_raw_ref, sems.at[chips + 1]))
    head_ref[...] = raw_ref[HALO : 2 * HALO, :wide]
    tail_ref[...] = raw_ref[count + HALO - 8 :, :wide]
    edge_ref[...] = toks_ref[count:, :]
    ready()
    lower = triangle(CHUNK, True).astype(F32)
    state_ref[...] = jnp.zeros_like(state_ref)

    def step_chunk(k, carry):
        base = pl.multiple_of(k * CHUNK, CHUNK)
        here = pl.ds(base, CHUNK)
        marks = cm_ref[pl.ds(base + HALO, CHUNK), :]
        for low in range(0, wide, STATE):
            lanes = slice(low, low + STATE)
            window = raw_ref[pl.ds(base + HALO - 8, CHUNK + 8), lanes]
            pre = convolve(window, marks, cw_ref, lanes)
            xb_ref[here, lanes] = (pre * jax.nn.sigmoid(pre)).astype(BF)
        raw_dt = raw_ref[pl.ds(base + HALO, CHUNK), wide:]
        step = softplus(raw_dt + hp_ref[0:1, :])
        cum = dot(lower, -hp_ref[1:2, :] * step, precision=EXACT)
        aux_ref[here, :LANES] = step
        aux_ref[here, LANES:] = cum
        end = cum[CHUNK - 1 :, :]
        gain = jnp.exp(end - cum) * marks[:, 3:4] * step
        scaled = (spread(gain, e2_ref) * xb_ref[here, :inner].astype(F32)).astype(BF)
        b_rows = xb_ref[here, inner : inner + STATE]
        local = dot(b_rows, scaled, ((0,), (0,)))
        keep = spread(jnp.exp(end) * lnk_ref[pl.ds(k * 8, 8), :], e2_ref)[0:1]
        sloc_ref[k] = state_ref[...].astype(BF)
        state_ref[...] = keep * state_ref[...] + local
        return carry

    lax.fori_loop(0, count // CHUNK, step_chunk, 0)
    send_ref[...] = state_ref[...].astype(BF)
    for copy in leaving:
        copy.wait()


def pair_lanes(values, lane):
    high = values.astype(BF).astype(F32)
    return jnp.where(lane == 0, high, jnp.where(lane == 1, values - high, 0.0)).astype(BF)


def read_pair(tile):
    return tile[:, 0:1].astype(F32) + tile[:, 1:2].astype(F32)


def scan_kernel(*refs, inner, half_size, ready):
    (at_ref, far_toks_ref, old_ref, rest_ref, aux_ref, sloc_ref, send_ref, sin_ref, tail_ref,
     head_ref, cm_ref, segr_ref, lnk_ref, gp_ref, cw_ref, e2_ref) = refs[:16]
    (*far_refs, part_ref, xb_ref, zl_ref, core_ref, act_ref, sst_ref, toks_ref,
     extra_ref, z_ref, wz_ref, wo_ref, sems) = refs[-17:]
    copy_toks = start_copy(far_toks_ref, toks_ref, sems.at[2])
    copy_z = fetch_rest(rest_ref, 0, wz_ref, sems.at[0])
    copy_out = fetch_rest(rest_ref, inner, wo_ref, sems.at[1])
    count = xb_ref.shape[0]
    wide = inner + 2 * STATE
    width = toks_ref.shape[1]
    lower = triangle(CHUNK, True)
    lane = lax.broadcasted_iota(jnp.int32, (CHUNK, STATE), 1)
    first = lane < HEADDIM
    copy_toks.wait()
    copy_z.wait()
    for low in range(0, inner, 2 * LANES):
        lanes = slice(low, min(low + 2 * LANES, inner))
        z_ref[:, lanes] = dot(toks_ref[HALO:, :], wz_ref[:, lanes])
    ready()
    xb_ref[...] = old_ref[...]
    marks = cm_ref[HALO : 2 * HALO, :]
    for low in range(0, wide, STATE):
        lanes = slice(low, low + STATE)
        window = jnp.concatenate([tail_ref[:, lanes], head_ref[:, lanes]], axis=0)
        pre = convolve(window, marks, cw_ref, lanes)
        xb_ref[:HALO, lanes] = (pre * jax.nn.sigmoid(pre)).astype(BF)
    end = aux_ref[CHUNK - 1 : CHUNK, LANES:]
    gain = jnp.exp(end - aux_ref[:HALO, LANES:]) * marks[:, 3:4] * aux_ref[:HALO, :LANES]
    gain = spread(gain, e2_ref)

    def local_state(rows):
        scaled = (gain * rows[:, :inner].astype(F32)).astype(BF)
        return dot(rows[:, inner : inner + STATE], scaled, ((0,), (0,)))

    change = local_state(xb_ref[:HALO, :]) - local_state(old_ref[:HALO, :])
    extra_ref[...] = sin_ref[...].astype(F32)

    def step_chunk(k, carry):
        base = pl.multiple_of(k * CHUNK, CHUNK)
        here = pl.ds(base, CHUNK)
        marks = cm_ref[pl.ds(base + HALO, CHUNK), :]
        incoming = (sloc_ref[k].astype(F32) + extra_ref[...]).astype(BF)
        sst_ref[k] = incoming
        b_rows = xb_ref[here, inner : inner + STATE]
        c_rows = xb_ref[here, inner + STATE : inner + 2 * STATE]
        scores = dot(c_rows, b_rows, ((1,), (1,)))
        allowed = (marks[:, 5:6] == segr_ref[0:1, here]) & lower
        scores = jnp.where(allowed, scores, 0.0)
        step = aux_ref[here, :LANES]
        cum = aux_ref[here, LANES:]
        cum_t = jnp.transpose(cum)
        step_wide = spread(step, e2_ref)
        carried = spread(jnp.exp(cum) * marks[:, 4:5], e2_ref) * dot(c_rows, incoming)
        squares = jnp.zeros((CHUNK, STATE), F32)
        for pair in range(inner // STATE):
            lanes = slice(pair * STATE, (pair + 1) * STATE)
            x_rows = xb_ref[here, lanes].astype(F32)
            scaled = step_wide[:, lanes] * x_rows
            within = carried[:, lanes] + gp_ref[1:2, lanes] * x_rows
            for half in range(2):
                head = 2 * pair + half
                decay = jnp.exp(
                    jnp.minimum(cum[:, head : head + 1] - cum_t[head : head + 1, :], 0.0)
                )
                mine = first if half == 0 else ~first
                part = jnp.where(mine, scaled, 0.0).astype(BF)
                within = within + dot((scores * decay).astype(BF), part)
            core_ref[here, lanes] = within
            z_rows = z_ref[here, lanes]
            zl_ref[here, lanes] = z_rows.astype(BF)
            gated = within * (z_rows * jax.nn.sigmoid(z_rows))
            act_ref[here, lanes] = (gated * gp_ref[0:1, lanes]).astype(BF)
            squares = squares + gated * gated
        part_ref[here, width:] = jnp.where(lane == 0, jnp.sum(squares, axis=1, keepdims=True), 0.0)
        end = cum[CHUNK - 1 :, :]
        keep = spread(jnp.exp(end) * lnk_ref[pl.ds(k * 8, 8), :], e2_ref)[0:1]
        extra_ref[...] = keep * extra_ref[...] + jnp.where(k == 0, change, 0.0)
        return carry

    chunks = count // CHUNK
    lax.fori_loop(0, chunks, step_chunk, 0)
    sst_ref[chunks] = (send_ref[...].astype(F32) + extra_ref[...]).astype(BF)
    here_refs = (xb_ref, zl_ref, core_ref, act_ref, sst_ref)
    leaving = [
        start_copy(near, far, sems.at[3 + i]) for i, (near, far) in enumerate(zip(here_refs, far_refs))
    ]
    copy_out.wait()
    for low in range(0, width, 2 * LANES):
        lanes = slice(low, low + 2 * LANES)
        part_ref[:, lanes] = dot(act_ref[...], wo_ref[lanes, :], ((1,), (1,)))
    for copy in leaving:
        copy.wait()


def sum_kernel(*refs, half_size, offset, noted, ready):
    at_ref, part_ref, came_ref = refs[:3]
    outs = refs[-half_size:] if noted else refs[-half_size - 1 : -1]
    block = outs[0].shape[0]
    width = part_ref.shape[1] - (LANES if noted else 0)
    lane = lax.broadcasted_iota(jnp.int32, (block, LANES), 1)
    for j in range(half_size):
        at = slice(j * block, (j + 1) * block)
        row = place(at_ref, j, at_ref[1], 2 * block, block) + offset
        stay = pl.ds(pl.multiple_of(row, HALO), block)
        total = part_ref[stay, :width] + came_ref[at, :width].astype(F32)
        outs[j][:, :width] = total.astype(outs[j].dtype)
        if noted:
            line = part_ref[stay, width : width + 1] + read_pair(came_ref[at, width:])
            if j == 0:
                outs[j][:, width:] = jnp.where(lane == 0, line, 0.0)
            else:
                outs[j][:, width:] = pair_lanes(line, lane)
    if offset:
        low = half_size * block
        refs[-1][...] = (part_ref[:offset, :] + came_ref[low:, :].astype(F32)).astype(BF)


def normalize(values, gain_ref):
    size = 1.0 / values.shape[1]
    inv_rms = lax.rsqrt(jnp.sum(values * values, axis=1, keepdims=True) * size + EPSILON)
    return values * inv_rms * gain_ref[0:1, :]


def grad_message(msg_ref, grad, mixed, inv_gate):
    width = grad.shape[1]
    scaled = (inv_gate * grad).astype(BF)
    msg_ref[:, :width] = scaled
    weight = jnp.sum(scaled.astype(F32) * mixed, axis=1, keepdims=True)
    lane = lax.broadcasted_iota(jnp.int32, (grad.shape[0], LANES), 1)
    msg_ref[:, width:] = pair_lanes(inv_gate * inv_gate * weight * (1.0 / INNER), lane)


def first_kernel(*refs, ready):
    x_ref, gain_ref = refs[:2]
    res_ref, normed_ref = refs[-2:]
    values = x_ref[...].astype(F32)
    res_ref[...] = values
    normed_ref[...] = normalize(values, gain_ref).astype(BF)


def own_kernel(*refs, half_size, top, ready):
    ready()
    sum_ref, others, refs = refs[0], refs[1:half_size], refs[half_size:]
    res_ref, more_ref = refs[:2]
    mixed_ref, gate_ref, new_ref, msg_ref = refs[-4:]
    width = res_ref.shape[1]
    mixed = sum_ref[:, :width]
    line = sum_ref[:, width : width + 1]
    for other in others:
        mixed = mixed + other[:, :width].astype(F32)
        line = line + read_pair(other[:, width:])
    inv_gate = lax.rsqrt(line * (1.0 / INNER) + EPSILON)
    mixed_ref[...] = mixed
    gate_ref[...] = jnp.broadcast_to(inv_gate, gate_ref.shape)
    values = res_ref[...] + inv_gate * mixed
    new_ref[...] = values
    if top:
        grad_message(msg_ref, more_ref[...], mixed, inv_gate)
    else:
        msg_ref[...] = normalize(values, more_ref).astype(BF)


def own_back_kernel(*refs, half_size, bottom, ready):
    ready()
    sum_ref, others, refs = refs[0], refs[1:half_size], refs[half_size:]
    halos, refs = refs[:half_size], refs[half_size:]
    grad_ref, res_ref, gain_ref = refs[:3]
    if bottom:
        new_ref, gnorm_ref, buf_ref = refs[-3:]
    else:
        mixed_ref, gate_ref = refs[3:5]
        new_ref, gnorm_ref, msg_ref, buf_ref = refs[-4:]
    block = sum_ref.shape[0]
    total = sum_ref[...]
    for other in others:
        total = total + other[...].astype(F32)
    buf_ref[...] = total
    for halo in halos:
        buf_ref[block - HALO :, :] += halo[...].astype(F32)
    total = buf_ref[...]
    values = res_ref[...]
    size = 1.0 / values.shape[1]
    inv_rms = lax.rsqrt(jnp.sum(values * values, axis=1, keepdims=True) * size + EPSILON)
    gnorm = jnp.sum(total * values * inv_rms, axis=0, keepdims=True)
    gnorm_ref[...] = jnp.broadcast_to(gnorm, gnorm_ref.shape)
    scaled = total * gain_ref[0:1, :]
    inner_term = jnp.sum(scaled * values, axis=1, keepdims=True) * size
    grad = grad_ref[...] + inv_rms * scaled - values * (inv_rms * inv_rms * inv_rms) * inner_term
    new_ref[...] = grad
    if not bottom:
        grad_message(msg_ref, grad, mixed_ref[...], gate_ref[:, 0:1])


def gate_back_kernel(*refs, inner, half_size, ready):
    at_ref, refs = refs[0], refs[1:]
    ours, theirs, refs = refs[:half_size], refs[half_size : 2 * half_size], refs[2 * half_size :]
    rest_ref, far_core_ref, far_z_ref, far_xb_ref, aux_ref, cm_ref, lnk_ref, gp_ref, e2_ref = refs[:9]
    (far_grows_ref, gcore_ref, gz_ref, ggain_ref, dsin_ref, state_ref, gg_ref, coef_ref,
     wo_ref, core_ref, z_ref, xb_ref, grows_ref, sems) = refs[-14:]
    copy_out = fetch_rest(rest_ref, inner, wo_ref, sems.at[0])
    copies = [
        start_copy(far_core_ref, core_ref, sems.at[1]),
        start_copy(far_z_ref, z_ref, sems.at[2]),
        start_copy(far_xb_ref, xb_ref, sems.at[3]),
    ]
    count = xb_ref.shape[0]
    chunks = count // CHUNK
    width = grows_ref.shape[1]
    block = ours[0].shape[0]
    core_at = at_ref[1]
    for j in range(half_size):
        for part, side in ((ours[j], core_at), (theirs[j], 1 - core_at)):
            at = pl.ds(place(at_ref, j, side, 2 * block, block), block)
            grows_ref[at, :] = part[:, :width]
            coef_ref[at, :] = jnp.broadcast_to(read_pair(part[:, width:]), (block, LANES))
    leaving = start_copy(grows_ref, far_grows_ref, sems.at[4])
    copy_out.wait()
    for low in range(0, inner, 2 * LANES):
        lanes = slice(low, min(low + 2 * LANES, inner))
        gg_ref[:, lanes] = dot(grows_ref[...], wo_ref[:, lanes])
    for copy in copies:
        copy.wait()
    ready()
    state_ref[...] = jnp.zeros_like(state_ref)
    ggain_ref[...] = jnp.zeros_like(ggain_ref)
    gz_ref[:HALO, :] = jnp.zeros((HALO, inner), BF)

    def step_chunk(turn, carry):
        k = chunks - 1 - turn
        base = pl.multiple_of(k * CHUNK, CHUNK)
        here = pl.ds(base, CHUNK)
        there = pl.ds(pl.multiple_of(base + HALO, HALO), CHUNK)
        marks = cm_ref[there, :]
        coef = coef_ref[here, 0:1]
        cum = aux_ref[here, LANES:]
        entry = spread(jnp.exp(cum) * marks[:, 4:5], e2_ref)
        c_rows = xb_ref[here, inner + STATE : inner + 2 * STATE]
        end = cum[CHUNK - 1 :, :]
        keep = spread(jnp.exp(end) * lnk_ref[pl.ds(k * 8, 8), :], e2_ref)[0:1]
        for pair in range(inner // STATE):
            lanes = slice(pair * STATE, (pair + 1) * STATE)
            z_rows = z_ref[here, lanes].astype(F32)
            core = core_ref[here, lanes]
            grad = gg_ref[here, lanes]
            sig = jax.nn.sigmoid(z_rows)
            act = z_rows * sig
            gated = core * act
            ggain_ref[0:1, lanes] += jnp.sum(grad * gated, axis=0, keepdims=True)
            grad_gated = gp_ref[0:1, lanes] * grad - coef * gated
            gcore = (grad_gated * act).astype(BF)
            gcore_ref[here, lanes] = gcore
            gz_ref[there, lanes] = (
                grad_gated * core * (sig * (1.0 + z_rows * (1.0 - sig)))
            ).astype(BF)
            scaled = (entry[:, lanes] * gcore.astype(F32)).astype(BF)
            state_ref[:, lanes] = keep[:, lanes] * state_ref[:, lanes] + dot(
                c_rows, scaled, ((0,), (0,))
            )
        return carry

    lax.fori_loop(0, chunks, step_chunk, 0)
    dsin_ref[...] = state_ref[...].astype(BF)
    leaving.wait()


def scan_back_kernel(*refs, inner, half_size, chips, ready):
    at_ref, refs = refs[0], refs[1:]
    pieces, refs = refs[:chips], refs[chips:]
    (rest_ref, far_raw_ref, far_xb_ref, far_core_ref, far_sst_ref, gcore_ref, gz_ref, aux_ref,
     dso_ref, tail_ref, cm_ref, segr_ref, lnk_ref, gp_ref, cw_ref, hp_ref, e2_ref, hm_ref) = refs[:18]
    (graw_ref, sgrad_ref, hgrad_ref, part_ref, state_ref, dpre_ref, qv_ref, xd_ref,
     raw_ref, wf_ref, wz_ref, xb_ref, core_ref, sst_ref, sems) = refs[-15:]
    first_copies = [
        start_copy(far_xb_ref, xb_ref, sems.at[chips + 2]),
        start_copy(far_sst_ref, sst_ref, sems.at[chips + 3]),
        start_copy(far_core_ref, core_ref, sems.at[chips + 4]),
    ]
    copy_raw = start_copy(far_raw_ref, raw_ref, sems.at[chips])
    copies = fetch_front(at_ref, pieces, wf_ref, sems)
    copies.append(fetch_rest(rest_ref, 0, wz_ref, sems.at[chips + 1]))
    count = xb_ref.shape[0]
    chunks = count // CHUNK
    wide = inner + 2 * STATE
    upper = triangle(CHUNK, False)
    first = lax.broadcasted_iota(jnp.int32, (CHUNK, STATE), 1) < HEADDIM
    state_ref[...] = dso_ref[...].astype(F32)
    sgrad_ref[...] = jnp.zeros_like(sgrad_ref)
    hgrad_ref[...] = jnp.zeros_like(hgrad_ref)
    dpre_ref[:HALO, :] = jnp.zeros((HALO, wide), F32)
    dpre_ref[HALO + count :, :] = jnp.zeros((HALO, wide), F32)
    graw_ref[:HALO, wide:] = jnp.zeros((HALO, LANES), BF)

    ready()
    for copy in first_copies:
        copy.wait()
    copy_raw.wait()
    raw_ref[:HALO, :wide] = jnp.concatenate(
        [jnp.zeros((HALO - 8, wide), F32), tail_ref[...]], axis=0
    ).astype(BF)

    def step_chunk(turn, carry):
        k = chunks - 1 - turn
        base = pl.multiple_of(k * CHUNK, CHUNK)
        here = pl.ds(base, CHUNK)
        there = pl.ds(pl.multiple_of(base + HALO, HALO), CHUNK)
        marks = cm_ref[there, :]
        step = aux_ref[here, :LANES]
        cum = aux_ref[here, LANES:]
        cum_t = jnp.transpose(cum)
        end = cum[CHUNK - 1 :, :]
        b_rows = xb_ref[here, inner : inner + STATE]
        c_rows = xb_ref[here, inner + STATE : wide]
        after = state_ref[...]
        after_low = after.astype(BF)
        product = jnp.sum(
            sst_ref[k + 1].astype(F32) * after_low.astype(F32), axis=0, keepdims=True
        )
        at_end = head_sum(jnp.broadcast_to(product, (8, inner)), hm_ref)[0:1]
        scores_t = dot(b_rows, c_rows, ((1,), (1,)))
        allowed = (marks[:, 5:6] == segr_ref[0:1, here]) & upper
        scores_t = jnp.where(allowed, scores_t, 0.0)
        gain = spread(jnp.exp(end - cum) * marks[:, 3:4], e2_ref)
        step_wide = spread(step, e2_ref)
        entry = spread(jnp.exp(cum) * marks[:, 4:5], e2_ref)
        keep = spread(jnp.exp(end) * lnk_ref[pl.ds(k * 8, 8), :], e2_ref)[0:1]
        outer = gain * dot(b_rows, after_low)
        scaled_grad = (entry * gcore_ref[here, :].astype(F32)).astype(BF)
        grad_c = dot(scaled_grad, sst_ref[k], ((1,), (1,)))
        scaled_x = (gain * (step_wide * xb_ref[here, :inner].astype(F32))).astype(BF)
        grad_b = dot(scaled_x, after_low, ((1,), (1,)))
        state_ref[...] = keep * after + dot(c_rows, scaled_grad, ((0,), (0,)))
        grad_scores = jnp.zeros((CHUNK, CHUNK), F32)
        for pair in range(inner // STATE):
            lanes = slice(pair * STATE, (pair + 1) * STATE)
            grad_low = gcore_ref[here, lanes]
            grad = grad_low.astype(F32)
            x_rows = xb_ref[here, lanes].astype(F32)
            wide_step = step_wide[:, lanes]
            scaled = wide_step * x_rows
            grad_u = outer[:, lanes]
            for half in range(2):
                head = 2 * pair + half
                decay = jnp.exp(
                    jnp.minimum(cum_t[head : head + 1, :] - cum[:, head : head + 1], 0.0)
                )
                mine = first if half == 0 else ~first
                part = jnp.where(mine, scaled, 0.0).astype(BF)
                grad_part = jnp.where(mine, grad, 0.0).astype(BF)
                grad_u = grad_u + dot((scores_t * decay).astype(BF), grad_part)
                grad_scores = grad_scores + dot(part, grad_low, ((1,), (1,))) * decay
            skip = gp_ref[1:2, lanes]
            qv_ref[:, lanes] = grad * (core_ref[here, lanes] - skip * x_rows) - (
                scaled.astype(BF).astype(F32) * grad_u
            )
            xd_ref[:, lanes] = x_rows * grad_u
            dpre_ref[there, lanes] = wide_step * grad_u + skip * grad
            sgrad_ref[5:6, lanes] += jnp.sum(grad * x_rows, axis=0, keepdims=True)
        grad_scores = jnp.where(allowed, grad_scores, 0.0).astype(BF)
        dpre_ref[there, inner : inner + STATE] = grad_b + dot(grad_scores, c_rows)
        dpre_ref[there, inner + STATE :] = grad_c + dot(grad_scores, b_rows, ((0,), (0,)))
        rate = hp_ref[1:2, :]
        grad_log = dot(upper.astype(F32), head_sum(qv_ref[...], hm_ref), precision=EXACT) + at_end
        grad_step = head_sum(xd_ref[...], hm_ref) - rate * grad_log
        raw_dt = raw_ref[there, wide:].astype(F32)
        grad_dt = grad_step * jax.nn.sigmoid(raw_dt + hp_ref[0:1, :])
        graw_ref[there, wide:] = grad_dt.astype(BF)
        hgrad_ref[0:1, :] += jnp.sum(grad_dt, axis=0, keepdims=True)
        hgrad_ref[1:2, :] -= rate * jnp.sum(step * grad_log, axis=0, keepdims=True)
        return carry

    lax.fori_loop(0, chunks, step_chunk, 0)

    def conv_chunk(k, carry):
        base = pl.multiple_of(k * CHUNK, CHUNK)
        there = pl.ds(pl.multiple_of(base + HALO, HALO), CHUNK)
        marks = cm_ref[there, :]
        for low in range(0, wide, STATE):
            lanes = slice(low, low + STATE)
            window = raw_ref[pl.ds(base, CHUNK + HALO), lanes].astype(F32)[HALO - 8 :]
            pre = convolve(window, marks, cw_ref, lanes)
            sig = jax.nn.sigmoid(pre)
            grad = dpre_ref[there, lanes] * (sig * (1.0 + pre * (1.0 - sig)))
            dpre_ref[there, lanes] = grad
            sgrad_ref[4:5, lanes] += jnp.sum(grad, axis=0, keepdims=True)
            sgrad_ref[3:4, lanes] += jnp.sum(grad * window[8:], axis=0, keepdims=True)
            for lag in (1, 2, 3):
                earlier = window[8 - lag : 8 - lag + CHUNK]
                sgrad_ref[3 - lag : 4 - lag, lanes] += jnp.sum(
                    grad * (earlier * marks[:, lag - 1 : lag]), axis=0, keepdims=True
                )
        return carry

    lax.fori_loop(0, chunks, conv_chunk, 0)

    def transpose_rows(start, size):
        marks = cm_ref[pl.ds(start, size + 8), :]
        for low in range(0, wide, STATE):
            lanes = slice(low, low + STATE)
            window = dpre_ref[pl.ds(start, size + 8), lanes]
            total = cw_ref[3:4, lanes] * window[:size]
            for lag in (1, 2, 3):
                masked = window[lag : lag + size] * marks[lag : lag + size, lag - 1 : lag]
                total = total + cw_ref[3 - lag : 4 - lag, lanes] * masked
            graw_ref[pl.ds(start, size), lanes] = total.astype(BF)

    transpose_rows(0, HALO)

    def back_chunk(k, carry):
        transpose_rows(pl.multiple_of(k * CHUNK + HALO, HALO), CHUNK)
        return carry

    lax.fori_loop(0, chunks, back_chunk, 0)
    width = part_ref.shape[1]
    for copy in copies:
        copy.wait()
    for low in range(0, width, 2 * LANES):
        lanes = slice(low, low + 2 * LANES)
        part_ref[:, lanes] = dot(gz_ref[...], wz_ref[lanes, :], ((1,), (1,))) + dot(
            graw_ref[...], wf_ref[lanes, :], ((1,), (1,))
        )


def weight_kernel(*refs, terms, halo, far, pieces, ready):
    refs = list(refs)
    sems = refs.pop()
    at_ref = refs.pop(0) if pieces else None
    out_ref = refs.pop()
    near = refs[-len(far) :]
    outs = refs[len(refs) - len(far) - max(pieces, 1) : len(refs) - len(far)]
    leaving = []
    copies = {}
    for i, (place_of, target) in enumerate(zip(far, near)):
        copies[place_of] = start_copy(refs[place_of], target, sems.at[i])
        refs[place_of] = target
    ready()
    tile = 2 * LANES
    low = 0
    for term in range(terms):
        left_a, right_a, left_b, right_b = refs[4 * term : 4 * term + 4]
        size = right_a.shape[1]
        for place_of in range(4 * term, 4 * term + 4):
            if place_of in copies:
                copies[place_of].wait()

        def step_tile(r, carry):
            at = pl.ds(pl.multiple_of(r * tile, tile), tile)
            total = dot(left_a[:, at], right_a[...], ((0,), (0,)))
            total = total + dot(left_b[:, at], right_b[...], ((0,), (0,)))
            if halo:
                edge_a, edge_b = refs[4 * terms : 4 * terms + 2]
                total = total + dot(edge_a[:, at], right_a[:HALO, :], ((0,), (0,)))
                total = total + dot(edge_b[:, at], right_b[:HALO, :], ((0,), (0,)))
            out_ref[at, low : low + size] = total.astype(BF)
            return carry

        lax.fori_loop(0, out_ref.shape[0] // tile, step_tile, 0)
        if not pieces:
            lanes = pl.ds(low, size)
            leaving.append(
                start_copy(out_ref.at[:, lanes], outs[0].at[:, lanes], sems.at[len(far) + term])
            )
        low += size
    for copy in leaving:
        copy.wait()
    if pieces:
        for j, piece_ref in enumerate(outs):
            size = piece_ref.shape[0]
            row = pl.multiple_of((at_ref[2] ^ j) * size, size)
            piece_ref[...] = out_ref[pl.ds(row, size), :]


def hold_kernel(*refs, ready):
    refs[-1][...] = refs[0][...]


def pick_kernel(*refs, inner, shard, layer, front, rest, ready):
    ready()
    at_ref, one_ref, two_ref = refs[:3]
    outs = refs[-(front + rest) :]
    for side in range(2):
        rows = slice(side * shard, (side + 1) * shard)
        value = jnp.where(at_ref[3] == side, one_ref[...], two_ref[...])
        low = 0
        if front:
            own_ref, other_ref = refs[3:5]
            outs[0][rows, :inner] = value[:, :inner]
            outs[0][rows, inner : inner + 2 * STATE] = jnp.where(
                at_ref[1] == side, own_ref[layer], other_ref[layer]
            )
            outs[0][rows, inner + 2 * STATE :] = value[:, inner : inner + LANES]
            low = inner + LANES
        if rest:
            outs[-1][rows, :] = value[:, low:]


def split_kernel(*refs, terms, shard, inner, front, ready):
    ready()
    at_ref, refs = refs[0], refs[1:]
    buf_ref = refs[-1]
    buf_ref[...] = tree_sum([ref[...] for ref in refs[:terms]])
    half, core = at_ref[3], at_ref[1]
    if front:
        one_ref, two_ref, keep_ref, away_ref = refs[-5:-1]
    else:
        one_ref, two_ref = refs[-3:-1]
    for out_ref, side in ((one_ref, half), (two_ref, 1 - half)):
        rows = pl.ds(pl.multiple_of(side * shard, HALO), shard)
        if front:
            out_ref[:, :inner] = buf_ref[rows, :inner].astype(BF)
            out_ref[:, inner:] = buf_ref[rows, inner + 2 * STATE :].astype(BF)
        else:
            out_ref[...] = buf_ref[rows, :].astype(BF)
    if front:
        lanes = slice(inner, inner + 2 * STATE)
        rows = pl.ds(pl.multiple_of(core * shard, HALO), shard)
        keep_ref[...] = buf_ref[rows, lanes]
        rows = pl.ds(pl.multiple_of((1 - core) * shard, HALO), shard)
        away_ref[...] = buf_ref[rows, lanes].astype(BF)


def final_kernel(*refs, layers, inner, heads, tensors, ready):
    gz_ref, gx_ref, gbc_ref, gdt_ref, gout_ref = refs[-5:]
    for l in range(layers):
        rest_one, rest_two, front_one, front_two = refs[4 * l : 4 * l + 4]
        total = rest_one[...].astype(F32) + rest_two[...].astype(F32)
        gz_ref[l] = total[:, :inner]
        gout_ref[l] = total[:, inner:]
        total = front_one[...].astype(F32) + front_two[...].astype(F32)
        gx_ref[l] = total[:, :inner]
        gdt_ref[l] = total[:, inner : inner + heads]
    gbc_ref[...] = tree_sum([ref[...] for ref in refs[4 * layers : 4 * layers + tensors]])


def gate_kernel(*refs, terms, ready):
    for source, target in zip(refs[:terms], refs[-terms:]):
        target[...] = source[...]


def away_kernel(*refs, half_size, offset, noted, ready):
    at_ref, part_ref, away_ref = refs[0], refs[1], refs[-1]
    block = (part_ref.shape[0] - offset) // (2 * half_size)
    width = part_ref.shape[1] - (LANES if noted else 0)
    lane = lax.broadcasted_iota(jnp.int32, (block, LANES), 1)
    for j in range(half_size):
        to = slice(j * block, (j + 1) * block)
        row = place(at_ref, j, 1 - at_ref[1], 2 * block, block) + offset
        go = pl.ds(pl.multiple_of(row, HALO), block)
        away_ref[to, :width] = part_ref[go, :width].astype(BF)
        if noted:
            away_ref[to, width:] = pair_lanes(part_ref[go, width : width + 1], lane)
    if offset:
        away_ref[half_size * block :, :] = part_ref[:offset, :].astype(BF)


def touch_kernel(*refs, ready):
    refs[-1][...] = jnp.zeros_like(refs[-1])


def tree_sum(values):
    values = [v.astype(F32) for v in values]
    while len(values) > 1:
        values = [a + b for a, b in zip(values[::2], values[1::2])]
    return values[0]


def add_kernel(*refs, terms, ready):
    refs[-1][...] = tree_sum([ref[...] for ref in refs[:terms]]).astype(refs[-1].dtype)


def pack_kernel(*refs, inner, layers, ready):
    out_ref = refs[-1]
    out_ref[...] = jnp.zeros_like(out_ref)
    for l in range(layers):
        ggain, sgrad, hgrad, gnorm = (
            refs[8 * l + 2 * i][...] + refs[8 * l + 2 * i + 1][...] for i in range(4)
        )
        out_ref[l, 0:5, :inner] = sgrad[0:5, :inner].astype(BF)
        out_ref[l, 5:6, :inner] = ggain[0:1, :].astype(BF)
        out_ref[l, 6:7, :inner] = sgrad[5:6, :inner].astype(BF)
        out_ref[l, 7:8, :LANES] = hgrad[0:1, :].astype(BF)
        out_ref[l, 7:8, LANES : 2 * LANES] = hgrad[1:2, :].astype(BF)
        out_ref[l, 8:13, : 2 * STATE] = sgrad[0:5, inner:].astype(BF)
        out_ref[l, 13:14, :] = gnorm[0:1, :].astype(BF)


class Queue:
    def __init__(self):
        self.last = None

    def run(
        self, kernel, operands, outs, scratch=(), scalars=0, far=(), far_out=(), staged=(),
        staged_out=(), after=(), limit=10,
    ):
        near = pl.BlockSpec(memory_space=pltpu.VMEM)
        distant = pl.BlockSpec(memory_space=pltpu.HBM)
        free = pl.BlockSpec(memory_space=pl.ANY)
        extra = list(after) + ([] if self.last is None else [self.last])
        outside = set(far) | set(staged)
        outside_out = set(far_out) | set(staged_out)
        count, staged, staged_out = len(operands), list(staged), list(staged_out)

        def wrapped(*refs):
            refs = list(refs)
            sems = refs.pop()
            base = count + len(extra)
            buffers = refs[len(refs) - len(staged) - len(staged_out) :]
            refs = refs[: len(refs) - len(buffers)]
            arriving = []
            for i, position in enumerate(staged):
                arriving.append(start_copy(refs[position], buffers[i], sems.at[i]))
                refs[position] = buffers[i]
            leaving = []
            for i, position in enumerate(staged_out, len(staged)):
                leaving.append((buffers[i], refs[base + position], sems.at[i]))
                refs[base + position] = buffers[i]

            def ready():
                for copy in arriving:
                    copy.wait()

            kernel(*refs, ready=ready)
            for copy in [start_copy(*parts) for parts in leaving]:
                copy.wait()

        specs = [pl.BlockSpec(memory_space=pltpu.SMEM)] * scalars
        specs += [distant if i in outside else near for i in range(scalars, count)]
        buffers = [(operands[i].shape, operands[i].dtype) for i in staged]
        buffers += [outs[i] for i in staged_out]
        operands = [
            pltpu.with_memory_space_constraint(v, pltpu.HBM) if i in outside else v
            for i, v in enumerate(operands)
        ]
        result = pl.pallas_call(
            wrapped,
            in_specs=specs + [free] * len(extra),
            out_specs=[distant if i in outside_out else near for i in range(len(outs))],
            out_shape=[
                pltpu.HBM(s, t) if i in outside_out else jax.ShapeDtypeStruct(s, t)
                for i, (s, t) in enumerate(outs)
            ],
            scratch_shapes=[
                pltpu.SemaphoreType.DMA(s) if t is None else pltpu.VMEM(s, t)
                for s, t in [*scratch, *buffers, ((max(len(buffers), 1),), None)]
            ],
            compiler_params=pltpu.CompilerParams(vmem_limit_bytes=limit * 1024 * 1024),
            cost_estimate=pl.CostEstimate(flops=1000, bytes_accessed=1000, transcendentals=0),
        )(*operands, *extra)
        self.last = result[-1]
        return result

    def gate(self, values, after):
        return self.run(
            functools.partial(gate_kernel, terms=len(values)), values,
            [(v.shape, v.dtype) for v in values], after=after,
        )

    def touch(self, values):
        self.run(touch_kernel, [], [((8, LANES), F32)], after=values)


def build(n_dp, n_tensor):
    axes = ("dp", "tensor")
    half_size = n_tensor // 2
    planes = [[d for d in range(n_dp) if d % 2 == c] for c in range(2)]
    plane_bits = [1 << b for b in range(1, n_dp.bit_length() - 1)]

    def pairs(route):
        found = []
        for d in range(n_dp):
            for t in range(n_tensor):
                goal = route(d, t)
                if goal is not None:
                    found.append((d * n_tensor + t, goal[0] * n_tensor + goal[1]))
        return found

    def send(value, route):
        return lax.ppermute(value, axes, pairs(route))

    def back(value, route):
        return lax.ppermute(value, axes, [(b, a) for a, b in pairs(route)])

    def to_core(d, t):
        return d ^ 1, t

    def to_plane(bits):
        return lambda d, t: (d ^ bits, t)

    def to_tensor(bits):
        return lambda d, t: (d, t ^ bits)

    def to_piece(j):
        return lambda d, t: (d, (t // half_size) * half_size + ((t % half_size) ^ j))

    def to_later(d, t):
        return (d, t + half_size) if t < half_size else None

    def to_halo(j):
        return lambda d, t: (d, half_size + j) if d % 2 == 1 and t == half_size - 1 else None

    def to_group(turn):
        def route(d, t):
            return (d & ~1) | (t % 2), t // 2 + half_size * ((d & 1) ^ turn)

        return route

    def matmul(left, right, dims=((1,), (0,))):
        return lax.dot_general(left, right, (dims, ((), ())), preferred_element_type=F32)

    def local(
        x_in, segments, norm_gain, w_z, w_x, w_bc, w_dt, conv_x, conv_x_bias, conv_bc, conv_bc_bias,
        dt_bias, a_log, d_skip, gate_gain, w_out, cotangent,
    ):
        inner = w_z.shape[2]
        heads = dt_bias.shape[1]
        piece, width = x_in.shape
        block = piece // 2
        count = half_size * piece
        rows = count + HALO
        chunks = count // CHUNK
        shard = w_z.shape[1]
        wide = inner + 2 * STATE
        place = lax.axis_index("tensor")
        dp_place = lax.axis_index("dp")
        core = dp_place % 2
        column = dp_place // 2
        half = place // half_size
        mine = place % half_size

        def cut(value, start, size):
            return lax.dynamic_slice(
                value, (start,) + (0,) * (value.ndim - 1), (size,) + value.shape[1:]
            )

        def put(value, part, start):
            return lax.dynamic_update_slice(value, part, (start,) + (0,) * (value.ndim - 1))

        def to_streams(value):
            keep, away = cut(value, core * block, block), cut(value, (1 - core) * block, block)
            came = send(away, to_core)
            return [jnp.where(core == 0, keep, came), jnp.where(core == 0, came, keep)]

        def from_streams(values):
            keep = jnp.where(core == 0, values[0], values[1])
            came = send(jnp.where(core == 0, values[1], values[0]), to_core)
            out = jnp.zeros((piece, width), F32)
            return put(put(out, keep, core * block), came, (1 - core) * block)

        def pad_lanes(value):
            return jnp.pad(value, ((0, 0), (0, LANES - value.shape[1])))

        queue = Queue()
        at = jnp.stack([mine, core, column, half]).astype(jnp.int32)
        chips = n_dp // 2

        def hold(value, after):
            return queue.run(hold_kernel, [value], [(value.shape, value.dtype)], after=after)[0]

        def regroup(value):
            return [send(value, to_group(0)), send(value, to_group(1))]

        bc_other = send(w_bc, to_core)
        def gather_plane(value):
            return lax.all_gather(value, "dp", axis=0, tiled=True, axis_index_groups=planes)

        def pick(parts, l, front, rest, after=()):
            outs = []
            if front:
                outs.append(((2 * shard, wide + LANES), BF))
            if rest:
                outs.append(((2 * shard, 2 * inner), BF))
            values = queue.run(
                functools.partial(
                    pick_kernel, inner=inner, shard=shard, layer=l, front=front, rest=rest
                ),
                [at, *parts] + ([w_bc, bc_other] if front else []),
                outs,
                scalars=1,
                after=after,
                staged_out=range(len(outs)),
            )
            values = [gather_plane(v) for v in values]
            if front:
                front_w[l] = [values[0]]
            if rest:
                rest_w[l] = values[-1]

        def front_part(l):
            return [w_x[l], pad_lanes(w_dt[l])]

        def rest_part(l):
            return [w_z[l], w_out[l].T]

        def row(value, size):
            return jnp.pad(value, ((0, 0), (0, size - value.shape[1])))[:, None]

        head_rows = jnp.concatenate([row(v, LANES) for v in (dt_bias, a_log, d_skip)], axis=2)
        head_rows = jnp.pad(head_rows, ((0, 0), (0, 0), (0, inner - 3 * LANES)))
        packed = jnp.concatenate(
            [conv_x, conv_x_bias[:, None], gate_gain[:, None], head_rows], axis=1
        )
        packed = send(packed, to_group(0))
        taps, bias, gain_own = packed[:, :4], packed[:, 4:5], packed[:, 5:6]
        dt_own, a_own, skip_own = (packed[:, 6, i * LANES : (i + 1) * LANES] for i in range(3))
        head_ok = jnp.arange(LANES) < heads
        rate_own = jnp.where(head_ok, jnp.exp(a_own), 0.0)
        skip_wide = jnp.repeat(skip_own[:, :heads], HEADDIM, axis=1)
        conv_w = jnp.concatenate(
            [
                jnp.concatenate([taps, conv_bc], axis=2),
                jnp.concatenate([bias, conv_bc_bias[:, None]], axis=2),
                jnp.zeros((LAYERS, 3, wide), F32),
            ],
            axis=1,
        )
        gate_p = jnp.concatenate(
            [gain_own, skip_wide[:, None], jnp.zeros((LAYERS, 6, inner), F32)], axis=1
        )
        head_p = jnp.concatenate(
            [dt_own[:, None], rate_own[:, None], jnp.zeros((LAYERS, 6, LANES), F32)], axis=1
        )
        member = np.arange(inner)[None, :] // HEADDIM == np.arange(LANES)[:, None]
        e2 = jnp.asarray(np.concatenate([member, member], axis=0), BF)
        hm = jnp.asarray(member.T, BF)

        seg = jnp.concatenate([jnp.full((HALO,), -1.0, F32), segments.astype(F32)])
        seg = cut(seg, half * count, rows)
        seg_other = send(seg, to_core)
        seg = jnp.stack([jnp.where(core == 0, seg, seg_other), jnp.where(core == 0, seg_other, seg)])
        tokens = seg[:, HALO:]
        lagged = [
            (tokens == seg[:, HALO - k : HALO - k + count]).astype(F32) for k in (1, 2, 3)
        ]
        by_chunk = tokens.reshape(2, chunks, CHUNK)
        last = by_chunk[:, :, -1]
        before = jnp.concatenate([seg[:, HALO - 1 : HALO], last[:, :-1]], axis=1)
        stays = (by_chunk == last[:, :, None]).astype(F32).reshape(2, count)
        enters = (by_chunk == before[:, :, None]).astype(F32).reshape(2, count)
        marks = jnp.stack(lagged + [stays, enters, tokens, tokens, tokens], axis=-1)
        marks = jnp.pad(marks, ((0, 0), (HALO, HALO), (0, 0)))
        seg_row = jnp.broadcast_to(tokens[:, None, :], (2, 8, count))
        links = (last == before).astype(F32)
        links = jnp.broadcast_to(links[:, :, None, None], (2, chunks, 8, LANES))
        links = links.reshape(2, chunks * 8, LANES)

        def exchange(value):
            return [value] + [send(value, to_piece(j)) for j in range(1, half_size)]

        def share(ours):
            return ours + [send(part, to_core) for part in ours]

        def pieces(values):
            return [send(values[j], to_piece(j)) for j in range(1, half_size)]

        mixer = functools.partial
        sizes = dict(inner=inner, half_size=half_size)
        noted = width + LANES
        gains = [jnp.broadcast_to(norm_gain[l][None], (8, width)) for l in range(LAYERS)]

        front_w, rest_w = [None] * LAYERS, [None] * LAYERS
        parts = regroup(jnp.concatenate(front_part(0), axis=1))
        start = to_streams(x_in)
        grads = to_streams(cotangent)
        residual = [[None, None] for _ in range(LAYERS + 1)]
        normed = [None, None]
        kept = [[{}, {}] for _ in range(LAYERS)]
        arrived = [None, None]

        def spread_tokens(s):
            arrived[s] = exchange(normed[s])

        def front(l, s, after=()):
            parts = [at, *share(arrived[s]), *front_w[l]]
            chips = len(front_w[l])
            (toks, raw, head, xb, aux, sloc, tail, edge, ends) = queue.run(
                mixer(front_kernel, chips=chips, **sizes),
                [*parts, marks[s], links[s], conv_w[l], head_p[l], e2],
                [((rows, width), BF), ((rows, wide + LANES), BF), ((HALO, wide), F32),
                 ((count, wide), BF), ((count, 2 * LANES), F32), ((chunks, STATE, inner), BF),
                 ((8, wide), F32), ((HALO, width), BF), ((STATE, inner), BF)],
                [((STATE, inner), F32), ((rows, wide + LANES), F32),
                 ((n_dp * shard, wide + LANES), BF), ((rows, width), BF),
                 ((rows, wide + LANES), BF), ((chips + 2,), None)],
                scalars=1,
                far=range(len(parts) - chips, len(parts)),
                far_out=(0, 1),
                staged=range(len(parts), len(parts) + 5),
                staged_out=(2, 3, 4, 5),
                limit=20,
            )
            tail, edge, ends = queue.gate([tail, edge, ends], after)
            kept[l][s].update(
                toks=toks, raw=raw, head=head, xb=xb, aux=aux, sloc=sloc, ends=ends,
                tail=send(tail, to_later), edge=send(edge, to_later), begins=send(ends, to_later),
            )

        def scan(l, s, after=()):
            v = kept[l][s]
            (xb, z, core_out, act, sst, part) = queue.run(
                mixer(scan_kernel, **sizes),
                [at, v["toks"], v["xb"], rest_w[l], v["aux"], v["sloc"], v["ends"], v["begins"],
                 v["tail"], v["head"], marks[s], seg_row[s], links[s], gate_p[l], conv_w[l], e2],
                [((count, wide), BF), ((count, inner), BF), ((count, inner), F32),
                 ((count, inner), BF), ((chunks + 1, STATE, inner), BF),
                 ((count, noted), F32)],
                [((count, wide), BF), ((count, inner), BF), ((count, inner), F32),
                 ((count, inner), BF), ((chunks + 1, STATE, inner), BF), ((rows, width), BF),
                 ((STATE, inner), F32), ((count, inner), F32), ((n_dp * shard, inner), BF),
                 ((n_dp * shard, inner), BF), ((8,), None)],
                scalars=1,
                after=[v["edge"]],
                far=(1, 3),
                far_out=range(5),
                staged=[2, 4, 5, 9, *range(10, 16)],
                limit=26,
            )
            v.update(xb=xb, z=z, core_out=core_out, act=act, sst=sst)
            send_away(v, part, 0, after)

        def send_away(v, part, offset, after):
            size = part.shape[1]
            away = queue.run(
                mixer(away_kernel, half_size=half_size, offset=offset, noted=offset == 0),
                [at, part], [((half_size * block + offset, size), BF)], scalars=1, after=after,
            )[0]
            v["sum"] = (part, send(away, to_core))

        def add_cores(l, s, has_note, after=()):
            part, came = kept[l][s]["sum"]
            size = part.shape[1]
            sums = queue.run(
                mixer(
                    sum_kernel, half_size=half_size, noted=has_note, offset=0 if has_note else HALO
                ),
                [at, part, came],
                [((block, size), F32)] + [((block, size), BF)] * (half_size - 1)
                + ([] if has_note else [((HALO, size), BF)]),
                scalars=1,
                after=after,
            )
            kept[l][s]["pieces"] = [sums[0]] + pieces(sums)
            if not has_note:
                kept[l][s]["halos"] = [back(sums[-1], to_halo(j)) for j in range(half_size)]

        def own(l, s):
            top = l == LAYERS - 1
            v = kept[l][s]
            mixed, gate, new, msg = queue.run(
                mixer(own_kernel, half_size=half_size, top=top),
                [*v["pieces"], residual[l][s], grads[s] if top else gains[l + 1]],
                [((block, width), F32), ((block, LANES), F32), ((block, width), F32),
                 ((block, noted if top else width), BF)],
                staged=(half_size, half_size + 1),
                staged_out=(0, 1, 2),
            )
            v.update(mixed=mixed, gate=gate)
            residual[l + 1][s] = new
            if top:
                arrived[s] = exchange(msg)
            else:
                normed[s] = msg
                spread_tokens(s)

        for s in range(2):
            residual[0][s], normed[s] = queue.run(
                first_kernel, [start[s], gains[0]], [((block, width), F32), ((block, width), BF)],
                staged_out=(0,),
            )
            spread_tokens(s)
        def sums_of(l, s):
            return kept[l][s]["pieces"][1:]

        pick(parts, 0, True, False)
        queue.touch([marks, seg_row, links, conv_w, gate_p, head_p])
        parts = regroup(hold(jnp.concatenate(rest_part(0), axis=1), []))
        pick(parts, 0, False, True, [*arrived[0], *arrived[1]])
        parts = [
            regroup(hold(jnp.concatenate(front_part(l) + rest_part(l), axis=1), []))
            for l in range(1, LAYERS)
        ]
        front(0, 0)
        front(0, 1, [kept[0][0]["begins"]])
        for l in range(1, LAYERS):
            pick(parts[l - 1], l, True, True)
        for l in range(LAYERS):
            scan(l, 0, arrived[1] if l > 0 else [kept[0][1]["begins"]])
            add_cores(l, 0, True)
            if l > 0:
                front(l, 1, sums_of(l, 0))
                own(l, 0)
                scan(l, 1, arrived[0])
            else:
                scan(l, 1, sums_of(l, 0))
                own(l, 0)
            add_cores(l, 1, True)
            if l + 1 < LAYERS:
                front(l + 1, 0, sums_of(l, 1))
                own(l, 1)

        def owners(messages):
            return [back(messages[0], to_group(0)), back(messages[1], to_group(1))]

        def split_rest(l):
            messages = queue.run(
                mixer(split_kernel, terms=1, shard=shard, inner=inner, front=False),
                [at, g_rest[l]],
                [((shard, 2 * inner), BF)] * 2,
                [(g_rest[l].shape, F32)],
                scalars=1,
                staged=(1,),
                limit=14,
            )
            done_rest[l] = owners(messages)

        def split_front(l, values, after=()):
            one, two, keep, away = queue.run(
                mixer(split_kernel, terms=len(values), shard=shard, inner=inner, front=True),
                [at, *values],
                [((shard, inner + LANES), BF)] * 2
                + [((shard, 2 * STATE), F32), ((shard, 2 * STATE), BF)],
                [(values[0].shape, F32)],
                scalars=1,
                after=after,
                limit=14,
            )
            done_front[l] = owners([one, two])
            bc_parts[l] = (keep, away)

        def offloaded_sum(value):
            return lax.psum_scatter(
                value, "dp", scatter_dimension=0, tiled=True, axis_index_groups=planes
            )

        def direct_start(values):
            return [values[0]] + [send(values[j], to_plane(2 * j)) for j in range(1, chips)]

        def add(parts, kind):
            return queue.run(
                mixer(add_kernel, terms=len(parts)), parts, [(parts[0].shape, kind)]
            )[0]

        all_tensor = [to_tensor(j) for j in range(1, n_tensor)]
        all_plane = [to_plane(2 * j) for j in range(1, n_dp // 2)]

        def gate_back(l, s, after=()):
            v = kept[l][s]
            (grows, gcore, gz, ggain, dsin) = queue.run(
                mixer(gate_back_kernel, **sizes),
                [at, *share(arrived[s]), rest_w[l], v["core_out"], v["z"], v["xb"], v["aux"], marks[s],
                 links[s], gate_p[l], e2],
                [((count, width), BF), ((count, inner), BF), ((rows, inner), BF), ((8, inner), F32),
                 ((STATE, inner), BF)],
                [((STATE, inner), F32), ((count, inner), F32), ((count, LANES), F32),
                 ((n_dp * shard, inner), BF), ((count, inner), F32), ((count, inner), BF),
                 ((count, wide), BF), ((count, width), BF), ((5,), None)],
                scalars=1,
                far=range(1 + 2 * half_size, 5 + 2 * half_size),
                far_out=(0,),
                staged_out=(1, 2),
                staged=range(5 + 2 * half_size, 10 + 2 * half_size),
                limit=20,
            )
            dsin, = queue.gate([dsin], after)
            v.update(grows=grows, gcore=gcore, gz=gz, ggain=ggain, dsout=back(dsin, to_later))

        def scan_back(l, s, after=()):
            v = kept[l][s]
            chips = len(front_w[l])
            (graw, sgrad, hgrad, part) = queue.run(
                mixer(scan_back_kernel, chips=chips, **sizes),
                [at, *front_w[l], rest_w[l], v["raw"], v["xb"], v["core_out"], v["sst"],
                 v["gcore"], v["gz"], v["aux"], v["dsout"], v["tail"], marks[s], seg_row[s], links[s],
                 gate_p[l], conv_w[l], head_p[l], e2, hm],
                [((rows, wide + LANES), BF), ((8, wide), F32), ((8, LANES), F32),
                 ((rows, width), F32)],
                [((STATE, inner), F32), ((count + 2 * HALO, wide), F32), ((CHUNK, inner), F32),
                 ((CHUNK, inner), F32), ((rows, wide + LANES), BF),
                 ((n_dp * shard, wide + LANES), BF), ((n_dp * shard, inner), BF),
                 ((count, wide), BF), ((count, inner), F32), ((chunks + 1, STATE, inner), BF),
                 ((chips + 5,), None)],
                scalars=1,
                far=range(1, chips + 6),
                staged=[*range(chips + 6, chips + 9), *range(chips + 10, chips + 19)],
                staged_out=(0,),
                limit=30,
            )
            send_away(v, part, HALO, after)
            v.update(graw=graw, sgrad=sgrad, hgrad=hgrad)

        def own_back(l, s, after=()):
            v = kept[l][s]
            bottom = l == 0
            before = [] if bottom else [kept[l - 1][s]["mixed"], kept[l - 1][s]["gate"]]
            result = queue.run(
                mixer(own_back_kernel, half_size=half_size, bottom=bottom),
                [*v["pieces"], *v["halos"], grads[s], residual[l][s], gains[l], *before],
                [((block, width), F32), ((8, width), F32)]
                + ([] if bottom else [((block, noted), BF)]),
                [((block, width), F32)],
                after=after,
                staged=range(2 * half_size, 2 * half_size + 3 + len(before)),
                staged_out=(0,),
            )
            grads[s], v["gnorm"] = result[:2]
            if not bottom:
                arrived[s] = exchange(result[2])

        def weights_back(l, names, pieces=0, after=()):
            one, two = kept[l]
            operands = []
            for left, right in names:
                operands += [one[left], one[right], two[left], two[right]]
            size = sum(one[right].shape[1] for _, right in names)
            halo = len(names) == 1
            if halo:
                operands += [one["edge"], two["edge"]]
            far = range(4 * len(names))
            count_out = chips if pieces else 1
            scratch = [(operands[i].shape, BF) for i in far] + [((width, size), BF)]
            result = queue.run(
                mixer(weight_kernel, terms=len(names), halo=halo, far=far, pieces=pieces),
                ([at] if pieces else []) + operands,
                [((width // count_out, size), BF)] * count_out,
                scratch + [((len(far) + len(names),), None)],
                scalars=1 if pieces else 0,
                far=[i + 1 for i in far] if pieces else far,
                far_out=() if pieces else (0,),
                staged=[len(operands) - 2 + bool(pieces), len(operands) - 1 + bool(pieces)] if halo else (),
                limit=22,
            )
            queue.touch(after)
            return result if pieces else result[0]

        rest_names = (("toks", "gz"), ("grows", "act"))
        front_names = (("toks", "graw"),)
        g_rest, g_front = [None] * LAYERS, [None] * LAYERS
        top = LAYERS - 1
        gate_back(top, 0, sums_of(top, 1))
        own(top, 1)
        gate_back(top, 1, [kept[top][0]["dsout"]])
        g_rest[top] = offloaded_sum(weights_back(top, rest_names, 0, [kept[top][1]["dsout"]]))
        done_rest, done_front, bc_parts = ([None] * LAYERS for _ in range(3))
        for l in reversed(range(LAYERS)):
            scan_back(l, 0)
            add_cores(l, 0, False)
            scan_back(l, 1, sums_of(l, 0) + kept[l][0]["halos"])
            if l == 0:
                own_back(l, 0)
                add_cores(l, 1, False)
                direct = direct_start(
                    weights_back(l, front_names, chips, sums_of(l, 1) + kept[l][1]["halos"])
                )
                for k in range(1, LAYERS):
                    split_front(k, [g_front[k]])
                split_rest(l)
                own_back(l, 1)
                earlier = [v for k in range(1, LAYERS) for v in done_front[k] + done_rest[k]]
                split_front(l, direct, done_rest[0] + earlier)
            else:
                own_back(l, 0)
                add_cores(l, 1, False)
                waiting = sums_of(l, 1) + kept[l][1]["halos"] + arrived[0]
                g_front[l] = offloaded_sum(weights_back(l, front_names, 0, waiting))
                own_back(l, 1)
                gate_back(l - 1, 0, arrived[1])
                gate_back(l - 1, 1, [kept[l - 1][0]["dsout"]])
                g_rest[l - 1] = offloaded_sum(
                    weights_back(l - 1, rest_names, 0, [kept[l - 1][1]["dsout"]])
                )
                split_rest(l)
        grad_in = from_streams(grads)
        output = from_streams(residual[LAYERS])

        names = ("ggain", "sgrad", "hgrad", "gnorm")
        packed = queue.run(
            mixer(pack_kernel, inner=inner, layers=LAYERS),
            [kept[l][s][k] for l in range(LAYERS) for k in names for s in range(2)],
            [((LAYERS, 2 * 8, width), BF)],
        )[0]
        packed = add([back(packed, to_group(0)), back(packed, to_group(1))], F32)
        common = packed[:, 8:].astype(BF)
        common = add([common] + [send(common, route) for route in all_tensor], F32)
        packed = jnp.concatenate([packed[:, :8], common], axis=1)
        low_packed = packed.astype(BF)
        packed = add([low_packed] + [send(low_packed, route) for route in all_plane], F32)

        g_bc = jnp.stack([keep for keep, _ in bc_parts]) + send(
            jnp.stack([away for _, away in bc_parts]), to_core
        ).astype(F32)
        g_bc = g_bc.astype(BF)
        parts = []
        for l in range(LAYERS):
            parts += [*done_rest[l], *done_front[l]]
        g_z, g_x, g_bc, g_dt, g_out = queue.run(
            mixer(final_kernel, layers=LAYERS, inner=inner, heads=heads, tensors=n_tensor),
            parts + [g_bc] + [send(g_bc, route) for route in all_tensor],
            [((LAYERS, shard, inner), F32), ((LAYERS, shard, inner), F32),
             ((LAYERS, shard, 2 * STATE), F32), ((LAYERS, shard, heads), F32),
             ((LAYERS, shard, inner), F32)],
            limit=16,
        )
        group, shared = packed[:, :8, :inner], packed[:, 8:]
        five = shared[:, :5, : 2 * STATE]
        head_grads = [group[:, 7, :heads], group[:, 7, LANES : LANES + heads]]
        head_grads.append(jnp.sum(group[:, 6].reshape(LAYERS, heads, HEADDIM), axis=2))
        return (
            output,
            grad_in,
            shared[:, 5],
            g_z,
            g_x,
            g_bc,
            g_dt,
            group[:, :4],
            group[:, 4],
            five[:, :4],
            five[:, 4],
            head_grads[0],
            head_grads[1],
            head_grads[2],
            group[:, 5],
            jnp.swapaxes(g_out, 1, 2),
        )

    return local


def solution(mesh):
    n_dp, n_tensor = mesh.shape["dp"], mesh.shape["tensor"]
    tokens = P(("dp", "tensor"), None)
    columns = P(None, "dp", "tensor")
    placed = (
        tokens,
        P("dp"),
        P(),
        columns,
        columns,
        P(None, "dp", None),
        columns,
        P(None, None, "tensor"),
        P(None, "tensor"),
        P(),
        P(),
        P(None, "tensor"),
        P(None, "tensor"),
        P(None, "tensor"),
        P(None, "tensor"),
        P(None, "tensor", "dp"),
        tokens,
    )
    return jax.shard_map(
        build(n_dp, n_tensor),
        mesh=mesh,
        in_specs=placed,
        out_specs=(
            tokens,
            tokens,
            P(),
            columns,
            columns,
            P(None, "dp", None),
            columns,
            P(None, None, "tensor"),
            P(None, "tensor"),
            P(),
            P(),
            P(None, "tensor"),
            P(None, "tensor"),
            P(None, "tensor"),
            P(None, "tensor"),
            P(None, "tensor", "dp"),
        ),
        check_vma=False,
    )
```

```python
import functools

import jax
import jax.numpy as jnp
import numpy as np
from jax import lax
from jax.experimental import pallas as pl
from jax.experimental.pallas import tpu as pltpu
from jax.sharding import PartitionSpec as P

INNER = 3072
HEADDIM = 64
STATE = 128
LAYERS = 2
EPSILON = 1e-05
HALO = 16
CHUNK = 128
LANES = 128

BF = jnp.bfloat16
F32 = jnp.float32
EXACT = lax.Precision.HIGHEST


def dot(left, right, dims=((1,), (0,)), precision=None):
    return lax.dot_general(
        left, right, (dims, ((), ())), preferred_element_type=F32, precision=precision
    )


def split(values):
    high = values.astype(BF)
    return high, (values - high.astype(F32)).astype(BF)


def spread(values, e2_ref):
    return dot(jnp.concatenate(split(values), axis=1), e2_ref[...])


def head_sum(values, hm_ref):
    high, low = split(values)
    return dot(high, hm_ref[...]) + dot(low, hm_ref[...])


def softplus(values):
    return jnp.maximum(values, 0.0) + jnp.log1p(jnp.exp(-jnp.abs(values)))


def triangle(size, lower):
    rows = lax.broadcasted_iota(jnp.int32, (size, size), 0)
    cols = lax.broadcasted_iota(jnp.int32, (size, size), 1)
    return rows >= cols if lower else rows <= cols


def convolve(window, marks, cw, lanes):
    size = window.shape[0] - 8
    total = cw[4:5, lanes] + cw[3:4, lanes] * window[8:]
    for lag in (1, 2, 3):
        earlier = window[8 - lag : 8 - lag + size]
        total = total + cw[3 - lag : 4 - lag, lanes] * (earlier * marks[:, lag - 1 : lag])
    return total


def place(at_ref, j, side, piece, block):
    return pl.multiple_of((at_ref[0] ^ j) * piece + side * block, block)


def fetch_front(at_ref, pieces, w_ref, sems):
    size = pieces[0].shape[0]
    copies = []
    for j, piece in enumerate(pieces):
        row = pl.multiple_of((at_ref[2] ^ j) * size, size) if len(pieces) > 1 else 0
        copies.append(pltpu.make_async_copy(piece, w_ref.at[pl.ds(row, size), :], sems.at[j]))
    for copy in copies:
        copy.start()
    return copies


def start_copy(source, target, sem):
    copy = pltpu.make_async_copy(source, target, sem)
    copy.start()
    return copy


def fetch_rest(rest_ref, low, w_ref, sem):
    copy = pltpu.make_async_copy(rest_ref.at[:, pl.ds(low, w_ref.shape[1])], w_ref, sem)
    copy.start()
    return copy


def front_kernel(*refs, inner, half_size, chips, ready):
    at_ref, refs = refs[0], refs[1:]
    ours, theirs, refs = refs[:half_size], refs[half_size : 2 * half_size], refs[2 * half_size :]
    pieces, refs = refs[:chips], refs[chips:]
    cm_ref, lnk_ref, cw_ref, hp_ref, e2_ref = refs[:5]
    (far_toks_ref, far_raw_ref, head_ref, xb_ref, aux_ref, sloc_ref, tail_ref, edge_ref, send_ref,
     state_ref, raw_ref, w_ref, toks_ref, rawl_ref, sems) = refs[-15:]
    copies = fetch_front(at_ref, pieces, w_ref, sems)
    count = xb_ref.shape[0]
    wide = inner + 2 * STATE
    block = ours[0].shape[0]
    core = at_ref[1]
    toks_ref[:HALO, :] = jnp.zeros((HALO, toks_ref.shape[1]), BF)
    for j in range(half_size):
        for part, side in ((ours[j], core), (theirs[j], 1 - core)):
            row = place(at_ref, j, side, 2 * block, block) + HALO
            toks_ref[pl.ds(pl.multiple_of(row, HALO), block), :] = part[...]
    leaving = [start_copy(toks_ref, far_toks_ref, sems.at[chips])]
    for copy in copies:
        copy.wait()
    for low in range(0, wide + LANES, 2 * LANES):
        lanes = slice(low, min(low + 2 * LANES, wide + LANES))
        raw_ref[:, lanes] = dot(toks_ref[...], w_ref[:, lanes])
        rawl_ref[:, lanes] = raw_ref[:, lanes].astype(BF)
    leaving.append(start_copy(rawl_ref, far_raw_ref, sems.at[chips + 1]))
    head_ref[...] = raw_ref[HALO : 2 * HALO, :wide]
    tail_ref[...] = raw_ref[count + HALO - 8 :, :wide]
    edge_ref[...] = toks_ref[count:, :]
    ready()
    lower = triangle(CHUNK, True).astype(F32)
    state_ref[...] = jnp.zeros_like(state_ref)

    def step_chunk(k, carry):
        base = pl.multiple_of(k * CHUNK, CHUNK)
        here = pl.ds(base, CHUNK)
        marks = cm_ref[pl.ds(base + HALO, CHUNK), :]
        for low in range(0, wide, STATE):
            lanes = slice(low, low + STATE)
            window = raw_ref[pl.ds(base + HALO - 8, CHUNK + 8), lanes]
            pre = convolve(window, marks, cw_ref, lanes)
            xb_ref[here, lanes] = (pre * jax.nn.sigmoid(pre)).astype(BF)
        raw_dt = raw_ref[pl.ds(base + HALO, CHUNK), wide:]
        step = softplus(raw_dt + hp_ref[0:1, :])
        cum = dot(lower, -hp_ref[1:2, :] * step, precision=EXACT)
        aux_ref[here, :LANES] = step
        aux_ref[here, LANES:] = cum
        end = cum[CHUNK - 1 :, :]
        gain = jnp.exp(end - cum) * marks[:, 3:4] * step
        scaled = (spread(gain, e2_ref) * xb_ref[here, :inner].astype(F32)).astype(BF)
        b_rows = xb_ref[here, inner : inner + STATE]
        local = dot(b_rows, scaled, ((0,), (0,)))
        keep = spread(jnp.exp(end) * lnk_ref[pl.ds(k * 8, 8), :], e2_ref)[0:1]
        sloc_ref[k] = state_ref[...].astype(BF)
        state_ref[...] = keep * state_ref[...] + local
        return carry

    lax.fori_loop(0, count // CHUNK, step_chunk, 0)
    send_ref[...] = state_ref[...].astype(BF)
    for copy in leaving:
        copy.wait()


def pair_lanes(values, lane):
    high = values.astype(BF).astype(F32)
    return jnp.where(lane == 0, high, jnp.where(lane == 1, values - high, 0.0)).astype(BF)


def read_pair(tile):
    return tile[:, 0:1].astype(F32) + tile[:, 1:2].astype(F32)


def scan_kernel(*refs, inner, half_size, ready):
    (at_ref, far_toks_ref, old_ref, rest_ref, aux_ref, sloc_ref, send_ref, sin_ref, tail_ref,
     head_ref, cm_ref, segr_ref, lnk_ref, gp_ref, cw_ref, e2_ref) = refs[:16]
    (*far_refs, part_ref, xb_ref, zl_ref, core_ref, act_ref, sst_ref, toks_ref,
     extra_ref, z_ref, wz_ref, wo_ref, sems) = refs[-17:]
    copy_toks = start_copy(far_toks_ref, toks_ref, sems.at[2])
    copy_z = fetch_rest(rest_ref, 0, wz_ref, sems.at[0])
    copy_out = fetch_rest(rest_ref, inner, wo_ref, sems.at[1])
    count = xb_ref.shape[0]
    wide = inner + 2 * STATE
    width = toks_ref.shape[1]
    lower = triangle(CHUNK, True)
    lane = lax.broadcasted_iota(jnp.int32, (CHUNK, STATE), 1)
    first = lane < HEADDIM
    copy_toks.wait()
    copy_z.wait()
    for low in range(0, inner, 2 * LANES):
        lanes = slice(low, min(low + 2 * LANES, inner))
        z_ref[:, lanes] = dot(toks_ref[HALO:, :], wz_ref[:, lanes])
    ready()
    xb_ref[...] = old_ref[...]
    marks = cm_ref[HALO : 2 * HALO, :]
    for low in range(0, wide, STATE):
        lanes = slice(low, low + STATE)
        window = jnp.concatenate([tail_ref[:, lanes], head_ref[:, lanes]], axis=0)
        pre = convolve(window, marks, cw_ref, lanes)
        xb_ref[:HALO, lanes] = (pre * jax.nn.sigmoid(pre)).astype(BF)
    end = aux_ref[CHUNK - 1 : CHUNK, LANES:]
    gain = jnp.exp(end - aux_ref[:HALO, LANES:]) * marks[:, 3:4] * aux_ref[:HALO, :LANES]
    gain = spread(gain, e2_ref)

    def local_state(rows):
        scaled = (gain * rows[:, :inner].astype(F32)).astype(BF)
        return dot(rows[:, inner : inner + STATE], scaled, ((0,), (0,)))

    change = local_state(xb_ref[:HALO, :]) - local_state(old_ref[:HALO, :])
    extra_ref[...] = sin_ref[...].astype(F32)

    def step_chunk(k, carry):
        base = pl.multiple_of(k * CHUNK, CHUNK)
        here = pl.ds(base, CHUNK)
        marks = cm_ref[pl.ds(base + HALO, CHUNK), :]
        incoming = (sloc_ref[k].astype(F32) + extra_ref[...]).astype(BF)
        sst_ref[k] = incoming
        b_rows = xb_ref[here, inner : inner + STATE]
        c_rows = xb_ref[here, inner + STATE : inner + 2 * STATE]
        scores = dot(c_rows, b_rows, ((1,), (1,)))
        allowed = (marks[:, 5:6] == segr_ref[0:1, here]) & lower
        scores = jnp.where(allowed, scores, 0.0)
        step = aux_ref[here, :LANES]
        cum = aux_ref[here, LANES:]
        cum_t = jnp.transpose(cum)
        step_wide = spread(step, e2_ref)
        carried = spread(jnp.exp(cum) * marks[:, 4:5], e2_ref) * dot(c_rows, incoming)
        squares = jnp.zeros((CHUNK, STATE), F32)
        for pair in range(inner // STATE):
            lanes = slice(pair * STATE, (pair + 1) * STATE)
            x_rows = xb_ref[here, lanes].astype(F32)
            scaled = step_wide[:, lanes] * x_rows
            within = carried[:, lanes] + gp_ref[1:2, lanes] * x_rows
            for half in range(2):
                head = 2 * pair + half
                decay = jnp.exp(
                    jnp.minimum(cum[:, head : head + 1] - cum_t[head : head + 1, :], 0.0)
                )
                mine = first if half == 0 else ~first
                part = jnp.where(mine, scaled, 0.0).astype(BF)
                within = within + dot((scores * decay).astype(BF), part)
            core_ref[here, lanes] = within
            z_rows = z_ref[here, lanes]
            zl_ref[here, lanes] = z_rows.astype(BF)
            gated = within * (z_rows * jax.nn.sigmoid(z_rows))
            act_ref[here, lanes] = (gated * gp_ref[0:1, lanes]).astype(BF)
            squares = squares + gated * gated
        part_ref[here, width:] = jnp.where(lane == 0, jnp.sum(squares, axis=1, keepdims=True), 0.0)
        end = cum[CHUNK - 1 :, :]
        keep = spread(jnp.exp(end) * lnk_ref[pl.ds(k * 8, 8), :], e2_ref)[0:1]
        extra_ref[...] = keep * extra_ref[...] + jnp.where(k == 0, change, 0.0)
        return carry

    chunks = count // CHUNK
    lax.fori_loop(0, chunks, step_chunk, 0)
    sst_ref[chunks] = (send_ref[...].astype(F32) + extra_ref[...]).astype(BF)
    here_refs = (xb_ref, zl_ref, core_ref, act_ref, sst_ref)
    leaving = [
        start_copy(near, far, sems.at[3 + i]) for i, (near, far) in enumerate(zip(here_refs, far_refs))
    ]
    copy_out.wait()
    for low in range(0, width, 2 * LANES):
        lanes = slice(low, low + 2 * LANES)
        part_ref[:, lanes] = dot(act_ref[...], wo_ref[lanes, :], ((1,), (1,)))
    for copy in leaving:
        copy.wait()


def sum_kernel(*refs, half_size, offset, noted, ready):
    at_ref, part_ref, came_ref = refs[:3]
    outs = refs[-half_size:] if noted else refs[-half_size - 1 : -1]
    block = outs[0].shape[0]
    width = part_ref.shape[1] - (LANES if noted else 0)
    lane = lax.broadcasted_iota(jnp.int32, (block, LANES), 1)
    for j in range(half_size):
        at = slice(j * block, (j + 1) * block)
        row = place(at_ref, j, at_ref[1], 2 * block, block) + offset
        stay = pl.ds(pl.multiple_of(row, HALO), block)
        total = part_ref[stay, :width] + came_ref[at, :width].astype(F32)
        outs[j][:, :width] = total.astype(outs[j].dtype)
        if noted:
            line = part_ref[stay, width : width + 1] + read_pair(came_ref[at, width:])
            if j == 0:
                outs[j][:, width:] = jnp.where(lane == 0, line, 0.0)
            else:
                outs[j][:, width:] = pair_lanes(line, lane)
    if offset:
        low = half_size * block
        refs[-1][...] = (part_ref[:offset, :] + came_ref[low:, :].astype(F32)).astype(BF)


def normalize(values, gain_ref):
    size = 1.0 / values.shape[1]
    inv_rms = lax.rsqrt(jnp.sum(values * values, axis=1, keepdims=True) * size + EPSILON)
    return values * inv_rms * gain_ref[0:1, :]


def grad_message(msg_ref, grad, mixed, inv_gate):
    width = grad.shape[1]
    scaled = (inv_gate * grad).astype(BF)
    msg_ref[:, :width] = scaled
    weight = jnp.sum(scaled.astype(F32) * mixed, axis=1, keepdims=True)
    lane = lax.broadcasted_iota(jnp.int32, (grad.shape[0], LANES), 1)
    msg_ref[:, width:] = pair_lanes(inv_gate * inv_gate * weight * (1.0 / INNER), lane)


def first_kernel(*refs, ready):
    x_ref, gain_ref = refs[:2]
    res_ref, normed_ref = refs[-2:]
    values = x_ref[...].astype(F32)
    res_ref[...] = values
    normed_ref[...] = normalize(values, gain_ref).astype(BF)


def own_kernel(*refs, half_size, top, ready):
    ready()
    sum_ref, others, refs = refs[0], refs[1:half_size], refs[half_size:]
    res_ref, more_ref = refs[:2]
    mixed_ref, gate_ref, new_ref, msg_ref = refs[-4:]
    width = res_ref.shape[1]
    mixed = sum_ref[:, :width]
    line = sum_ref[:, width : width + 1]
    for other in others:
        mixed = mixed + other[:, :width].astype(F32)
        line = line + read_pair(other[:, width:])
    inv_gate = lax.rsqrt(line * (1.0 / INNER) + EPSILON)
    mixed_ref[...] = mixed
    gate_ref[...] = jnp.broadcast_to(inv_gate, gate_ref.shape)
    values = res_ref[...] + inv_gate * mixed
    new_ref[...] = values
    if top:
        grad_message(msg_ref, more_ref[...], mixed, inv_gate)
    else:
        msg_ref[...] = normalize(values, more_ref).astype(BF)


def own_back_kernel(*refs, half_size, bottom, ready):
    ready()
    sum_ref, others, refs = refs[0], refs[1:half_size], refs[half_size:]
    halos, refs = refs[:half_size], refs[half_size:]
    grad_ref, res_ref, gain_ref = refs[:3]
    if bottom:
        new_ref, gnorm_ref, buf_ref = refs[-3:]
    else:
        mixed_ref, gate_ref = refs[3:5]
        new_ref, gnorm_ref, msg_ref, buf_ref = refs[-4:]
    block = sum_ref.shape[0]
    total = sum_ref[...]
    for other in others:
        total = total + other[...].astype(F32)
    buf_ref[...] = total
    for halo in halos:
        buf_ref[block - HALO :, :] += halo[...].astype(F32)
    total = buf_ref[...]
    values = res_ref[...]
    size = 1.0 / values.shape[1]
    inv_rms = lax.rsqrt(jnp.sum(values * values, axis=1, keepdims=True) * size + EPSILON)
    gnorm = jnp.sum(total * values * inv_rms, axis=0, keepdims=True)
    gnorm_ref[...] = jnp.broadcast_to(gnorm, gnorm_ref.shape)
    scaled = total * gain_ref[0:1, :]
    inner_term = jnp.sum(scaled * values, axis=1, keepdims=True) * size
    grad = grad_ref[...] + inv_rms * scaled - values * (inv_rms * inv_rms * inv_rms) * inner_term
    new_ref[...] = grad
    if not bottom:
        grad_message(msg_ref, grad, mixed_ref[...], gate_ref[:, 0:1])


def gate_back_kernel(*refs, inner, half_size, ready):
    at_ref, refs = refs[0], refs[1:]
    ours, theirs, refs = refs[:half_size], refs[half_size : 2 * half_size], refs[2 * half_size :]
    rest_ref, far_core_ref, far_z_ref, far_xb_ref, aux_ref, cm_ref, lnk_ref, gp_ref, e2_ref = refs[:9]
    (far_grows_ref, gcore_ref, gz_ref, ggain_ref, dsin_ref, state_ref, gg_ref, coef_ref,
     wo_ref, core_ref, z_ref, xb_ref, grows_ref, sems) = refs[-14:]
    copy_out = fetch_rest(rest_ref, inner, wo_ref, sems.at[0])
    copies = [
        start_copy(far_core_ref, core_ref, sems.at[1]),
        start_copy(far_z_ref, z_ref, sems.at[2]),
        start_copy(far_xb_ref, xb_ref, sems.at[3]),
    ]
    count = xb_ref.shape[0]
    chunks = count // CHUNK
    width = grows_ref.shape[1]
    block = ours[0].shape[0]
    core_at = at_ref[1]
    for j in range(half_size):
        for part, side in ((ours[j], core_at), (theirs[j], 1 - core_at)):
            at = pl.ds(place(at_ref, j, side, 2 * block, block), block)
            grows_ref[at, :] = part[:, :width]
            coef_ref[at, :] = jnp.broadcast_to(read_pair(part[:, width:]), (block, LANES))
    leaving = start_copy(grows_ref, far_grows_ref, sems.at[4])
    copy_out.wait()
    for low in range(0, inner, 2 * LANES):
        lanes = slice(low, min(low + 2 * LANES, inner))
        gg_ref[:, lanes] = dot(grows_ref[...], wo_ref[:, lanes])
    for copy in copies:
        copy.wait()
    ready()
    state_ref[...] = jnp.zeros_like(state_ref)
    ggain_ref[...] = jnp.zeros_like(ggain_ref)
    gz_ref[:HALO, :] = jnp.zeros((HALO, inner), BF)

    def step_chunk(turn, carry):
        k = chunks - 1 - turn
        base = pl.multiple_of(k * CHUNK, CHUNK)
        here = pl.ds(base, CHUNK)
        there = pl.ds(pl.multiple_of(base + HALO, HALO), CHUNK)
        marks = cm_ref[there, :]
        coef = coef_ref[here, 0:1]
        cum = aux_ref[here, LANES:]
        entry = spread(jnp.exp(cum) * marks[:, 4:5], e2_ref)
        c_rows = xb_ref[here, inner + STATE : inner + 2 * STATE]
        end = cum[CHUNK - 1 :, :]
        keep = spread(jnp.exp(end) * lnk_ref[pl.ds(k * 8, 8), :], e2_ref)[0:1]
        for pair in range(inner // STATE):
            lanes = slice(pair * STATE, (pair + 1) * STATE)
            z_rows = z_ref[here, lanes].astype(F32)
            core = core_ref[here, lanes]
            grad = gg_ref[here, lanes]
            sig = jax.nn.sigmoid(z_rows)
            act = z_rows * sig
            gated = core * act
            ggain_ref[0:1, lanes] += jnp.sum(grad * gated, axis=0, keepdims=True)
            grad_gated = gp_ref[0:1, lanes] * grad - coef * gated
            gcore = (grad_gated * act).astype(BF)
            gcore_ref[here, lanes] = gcore
            gz_ref[there, lanes] = (
                grad_gated * core * (sig * (1.0 + z_rows * (1.0 - sig)))
            ).astype(BF)
            scaled = (entry[:, lanes] * gcore.astype(F32)).astype(BF)
            state_ref[:, lanes] = keep[:, lanes] * state_ref[:, lanes] + dot(
                c_rows, scaled, ((0,), (0,))
            )
        return carry

    lax.fori_loop(0, chunks, step_chunk, 0)
    dsin_ref[...] = state_ref[...].astype(BF)
    leaving.wait()


def scan_back_kernel(*refs, inner, half_size, chips, ready):
    at_ref, refs = refs[0], refs[1:]
    pieces, refs = refs[:chips], refs[chips:]
    (rest_ref, far_raw_ref, far_xb_ref, far_core_ref, far_sst_ref, gcore_ref, gz_ref, aux_ref,
     dso_ref, tail_ref, cm_ref, segr_ref, lnk_ref, gp_ref, cw_ref, hp_ref, e2_ref, hm_ref) = refs[:18]
    (graw_ref, sgrad_ref, hgrad_ref, part_ref, state_ref, dpre_ref, qv_ref, xd_ref,
     raw_ref, wf_ref, wz_ref, xb_ref, core_ref, sst_ref, sems) = refs[-15:]
    first_copies = [
        start_copy(far_xb_ref, xb_ref, sems.at[chips + 2]),
        start_copy(far_sst_ref, sst_ref, sems.at[chips + 3]),
        start_copy(far_core_ref, core_ref, sems.at[chips + 4]),
    ]
    copy_raw = start_copy(far_raw_ref, raw_ref, sems.at[chips])
    copies = fetch_front(at_ref, pieces, wf_ref, sems)
    copies.append(fetch_rest(rest_ref, 0, wz_ref, sems.at[chips + 1]))
    count = xb_ref.shape[0]
    chunks = count // CHUNK
    wide = inner + 2 * STATE
    upper = triangle(CHUNK, False)
    first = lax.broadcasted_iota(jnp.int32, (CHUNK, STATE), 1) < HEADDIM
    state_ref[...] = dso_ref[...].astype(F32)
    sgrad_ref[...] = jnp.zeros_like(sgrad_ref)
    hgrad_ref[...] = jnp.zeros_like(hgrad_ref)
    dpre_ref[:HALO, :] = jnp.zeros((HALO, wide), F32)
    dpre_ref[HALO + count :, :] = jnp.zeros((HALO, wide), F32)
    graw_ref[:HALO, wide:] = jnp.zeros((HALO, LANES), BF)

    ready()
    for copy in first_copies:
        copy.wait()
    copy_raw.wait()
    raw_ref[:HALO, :wide] = jnp.concatenate(
        [jnp.zeros((HALO - 8, wide), F32), tail_ref[...]], axis=0
    ).astype(BF)

    def step_chunk(turn, carry):
        k = chunks - 1 - turn
        base = pl.multiple_of(k * CHUNK, CHUNK)
        here = pl.ds(base, CHUNK)
        there = pl.ds(pl.multiple_of(base + HALO, HALO), CHUNK)
        marks = cm_ref[there, :]
        step = aux_ref[here, :LANES]
        cum = aux_ref[here, LANES:]
        cum_t = jnp.transpose(cum)
        end = cum[CHUNK - 1 :, :]
        b_rows = xb_ref[here, inner : inner + STATE]
        c_rows = xb_ref[here, inner + STATE : wide]
        after = state_ref[...]
        after_low = after.astype(BF)
        product = jnp.sum(
            sst_ref[k + 1].astype(F32) * after_low.astype(F32), axis=0, keepdims=True
        )
        at_end = head_sum(jnp.broadcast_to(product, (8, inner)), hm_ref)[0:1]
        scores_t = dot(b_rows, c_rows, ((1,), (1,)))
        allowed = (marks[:, 5:6] == segr_ref[0:1, here]) & upper
        scores_t = jnp.where(allowed, scores_t, 0.0)
        gain = spread(jnp.exp(end - cum) * marks[:, 3:4], e2_ref)
        step_wide = spread(step, e2_ref)
        entry = spread(jnp.exp(cum) * marks[:, 4:5], e2_ref)
        keep = spread(jnp.exp(end) * lnk_ref[pl.ds(k * 8, 8), :], e2_ref)[0:1]
        outer = gain * dot(b_rows, after_low)
        scaled_grad = (entry * gcore_ref[here, :].astype(F32)).astype(BF)
        grad_c = dot(scaled_grad, sst_ref[k], ((1,), (1,)))
        scaled_x = (gain * (step_wide * xb_ref[here, :inner].astype(F32))).astype(BF)
        grad_b = dot(scaled_x, after_low, ((1,), (1,)))
        state_ref[...] = keep * after + dot(c_rows, scaled_grad, ((0,), (0,)))
        grad_scores = jnp.zeros((CHUNK, CHUNK), F32)
        for pair in range(inner // STATE):
            lanes = slice(pair * STATE, (pair + 1) * STATE)
            grad_low = gcore_ref[here, lanes]
            grad = grad_low.astype(F32)
            x_rows = xb_ref[here, lanes].astype(F32)
            wide_step = step_wide[:, lanes]
            scaled = wide_step * x_rows
            grad_u = outer[:, lanes]
            for half in range(2):
                head = 2 * pair + half
                decay = jnp.exp(
                    jnp.minimum(cum_t[head : head + 1, :] - cum[:, head : head + 1], 0.0)
                )
                mine = first if half == 0 else ~first
                part = jnp.where(mine, scaled, 0.0).astype(BF)
                grad_part = jnp.where(mine, grad, 0.0).astype(BF)
                grad_u = grad_u + dot((scores_t * decay).astype(BF), grad_part)
                grad_scores = grad_scores + dot(part, grad_low, ((1,), (1,))) * decay
            skip = gp_ref[1:2, lanes]
            qv_ref[:, lanes] = grad * (core_ref[here, lanes] - skip * x_rows) - (
                scaled.astype(BF).astype(F32) * grad_u
            )
            xd_ref[:, lanes] = x_rows * grad_u
            dpre_ref[there, lanes] = wide_step * grad_u + skip * grad
            sgrad_ref[5:6, lanes] += jnp.sum(grad * x_rows, axis=0, keepdims=True)
        grad_scores = jnp.where(allowed, grad_scores, 0.0).astype(BF)
        dpre_ref[there, inner : inner + STATE] = grad_b + dot(grad_scores, c_rows)
        dpre_ref[there, inner + STATE :] = grad_c + dot(grad_scores, b_rows, ((0,), (0,)))
        rate = hp_ref[1:2, :]
        grad_log = dot(upper.astype(F32), head_sum(qv_ref[...], hm_ref), precision=EXACT) + at_end
        grad_step = head_sum(xd_ref[...], hm_ref) - rate * grad_log
        raw_dt = raw_ref[there, wide:].astype(F32)
        grad_dt = grad_step * jax.nn.sigmoid(raw_dt + hp_ref[0:1, :])
        graw_ref[there, wide:] = grad_dt.astype(BF)
        hgrad_ref[0:1, :] += jnp.sum(grad_dt, axis=0, keepdims=True)
        hgrad_ref[1:2, :] -= rate * jnp.sum(step * grad_log, axis=0, keepdims=True)
        return carry

    lax.fori_loop(0, chunks, step_chunk, 0)

    def conv_chunk(k, carry):
        base = pl.multiple_of(k * CHUNK, CHUNK)
        there = pl.ds(pl.multiple_of(base + HALO, HALO), CHUNK)
        marks = cm_ref[there, :]
        for low in range(0, wide, STATE):
            lanes = slice(low, low + STATE)
            window = raw_ref[pl.ds(base, CHUNK + HALO), lanes].astype(F32)[HALO - 8 :]
            pre = convolve(window, marks, cw_ref, lanes)
            sig = jax.nn.sigmoid(pre)
            grad = dpre_ref[there, lanes] * (sig * (1.0 + pre * (1.0 - sig)))
            dpre_ref[there, lanes] = grad
            sgrad_ref[4:5, lanes] += jnp.sum(grad, axis=0, keepdims=True)
            sgrad_ref[3:4, lanes] += jnp.sum(grad * window[8:], axis=0, keepdims=True)
            for lag in (1, 2, 3):
                earlier = window[8 - lag : 8 - lag + CHUNK]
                sgrad_ref[3 - lag : 4 - lag, lanes] += jnp.sum(
                    grad * (earlier * marks[:, lag - 1 : lag]), axis=0, keepdims=True
                )
        return carry

    lax.fori_loop(0, chunks, conv_chunk, 0)

    def transpose_rows(start, size):
        marks = cm_ref[pl.ds(start, size + 8), :]
        for low in range(0, wide, STATE):
            lanes = slice(low, low + STATE)
            window = dpre_ref[pl.ds(start, size + 8), lanes]
            total = cw_ref[3:4, lanes] * window[:size]
            for lag in (1, 2, 3):
                masked = window[lag : lag + size] * marks[lag : lag + size, lag - 1 : lag]
                total = total + cw_ref[3 - lag : 4 - lag, lanes] * masked
            graw_ref[pl.ds(start, size), lanes] = total.astype(BF)

    transpose_rows(0, HALO)

    def back_chunk(k, carry):
        transpose_rows(pl.multiple_of(k * CHUNK + HALO, HALO), CHUNK)
        return carry

    lax.fori_loop(0, chunks, back_chunk, 0)
    width = part_ref.shape[1]
    for copy in copies:
        copy.wait()
    for low in range(0, width, 2 * LANES):
        lanes = slice(low, low + 2 * LANES)
        part_ref[:, lanes] = dot(gz_ref[...], wz_ref[lanes, :], ((1,), (1,))) + dot(
            graw_ref[...], wf_ref[lanes, :], ((1,), (1,))
        )


def weight_kernel(*refs, terms, tokens, halo, far, pieces, ready):
    refs = list(refs)
    sems = refs.pop()
    at_ref = refs.pop(0) if pieces else None
    out_ref = refs.pop()
    near = refs[-len(far) :]
    outs = refs[len(refs) - len(far) - max(pieces, 1) : len(refs) - len(far)]
    leaving = []
    copies = {}
    for i, (place_of, target) in enumerate(zip(far, near)):
        copies[place_of] = start_copy(refs[place_of], target, sems.at[i])
        refs[place_of] = target
    ready()
    tile = 2 * LANES
    low = 0
    for term in range(terms):
        left_a, right_a, left_b, right_b = refs[4 * term : 4 * term + 4]
        size = right_a.shape[1]
        for place_of in range(4 * term, 4 * term + 4):
            if place_of in copies:
                copies[place_of].wait()

        def step_tile(r, carry):
            at = pl.ds(pl.multiple_of(r * tile, tile), tile)
            skip_l, skip_r = left_a.shape[0] - tokens, right_a.shape[0] - tokens
            total = dot(left_a[skip_l:, at], right_a[skip_r:, :], ((0,), (0,)))
            total = total + dot(left_b[skip_l:, at], right_b[skip_r:, :], ((0,), (0,)))
            if halo:
                edges = jnp.concatenate([edge[:, at] for edge in refs[4 * terms : 4 * terms + 2]])
                heads = jnp.concatenate([right_a[:HALO, :], right_b[:HALO, :]])
                total = total + dot(edges, heads, ((0,), (0,)))
            out_ref[at, low : low + size] = total.astype(BF)
            return carry

        lax.fori_loop(0, out_ref.shape[0] // tile, step_tile, 0)
        if not pieces:
            lanes = pl.ds(low, size)
            leaving.append(
                start_copy(out_ref.at[:, lanes], outs[0].at[:, lanes], sems.at[len(far) + term])
            )
        low += size
    for copy in leaving:
        copy.wait()
    if pieces:
        for j, piece_ref in enumerate(outs):
            size = piece_ref.shape[0]
            row = pl.multiple_of((at_ref[2] ^ j) * size, size)
            piece_ref[...] = out_ref[pl.ds(row, size), :]


def hold_kernel(*refs, ready):
    refs[-1][...] = refs[0][...]


def pick_kernel(*refs, inner, shard, layer, front, rest, ready):
    ready()
    at_ref, one_ref, two_ref = refs[:3]
    outs = refs[-(front + rest) :]
    for side in range(2):
        rows = slice(side * shard, (side + 1) * shard)
        value = jnp.where(at_ref[3] == side, one_ref[...], two_ref[...])
        low = 0
        if front:
            own_ref, other_ref = refs[3:5]
            outs[0][rows, :inner] = value[:, :inner]
            outs[0][rows, inner : inner + 2 * STATE] = jnp.where(
                at_ref[1] == side, own_ref[layer], other_ref[layer]
            )
            outs[0][rows, inner + 2 * STATE :] = value[:, inner : inner + LANES]
            low = inner + LANES
        if rest:
            outs[-1][rows, :] = value[:, low:]


def split_kernel(*refs, terms, shard, inner, front, ready):
    ready()
    at_ref, refs = refs[0], refs[1:]
    buf_ref = refs[-1]
    buf_ref[...] = tree_sum([ref[...] for ref in refs[:terms]])
    half, core = at_ref[3], at_ref[1]
    if front:
        one_ref, two_ref, keep_ref, away_ref = refs[-5:-1]
    else:
        one_ref, two_ref = refs[-3:-1]
    for out_ref, side in ((one_ref, half), (two_ref, 1 - half)):
        rows = pl.ds(pl.multiple_of(side * shard, HALO), shard)
        if front:
            out_ref[:, :inner] = buf_ref[rows, :inner].astype(BF)
            out_ref[:, inner:] = buf_ref[rows, inner + 2 * STATE :].astype(BF)
        else:
            out_ref[...] = buf_ref[rows, :].astype(BF)
    if front:
        lanes = slice(inner, inner + 2 * STATE)
        rows = pl.ds(pl.multiple_of(core * shard, HALO), shard)
        keep_ref[...] = buf_ref[rows, lanes]
        rows = pl.ds(pl.multiple_of((1 - core) * shard, HALO), shard)
        away_ref[...] = buf_ref[rows, lanes].astype(BF)


def final_kernel(*refs, layers, inner, heads, tensors, chips, ready):
    (gz_ref, gx_ref, gbc_ref, gdt_ref, gout_ref, taps_ref, bias_ref, taps_bc_ref, bias_bc_ref,
     dt_ref, log_ref, skip_ref, gate_ref, norm_ref) = refs[-14:]
    low = layers * (4 + tensors)
    small = tree_sum([ref[...] for ref in refs[low : low + chips]])
    hm_ref = refs[low + chips]
    for l in range(layers):
        rest_one, rest_two, front_one, front_two = refs[4 * l : 4 * l + 4]
        total = rest_one[...].astype(F32) + rest_two[...].astype(F32)
        gz_ref[l] = total[:, :inner]
        gout_ref[l] = total[:, inner:]
        total = front_one[...].astype(F32) + front_two[...].astype(F32)
        gx_ref[l] = total[:, :inner]
        gdt_ref[l] = total[:, inner : inner + heads]
        low = 4 * layers + l * tensors
        gbc_ref[l] = tree_sum([ref[...] for ref in refs[low : low + tensors]])
        row = slice(l, l + 1)
        mine = small[l]
        taps_ref[l] = mine[0:4, :inner]
        bias_ref[row, :] = mine[4:5, :inner]
        gate_ref[row, :] = mine[5:6, :inner]
        skips = dot(mine[0:8, :inner], hm_ref[...].astype(F32), precision=EXACT)
        skip_ref[row, :] = skips[6:7, :heads]
        dt_ref[row, :] = mine[7:8, :heads]
        log_ref[row, :] = mine[7:8, LANES : LANES + heads]
        taps_bc_ref[l] = mine[8:12, : 2 * STATE]
        bias_bc_ref[row, :] = mine[12:13, : 2 * STATE]
        norm_ref[row, :] = mine[13:14, :]


def nothing_kernel(*refs):
    pass


def gate_kernel(*refs, terms, ready):
    for source, target in zip(refs[:terms], refs[-terms:]):
        target[...] = source[...]


def away_kernel(*refs, half_size, offset, noted, ready):
    at_ref, part_ref, away_ref = refs[0], refs[1], refs[-1]
    block = (part_ref.shape[0] - offset) // (2 * half_size)
    width = part_ref.shape[1] - (LANES if noted else 0)
    lane = lax.broadcasted_iota(jnp.int32, (block, LANES), 1)
    for j in range(half_size):
        to = slice(j * block, (j + 1) * block)
        row = place(at_ref, j, 1 - at_ref[1], 2 * block, block) + offset
        go = pl.ds(pl.multiple_of(row, HALO), block)
        away_ref[to, :width] = part_ref[go, :width].astype(BF)
        if noted:
            away_ref[to, width:] = pair_lanes(part_ref[go, width : width + 1], lane)
    if offset:
        away_ref[half_size * block :, :] = part_ref[:offset, :].astype(BF)


def touch_kernel(*refs, ready):
    refs[-1][...] = jnp.zeros_like(refs[-1])


def tree_sum(values):
    values = [v.astype(F32) for v in values]
    while len(values) > 1:
        values = [a + b for a, b in zip(values[::2], values[1::2])]
    return values[0]


def add_kernel(*refs, terms, ready):
    refs[-1][...] = tree_sum([ref[...] for ref in refs[:terms]]).astype(refs[-1].dtype)


def pack_kernel(*refs, inner, layers, ready):
    out_ref = refs[-1]
    out_ref[...] = jnp.zeros_like(out_ref)
    for l in range(layers):
        ggain, sgrad, hgrad, gnorm = (
            refs[8 * l + 2 * i][...] + refs[8 * l + 2 * i + 1][...] for i in range(4)
        )
        out_ref[l, 0:5, :inner] = sgrad[0:5, :inner].astype(BF)
        out_ref[l, 5:6, :inner] = ggain[0:1, :].astype(BF)
        out_ref[l, 6:7, :inner] = sgrad[5:6, :inner].astype(BF)
        out_ref[l, 7:8, :LANES] = hgrad[0:1, :].astype(BF)
        out_ref[l, 7:8, LANES : 2 * LANES] = hgrad[1:2, :].astype(BF)
        out_ref[l, 8:13, : 2 * STATE] = sgrad[0:5, inner:].astype(BF)
        out_ref[l, 13:14, :] = gnorm[0:1, :].astype(BF)


class Queue:
    def __init__(self):
        self.last = None

    def run(
        self, kernel, operands, outs, scratch=(), scalars=0, far=(), far_out=(), staged=(),
        staged_out=(), after=(), limit=10,
    ):
        near = pl.BlockSpec(memory_space=pltpu.VMEM)
        distant = pl.BlockSpec(memory_space=pltpu.HBM)
        free = pl.BlockSpec(memory_space=pl.ANY)
        extra = list(after) + ([] if self.last is None else [self.last])
        outside = set(far) | set(staged)
        outside_out = set(far_out) | set(staged_out)
        count, staged, staged_out = len(operands), list(staged), list(staged_out)

        def wrapped(*refs):
            refs = list(refs)
            sems = refs.pop()
            base = count + len(extra)
            buffers = refs[len(refs) - len(staged) - len(staged_out) :]
            refs = refs[: len(refs) - len(buffers)]
            arriving = []
            for i, position in enumerate(staged):
                arriving.append(start_copy(refs[position], buffers[i], sems.at[i]))
                refs[position] = buffers[i]
            leaving = []
            for i, position in enumerate(staged_out, len(staged)):
                leaving.append((buffers[i], refs[base + position], sems.at[i]))
                refs[base + position] = buffers[i]

            def ready():
                for copy in arriving:
                    copy.wait()

            kernel(*refs, ready=ready)
            for copy in [start_copy(*parts) for parts in leaving]:
                copy.wait()

        specs = [pl.BlockSpec(memory_space=pltpu.SMEM)] * scalars
        specs += [distant if i in outside else near for i in range(scalars, count)]
        buffers = [(operands[i].shape, operands[i].dtype) for i in staged]
        buffers += [outs[i] for i in staged_out]
        operands = [
            pltpu.with_memory_space_constraint(v, pltpu.HBM) if i in outside else v
            for i, v in enumerate(operands)
        ]
        result = pl.pallas_call(
            wrapped,
            in_specs=specs + [free] * len(extra),
            out_specs=[distant if i in outside_out else near for i in range(len(outs))],
            out_shape=[
                pltpu.HBM(s, t) if i in outside_out else jax.ShapeDtypeStruct(s, t)
                for i, (s, t) in enumerate(outs)
            ],
            scratch_shapes=[
                pltpu.SemaphoreType.DMA(s) if t is None else pltpu.VMEM(s, t)
                for s, t in [*scratch, *buffers, ((max(len(buffers), 1),), None)]
            ],
            compiler_params=pltpu.CompilerParams(vmem_limit_bytes=limit * 1024 * 1024),
            cost_estimate=pl.CostEstimate(flops=1000, bytes_accessed=1000, transcendentals=0),
        )(*operands, *extra)
        self.last = result[-1]
        return result

    def gate(self, values, after):
        return self.run(
            functools.partial(gate_kernel, terms=len(values)), values,
            [(v.shape, v.dtype) for v in values], after=after,
        )

    def pass_on(self, value, after):
        free = pl.BlockSpec(memory_space=pl.ANY)
        distant = pl.BlockSpec(memory_space=pltpu.HBM)
        extra = list(after) + ([] if self.last is value else [self.last])
        self.last = pl.pallas_call(
            nothing_kernel,
            in_specs=[distant] + [free] * len(extra),
            out_specs=distant,
            out_shape=pltpu.HBM(value.shape, value.dtype),
            input_output_aliases={0: 0},
            cost_estimate=pl.CostEstimate(flops=1000, bytes_accessed=1000, transcendentals=0),
        )(pltpu.with_memory_space_constraint(value, pltpu.HBM), *extra)
        return self.last

    def touch(self, values):
        self.run(touch_kernel, [], [((8, LANES), F32)], after=values)


def build(n_dp, n_tensor):
    axes = ("dp", "tensor")
    half_size = n_tensor // 2
    planes = [[d for d in range(n_dp) if d % 2 == c] for c in range(2)]
    plane_bits = [1 << b for b in range(1, n_dp.bit_length() - 1)]

    def pairs(route):
        found = []
        for d in range(n_dp):
            for t in range(n_tensor):
                goal = route(d, t)
                if goal is not None:
                    found.append((d * n_tensor + t, goal[0] * n_tensor + goal[1]))
        return found

    def send(value, route):
        return lax.ppermute(value, axes, pairs(route))

    def back(value, route):
        return lax.ppermute(value, axes, [(b, a) for a, b in pairs(route)])

    def to_core(d, t):
        return d ^ 1, t

    def to_plane(bits):
        return lambda d, t: (d ^ bits, t)

    def to_tensor(bits):
        return lambda d, t: (d, t ^ bits)

    def to_piece(j):
        return lambda d, t: (d, (t // half_size) * half_size + ((t % half_size) ^ j))

    def to_later(d, t):
        return (d, t + half_size) if t < half_size else None

    def to_halo(j):
        return lambda d, t: (d, half_size + j) if d % 2 == 1 and t == half_size - 1 else None

    def to_group(turn):
        def route(d, t):
            return (d & ~1) | (t % 2), t // 2 + half_size * ((d & 1) ^ turn)

        return route

    def matmul(left, right, dims=((1,), (0,))):
        return lax.dot_general(left, right, (dims, ((), ())), preferred_element_type=F32)

    def local(
        x_in, segments, norm_gain, w_z, w_x, w_bc, w_dt, conv_x, conv_x_bias, conv_bc, conv_bc_bias,
        dt_bias, a_log, d_skip, gate_gain, w_out, cotangent,
    ):
        inner = w_z.shape[2]
        heads = dt_bias.shape[1]
        piece, width = x_in.shape
        block = piece // 2
        count = half_size * piece
        rows = count + HALO
        chunks = count // CHUNK
        shard = w_z.shape[1]
        wide = inner + 2 * STATE
        place = lax.axis_index("tensor")
        dp_place = lax.axis_index("dp")
        core = dp_place % 2
        column = dp_place // 2
        half = place // half_size
        mine = place % half_size

        def cut(value, start, size):
            return lax.dynamic_slice(
                value, (start,) + (0,) * (value.ndim - 1), (size,) + value.shape[1:]
            )

        def put(value, part, start):
            return lax.dynamic_update_slice(value, part, (start,) + (0,) * (value.ndim - 1))

        def to_streams(value):
            keep, away = cut(value, core * block, block), cut(value, (1 - core) * block, block)
            came = send(away, to_core)
            return [jnp.where(core == 0, keep, came), jnp.where(core == 0, came, keep)]

        def from_streams(values):
            keep = jnp.where(core == 0, values[0], values[1])
            came = send(jnp.where(core == 0, values[1], values[0]), to_core)
            out = jnp.zeros((piece, width), F32)
            return put(put(out, keep, core * block), came, (1 - core) * block)

        def pad_lanes(value):
            return jnp.pad(value, ((0, 0), (0, LANES - value.shape[1])))

        queue = Queue()
        at = jnp.stack([mine, core, column, half]).astype(jnp.int32)
        chips = n_dp // 2

        def hold(value, after):
            return queue.run(hold_kernel, [value], [(value.shape, value.dtype)], after=after)[0]

        def regroup(value):
            return [send(value, to_group(0)), send(value, to_group(1))]

        bc_other = send(w_bc, to_core)
        def gather_plane(value):
            return lax.all_gather(value, "dp", axis=0, tiled=True, axis_index_groups=planes)

        def direct_start(values):
            return [values[0]] + [
                send(values[j % len(values)], to_plane(2 * j)) for j in range(1, chips)
            ]

        def pick(parts, l, front, rest, after=(), direct=False):
            outs = []
            if front:
                outs.append(((2 * shard, wide + LANES), BF))
            if rest:
                outs.append(((2 * shard, 2 * inner), BF))
            values = queue.run(
                functools.partial(
                    pick_kernel, inner=inner, shard=shard, layer=l, front=front, rest=rest
                ),
                [at, *parts] + ([w_bc, bc_other] if front else []),
                outs,
                scalars=1,
                after=after,
                staged_out=range(len(outs)),
            )
            if direct:
                front_w[l] = direct_start(values)
                return
            values = [gather_plane(v) for v in values]
            if front:
                front_w[l] = [values[0]]
            if rest:
                rest_w[l] = values[-1]

        def front_part(l):
            return [w_x[l], pad_lanes(w_dt[l])]

        def rest_part(l):
            return [w_z[l], w_out[l].T]

        def row(value, size):
            return jnp.pad(value, ((0, 0), (0, size - value.shape[1])))[:, None]

        head_rows = jnp.concatenate([row(v, LANES) for v in (dt_bias, a_log, d_skip)], axis=2)
        head_rows = jnp.pad(head_rows, ((0, 0), (0, 0), (0, inner - 3 * LANES)))
        packed = jnp.concatenate(
            [conv_x, conv_x_bias[:, None], gate_gain[:, None], head_rows], axis=1
        )
        packed = send(packed, to_group(0))
        taps, bias, gain_own = packed[:, :4], packed[:, 4:5], packed[:, 5:6]
        dt_own, a_own, skip_own = (packed[:, 6, i * LANES : (i + 1) * LANES] for i in range(3))
        head_ok = jnp.arange(LANES) < heads
        rate_own = jnp.where(head_ok, jnp.exp(a_own), 0.0)
        skip_wide = jnp.repeat(skip_own[:, :heads], HEADDIM, axis=1)
        conv_w = jnp.concatenate(
            [
                jnp.concatenate([taps, conv_bc], axis=2),
                jnp.concatenate([bias, conv_bc_bias[:, None]], axis=2),
                jnp.zeros((LAYERS, 3, wide), F32),
            ],
            axis=1,
        )
        gate_p = jnp.concatenate(
            [gain_own, skip_wide[:, None], jnp.zeros((LAYERS, 6, inner), F32)], axis=1
        )
        head_p = jnp.concatenate(
            [dt_own[:, None], rate_own[:, None], jnp.zeros((LAYERS, 6, LANES), F32)], axis=1
        )
        member = np.arange(inner)[None, :] // HEADDIM == np.arange(LANES)[:, None]
        e2 = jnp.asarray(np.concatenate([member, member], axis=0), BF)
        hm = jnp.asarray(member.T, BF)

        seg = jnp.concatenate([jnp.full((HALO,), -1.0, F32), segments.astype(F32)])
        seg = cut(seg, half * count, rows)
        seg_other = send(seg, to_core)
        seg = jnp.stack([jnp.where(core == 0, seg, seg_other), jnp.where(core == 0, seg_other, seg)])
        tokens = seg[:, HALO:]
        lagged = [
            (tokens == seg[:, HALO - k : HALO - k + count]).astype(F32) for k in (1, 2, 3)
        ]
        by_chunk = tokens.reshape(2, chunks, CHUNK)
        last = by_chunk[:, :, -1]
        before = jnp.concatenate([seg[:, HALO - 1 : HALO], last[:, :-1]], axis=1)
        stays = (by_chunk == last[:, :, None]).astype(F32).reshape(2, count)
        enters = (by_chunk == before[:, :, None]).astype(F32).reshape(2, count)
        marks = jnp.stack(lagged + [stays, enters, tokens, tokens, tokens], axis=-1)
        marks = jnp.pad(marks, ((0, 0), (HALO, HALO), (0, 0)))
        seg_row = jnp.broadcast_to(tokens[:, None, :], (2, 8, count))
        links = (last == before).astype(F32)
        links = jnp.broadcast_to(links[:, :, None, None], (2, chunks, 8, LANES))
        links = links.reshape(2, chunks * 8, LANES)

        def exchange(value):
            return [value] + [send(value, to_piece(j)) for j in range(1, half_size)]

        def share(ours):
            return ours + [send(part, to_core) for part in ours]

        def pieces(values):
            return [send(values[j], to_piece(j)) for j in range(1, half_size)]

        mixer = functools.partial
        sizes = dict(inner=inner, half_size=half_size)
        noted = width + LANES
        gains = [jnp.broadcast_to(norm_gain[l][None], (8, width)) for l in range(LAYERS)]

        front_w, rest_w = [None] * LAYERS, [None] * LAYERS
        parts = regroup(jnp.concatenate(front_part(0), axis=1))
        start = to_streams(x_in)
        grads = to_streams(cotangent)
        residual = [[None, None] for _ in range(LAYERS + 1)]
        normed = [None, None]
        kept = [[{}, {}] for _ in range(LAYERS)]
        arrived = [None, None]

        def spread_tokens(s):
            arrived[s] = exchange(normed[s])

        def front(l, s, after=()):
            parts = [at, *share(arrived[s]), *front_w[l]]
            chips = len(front_w[l])
            (toks, raw, head, xb, aux, sloc, tail, edge, ends) = queue.run(
                mixer(front_kernel, chips=chips, **sizes),
                [*parts, marks[s], links[s], conv_w[l], head_p[l], e2],
                [((rows, width), BF), ((rows, wide + LANES), BF), ((HALO, wide), F32),
                 ((count, wide), BF), ((count, 2 * LANES), F32), ((chunks, STATE, inner), BF),
                 ((8, wide), F32), ((HALO, width), BF), ((STATE, inner), BF)],
                [((STATE, inner), F32), ((rows, wide + LANES), F32),
                 ((n_dp * shard, wide + LANES), BF), ((rows, width), BF),
                 ((rows, wide + LANES), BF), ((chips + 2,), None)],
                scalars=1,
                far=range(len(parts) - chips, len(parts)),
                far_out=(0, 1),
                staged=range(len(parts), len(parts) + 5),
                staged_out=(2, 3, 4, 5),
                limit=20,
            )
            tail, edge, ends = queue.gate([tail, edge, ends], after)
            kept[l][s].update(
                toks=toks, raw=raw, head=head, xb=xb, aux=aux, sloc=sloc, ends=ends,
                tail=send(tail, to_later), edge=send(edge, to_later), begins=send(ends, to_later),
            )

        def states(l, s):
            return [kept[l][s][k] for k in ("begins", "tail", "edge")]

        def scan(l, s, after=()):
            v = kept[l][s]
            (xb, z, core_out, act, sst, part) = queue.run(
                mixer(scan_kernel, **sizes),
                [at, v["toks"], v["xb"], rest_w[l], v["aux"], v["sloc"], v["ends"], v["begins"],
                 v["tail"], v["head"], marks[s], seg_row[s], links[s], gate_p[l], conv_w[l], e2],
                [((count, wide), BF), ((count, inner), BF), ((count, inner), F32),
                 ((count, inner), BF), ((chunks + 1, STATE, inner), BF),
                 ((count, noted), F32)],
                [((count, wide), BF), ((count, inner), BF), ((count, inner), F32),
                 ((count, inner), BF), ((chunks + 1, STATE, inner), BF), ((rows, width), BF),
                 ((STATE, inner), F32), ((count, inner), F32), ((n_dp * shard, inner), BF),
                 ((n_dp * shard, inner), BF), ((8,), None)],
                scalars=1,
                after=[v["edge"]],
                far=(1, 3),
                far_out=range(5),
                staged=[2, 4, 5, 9, *range(10, 16)],
                limit=26,
            )
            v.update(xb=xb, z=z, core_out=core_out, act=act, sst=sst)
            send_away(v, part, 0, after)

        def send_away(v, part, offset, after):
            size = part.shape[1]
            away = queue.run(
                mixer(away_kernel, half_size=half_size, offset=offset, noted=offset == 0),
                [at, part], [((half_size * block + offset, size), BF)], scalars=1, after=after,
            )[0]
            v["sum"] = (part, send(away, to_core))

        def add_cores(l, s, has_note, after=()):
            part, came = kept[l][s]["sum"]
            size = part.shape[1]
            sums = queue.run(
                mixer(
                    sum_kernel, half_size=half_size, noted=has_note, offset=0 if has_note else HALO
                ),
                [at, part, came],
                [((block, size), F32)] + [((block, size), BF)] * (half_size - 1)
                + ([] if has_note else [((HALO, size), BF)]),
                scalars=1,
                after=after,
            )
            kept[l][s]["pieces"] = [sums[0]] + pieces(sums)
            if not has_note:
                kept[l][s]["halos"] = [back(sums[-1], to_halo(j)) for j in range(half_size)]

        def own(l, s):
            top = l == LAYERS - 1
            v = kept[l][s]
            mixed, gate, new, msg = queue.run(
                mixer(own_kernel, half_size=half_size, top=top),
                [*v["pieces"], residual[l][s], grads[s] if top else gains[l + 1]],
                [((block, width), F32), ((block, LANES), F32), ((block, width), F32),
                 ((block, noted if top else width), BF)],
                staged=(half_size, half_size + 1),
                staged_out=(0, 1, 2),
            )
            v.update(mixed=mixed, gate=gate)
            residual[l + 1][s] = new
            if top:
                arrived[s] = exchange(msg)
            else:
                normed[s] = msg
                spread_tokens(s)

        for s in range(2):
            residual[0][s], normed[s] = queue.run(
                first_kernel, [start[s], gains[0]], [((block, width), F32), ((block, width), BF)],
                staged_out=(0,),
            )
            spread_tokens(s)
        def sums_of(l, s):
            return kept[l][s]["pieces"][1:]

        pick(parts, 0, True, False)
        parts = regroup(hold(jnp.concatenate(rest_part(0), axis=1), []))
        pick(parts, 0, False, True, [*arrived[0], *arrived[1]])
        queue.touch([marks, seg_row, links, conv_w, gate_p, head_p])
        parts = [
            regroup(hold(jnp.concatenate(front_part(l) + rest_part(l), axis=1), []))
            for l in range(1, LAYERS)
        ]
        front(0, 0)
        front(0, 1, states(0, 0))
        for l in range(1, LAYERS):
            pick(parts[l - 1], l, True, True)
        for l in range(LAYERS):
            if l > 0:
                front(l, 1, states(l, 0))
            scan(l, 0, states(l, 1))
            add_cores(l, 0, True)
            scan(l, 1, sums_of(l, 0))
            own(l, 0)
            add_cores(l, 1, True)
            if l + 1 < LAYERS:
                front(l + 1, 0, sums_of(l, 1))
            own(l, 1)

        def owners(messages):
            return [back(messages[0], to_group(0)), back(messages[1], to_group(1))]

        def split_rest(l, after=()):
            messages = queue.run(
                mixer(split_kernel, terms=1, shard=shard, inner=inner, front=False),
                [at, g_rest[l]],
                [((shard, 2 * inner), BF)] * 2,
                [(g_rest[l].shape, F32)],
                scalars=1,
                after=after,
                staged=(1,),
                limit=14,
            )
            done_rest[l] = owners(messages)

        def split_front(l, values, after=()):
            one, two, keep, away = queue.run(
                mixer(split_kernel, terms=len(values), shard=shard, inner=inner, front=True),
                [at, *values],
                [((shard, inner + LANES), BF)] * 2
                + [((shard, 2 * STATE), F32), ((shard, 2 * STATE), BF)],
                [(values[0].shape, F32)],
                scalars=1,
                after=after,
                limit=14,
            )
            done_front[l] = owners([one, two])
            shared = (keep + send(away, to_core).astype(F32)).astype(BF)
            g_bc[l] = [shared] + [send(shared, route) for route in all_tensor]

        def offloaded_sum(value):
            return lax.psum_scatter(
                value, "dp", scatter_dimension=0, tiled=True, axis_index_groups=planes
            )

        def add(parts, kind):
            return queue.run(
                mixer(add_kernel, terms=len(parts)), parts, [(parts[0].shape, kind)]
            )[0]

        all_tensor = [to_tensor(j) for j in range(1, n_tensor)]
        all_plane = [to_plane(2 * j) for j in range(1, n_dp // 2)]

        def gate_back(l, s, after=(), through=None):
            v = kept[l][s]
            (grows, gcore, gz, ggain, dsin) = queue.run(
                mixer(gate_back_kernel, **sizes),
                [at, *share(arrived[s]), rest_w[l], v["core_out"], v["z"], v["xb"], v["aux"], marks[s],
                 links[s], gate_p[l], e2],
                [((count, width), BF), ((count, inner), BF), ((rows, inner), BF), ((8, inner), F32),
                 ((STATE, inner), BF)],
                [((STATE, inner), F32), ((count, inner), F32), ((count, LANES), F32),
                 ((n_dp * shard, inner), BF), ((count, inner), F32), ((count, inner), BF),
                 ((count, wide), BF), ((count, width), BF), ((5,), None)],
                scalars=1,
                far=range(1 + 2 * half_size, 5 + 2 * half_size),
                far_out=(0,),
                staged_out=(1, 2),
                staged=range(5 + 2 * half_size, 10 + 2 * half_size),
                limit=20,
            )
            moved = [] if through is None else arrived[through][1:]
            dsin, *moved = queue.gate([dsin, *moved], after)
            if through is not None:
                arrived[through] = arrived[through][:1] + moved
            v.update(grows=grows, gcore=gcore, gz=gz, ggain=ggain, dsout=back(dsin, to_later))

        def scan_back(l, s, after=()):
            v = kept[l][s]
            chips = len(front_w[l])
            (graw, sgrad, hgrad, part) = queue.run(
                mixer(scan_back_kernel, chips=chips, **sizes),
                [at, *front_w[l], rest_w[l], v["raw"], v["xb"], v["core_out"], v["sst"],
                 v["gcore"], v["gz"], v["aux"], v["dsout"], v["tail"], marks[s], seg_row[s], links[s],
                 gate_p[l], conv_w[l], head_p[l], e2, hm],
                [((rows, wide + LANES), BF), ((8, wide), F32), ((8, LANES), F32),
                 ((rows, width), F32)],
                [((STATE, inner), F32), ((count + 2 * HALO, wide), F32), ((CHUNK, inner), F32),
                 ((CHUNK, inner), F32), ((rows, wide + LANES), BF),
                 ((n_dp * shard, wide + LANES), BF), ((n_dp * shard, inner), BF),
                 ((count, wide), BF), ((count, inner), F32), ((chunks + 1, STATE, inner), BF),
                 ((chips + 5,), None)],
                scalars=1,
                far=range(1, chips + 6),
                staged=[*range(chips + 6, chips + 9), *range(chips + 10, chips + 19)],
                staged_out=(0,),
                limit=30,
            )
            send_away(v, part, HALO, after)
            v.update(graw=graw, sgrad=sgrad, hgrad=hgrad)

        def own_back(l, s, after=()):
            v = kept[l][s]
            bottom = l == 0
            before = [] if bottom else [kept[l - 1][s]["mixed"], kept[l - 1][s]["gate"]]
            result = queue.run(
                mixer(own_back_kernel, half_size=half_size, bottom=bottom),
                [*v["pieces"], *v["halos"], grads[s], residual[l][s], gains[l], *before],
                [((block, width), F32), ((8, width), F32)]
                + ([] if bottom else [((block, noted), BF)]),
                [((block, width), F32)],
                after=after,
                staged=range(2 * half_size, 2 * half_size + 3 + len(before)),
                staged_out=(0,),
            )
            grads[s], v["gnorm"] = result[:2]
            if not bottom:
                arrived[s] = exchange(result[2])

        def weights_back(l, names, pieces=0, after=()):
            one, two = kept[l]
            operands = []
            for left, right in names:
                operands += [one[left], one[right], two[left], two[right]]
            size = sum(one[right].shape[1] for _, right in names)
            halo = len(names) == 1
            if halo:
                operands += [one["edge"], two["edge"]]
            far = range(4 * len(names))
            count_out = chips if pieces else 1
            scratch = [(operands[i].shape, BF) for i in far] + [((width, size), BF)]
            result = queue.run(
                mixer(
                    weight_kernel, terms=len(names), tokens=count, halo=halo, far=far, pieces=pieces
                ),
                ([at] if pieces else []) + operands,
                [((width // count_out, size), BF)] * count_out,
                scratch + [((len(far) + len(names),), None)],
                scalars=1 if pieces else 0,
                far=[i + 1 for i in far] if pieces else far,
                far_out=() if pieces else (0,),
                staged=[len(operands) - 2 + bool(pieces), len(operands) - 1 + bool(pieces)] if halo else (),
                limit=22,
            )
            if pieces:
                return result
            return queue.pass_on(result[0], after)

        rest_names = (("toks", "gz"), ("grows", "act"))
        front_names = (("toks", "graw"),)
        g_rest, g_front = [None] * LAYERS, [None] * LAYERS
        top = LAYERS - 1
        gate_back(top, 0, through=1)
        gate_back(top, 1, [kept[top][0]["dsout"]])
        g_rest[top] = offloaded_sum(weights_back(top, rest_names))
        done_rest, done_front, g_bc = ([None] * LAYERS for _ in range(3))
        for l in reversed(range(LAYERS)):
            ready = [kept[l][1]["dsout"]]
            if l < top:
                ready.append(done_rest[l + 1][1])
            scan_back(l, 0, ready)
            add_cores(l, 0, False)
            ready = sums_of(l, 0) + kept[l][0]["halos"]
            if l < top:
                split_front(l + 1, [g_front[l + 1]])
                ready += done_front[l + 1]
            scan_back(l, 1, ready)
            own_back(l, 0)
            add_cores(l, 1, False)
            if l == 0:
                direct = direct_start(weights_back(l, front_names, chips))
                split_rest(l)
                own_back(l, 1, [v for k in range(1, LAYERS) for v in g_bc[k]])
                split_front(l, direct, done_rest[0])
            else:
                waiting = sums_of(l, 1) + kept[l][1]["halos"] + arrived[0]
                g_front[l] = offloaded_sum(weights_back(l, front_names, 0, waiting))
                split_rest(l)
                own_back(l, 1)
                gate_back(l - 1, 0, through=1)
                gate_back(l - 1, 1, [kept[l - 1][0]["dsout"]])
                g_rest[l - 1] = offloaded_sum(
                    weights_back(l - 1, rest_names, 0, [done_rest[l][0]])
                )
        grad_in = from_streams(grads)
        output = from_streams(residual[LAYERS])

        names = ("ggain", "sgrad", "hgrad", "gnorm")
        packed = queue.run(
            mixer(pack_kernel, inner=inner, layers=LAYERS),
            [kept[l][s][k] for l in range(LAYERS) for k in names for s in range(2)],
            [((LAYERS, 2 * 8, width), BF)],
        )[0]
        packed = add([back(packed, to_group(0)), back(packed, to_group(1))], F32)
        common = packed[:, 8:].astype(BF)
        common = add([common] + [send(common, route) for route in all_tensor], F32)
        packed = jnp.concatenate([packed[:, :8], common], axis=1)
        low_packed = packed.astype(BF)
        packed = [low_packed] + [send(low_packed, route) for route in all_plane]

        parts = []
        for l in range(LAYERS):
            parts += [*done_rest[l], *done_front[l]]
        smalls = queue.run(
            mixer(
                final_kernel, layers=LAYERS, inner=inner, heads=heads, tensors=n_tensor, chips=chips
            ),
            parts + [v for parts_l in g_bc for v in parts_l] + packed + [hm],
            [(shape, F32) for shape in (
                (LAYERS, shard, inner), (LAYERS, shard, inner), (LAYERS, shard, 2 * STATE),
                (LAYERS, shard, heads), (LAYERS, shard, inner), (LAYERS, 4, inner), (LAYERS, inner),
                (LAYERS, 4, 2 * STATE), (LAYERS, 2 * STATE), (LAYERS, heads), (LAYERS, heads),
                (LAYERS, heads), (LAYERS, inner), (LAYERS, width),
            )],
            limit=20,
        )
        (g_z, g_x, g_shared, g_dt, g_out, g_taps, g_bias, g_taps_bc, g_bias_bc, g_dt_bias, g_log,
         g_skip, g_gate, g_norm) = smalls
        return (
            output, grad_in, g_norm, g_z, g_x, g_shared, g_dt, g_taps, g_bias, g_taps_bc, g_bias_bc,
            g_dt_bias, g_log, g_skip, g_gate, jnp.swapaxes(g_out, 1, 2),
        )

    return local


def solution(mesh):
    n_dp, n_tensor = mesh.shape["dp"], mesh.shape["tensor"]
    tokens = P(("dp", "tensor"), None)
    columns = P(None, "dp", "tensor")
    placed = (
        tokens,
        P("dp"),
        P(),
        columns,
        columns,
        P(None, "dp", None),
        columns,
        P(None, None, "tensor"),
        P(None, "tensor"),
        P(),
        P(),
        P(None, "tensor"),
        P(None, "tensor"),
        P(None, "tensor"),
        P(None, "tensor"),
        P(None, "tensor", "dp"),
        tokens,
    )
    return jax.shard_map(
        build(n_dp, n_tensor),
        mesh=mesh,
        in_specs=placed,
        out_specs=(
            tokens,
            tokens,
            P(),
            columns,
            columns,
            P(None, "dp", None),
            columns,
            P(None, None, "tensor"),
            P(None, "tensor"),
            P(),
            P(),
            P(None, "tensor"),
            P(None, "tensor"),
            P(None, "tensor"),
            P(None, "tensor"),
            P(None, "tensor", "dp"),
        ),
        check_vma=False,
    )
```

```python
import functools

import jax
import jax.numpy as jnp
import numpy as np
from jax import lax
from jax.experimental import pallas as pl
from jax.experimental.pallas import tpu as pltpu
from jax.sharding import PartitionSpec as P

INNER = 3072
HEADDIM = 64
STATE = 128
LAYERS = 2
EPSILON = 1e-05
HALO = 16
CHUNK = 256
LANES = 128

BF = jnp.bfloat16
F32 = jnp.float32
EXACT = lax.Precision.HIGHEST


def dot(left, right, dims=((1,), (0,)), precision=None):
    return lax.dot_general(
        left, right, (dims, ((), ())), preferred_element_type=F32, precision=precision
    )


def split(values):
    high = values.astype(BF)
    return high, (values - high.astype(F32)).astype(BF)


def spread(values, e2_ref):
    return dot(jnp.concatenate(split(values), axis=1), e2_ref[...])


def head_sum(values, hm_ref):
    high, low = split(values)
    return dot(high, hm_ref[...]) + dot(low, hm_ref[...])


def softplus(values):
    return jnp.maximum(values, 0.0) + jnp.log1p(jnp.exp(-jnp.abs(values)))


def triangle(size, lower):
    rows = lax.broadcasted_iota(jnp.int32, (size, size), 0)
    cols = lax.broadcasted_iota(jnp.int32, (size, size), 1)
    return rows >= cols if lower else rows <= cols


def convolve(window, marks, cw, lanes):
    size = window.shape[0] - 8
    total = cw[4:5, lanes] + cw[3:4, lanes] * window[8:]
    for lag in (1, 2, 3):
        earlier = window[8 - lag : 8 - lag + size]
        total = total + cw[3 - lag : 4 - lag, lanes] * (earlier * marks[:, lag - 1 : lag])
    return total


def place(at_ref, j, side, piece, block):
    return pl.multiple_of((at_ref[0] ^ j) * piece + side * block, block)


def fetch_front(at_ref, pieces, w_ref, sems):
    size = pieces[0].shape[0]
    copies = []
    for j, piece in enumerate(pieces):
        row = pl.multiple_of((at_ref[2] ^ j) * size, size) if len(pieces) > 1 else 0
        copies.append(pltpu.make_async_copy(piece, w_ref.at[pl.ds(row, size), :], sems.at[j]))
    for copy in copies:
        copy.start()
    return copies


def start_copy(source, target, sem):
    copy = pltpu.make_async_copy(source, target, sem)
    copy.start()
    return copy


def fetch_rest(rest_ref, low, w_ref, sem):
    copy = pltpu.make_async_copy(rest_ref.at[:, pl.ds(low, w_ref.shape[1])], w_ref, sem)
    copy.start()
    return copy


def front_kernel(*refs, inner, half_size, chips, ready):
    at_ref, refs = refs[0], refs[1:]
    ours, theirs, refs = refs[:half_size], refs[half_size : 2 * half_size], refs[2 * half_size :]
    pieces, refs = refs[:chips], refs[chips:]
    cm_ref, lnk_ref, cw_ref, hp_ref, e2_ref = refs[:5]
    (far_toks_ref, far_raw_ref, head_ref, xb_ref, aux_ref, sloc_ref, tail_ref, edge_ref, send_ref,
     state_ref, raw_ref, w_ref, toks_ref, rawl_ref, sems) = refs[-15:]
    copies = fetch_front(at_ref, pieces, w_ref, sems)
    count = xb_ref.shape[0]
    wide = inner + 2 * STATE
    block = ours[0].shape[0]
    core = at_ref[1]
    toks_ref[:HALO, :] = jnp.zeros((HALO, toks_ref.shape[1]), BF)
    for j in range(half_size):
        for part, side in ((ours[j], core), (theirs[j], 1 - core)):
            row = place(at_ref, j, side, 2 * block, block) + HALO
            toks_ref[pl.ds(pl.multiple_of(row, HALO), block), :] = part[...]
    leaving = [start_copy(toks_ref, far_toks_ref, sems.at[chips])]
    for copy in copies:
        copy.wait()
    for low in range(0, wide + LANES, 2 * LANES):
        lanes = slice(low, min(low + 2 * LANES, wide + LANES))
        raw_ref[:, lanes] = dot(toks_ref[...], w_ref[:, lanes])
        rawl_ref[:, lanes] = raw_ref[:, lanes].astype(BF)
    leaving.append(start_copy(rawl_ref, far_raw_ref, sems.at[chips + 1]))
    head_ref[...] = raw_ref[HALO : 2 * HALO, :wide]
    tail_ref[...] = raw_ref[count + HALO - 8 :, :wide]
    edge_ref[...] = toks_ref[count:, :]
    ready()
    lower = triangle(CHUNK, True).astype(F32)
    state_ref[...] = jnp.zeros_like(state_ref)

    def step_chunk(k, carry):
        base = pl.multiple_of(k * CHUNK, CHUNK)
        here = pl.ds(base, CHUNK)
        marks = cm_ref[pl.ds(base + HALO, CHUNK), :]
        for low in range(0, wide, STATE):
            lanes = slice(low, low + STATE)
            window = raw_ref[pl.ds(base + HALO - 8, CHUNK + 8), lanes]
            pre = convolve(window, marks, cw_ref, lanes)
            xb_ref[here, lanes] = (pre * jax.nn.sigmoid(pre)).astype(BF)
        raw_dt = raw_ref[pl.ds(base + HALO, CHUNK), wide:]
        step = softplus(raw_dt + hp_ref[0:1, :])
        cum = dot(lower, -hp_ref[1:2, :] * step, precision=EXACT)
        aux_ref[here, :LANES] = step
        aux_ref[here, LANES:] = cum
        end = cum[CHUNK - 1 :, :]
        gain = jnp.exp(end - cum) * marks[:, 3:4] * step
        scaled = (spread(gain, e2_ref) * xb_ref[here, :inner].astype(F32)).astype(BF)
        b_rows = xb_ref[here, inner : inner + STATE]
        local = dot(b_rows, scaled, ((0,), (0,)))
        keep = spread(jnp.exp(end) * lnk_ref[pl.ds(k * 8, 8), :], e2_ref)[0:1]
        sloc_ref[k] = state_ref[...].astype(BF)
        state_ref[...] = keep * state_ref[...] + local
        return carry

    lax.fori_loop(0, count // CHUNK, step_chunk, 0)
    send_ref[...] = state_ref[...].astype(BF)
    for copy in leaving:
        copy.wait()


def pair_lanes(values, lane):
    high = values.astype(BF).astype(F32)
    return jnp.where(lane == 0, high, jnp.where(lane == 1, values - high, 0.0)).astype(BF)


def read_pair(tile):
    return tile[:, 0:1].astype(F32) + tile[:, 1:2].astype(F32)


def scan_kernel(*refs, inner, half_size, ready):
    (at_ref, far_toks_ref, old_ref, rest_ref, aux_ref, sloc_ref, send_ref, sin_ref, tail_ref,
     head_ref, cm_ref, segr_ref, lnk_ref, gp_ref, cw_ref, e2_ref) = refs[:16]
    (*far_refs, part_ref, xb_ref, zl_ref, core_ref, act_ref, sst_ref, toks_ref,
     extra_ref, z_ref, wz_ref, wo_ref, sems) = refs[-17:]
    copy_toks = start_copy(far_toks_ref, toks_ref, sems.at[2])
    copy_z = fetch_rest(rest_ref, 0, wz_ref, sems.at[0])
    count = xb_ref.shape[0]
    wide = inner + 2 * STATE
    width = toks_ref.shape[1]
    lower = triangle(CHUNK, True)
    lane = lax.broadcasted_iota(jnp.int32, (CHUNK, STATE), 1)
    first = lane < HEADDIM
    copy_toks.wait()
    copy_z.wait()
    copy_out = fetch_rest(rest_ref, inner, wo_ref, sems.at[1])
    for low in range(0, inner, 2 * LANES):
        lanes = slice(low, min(low + 2 * LANES, inner))
        z_ref[:, lanes] = dot(toks_ref[HALO:, :], wz_ref[:, lanes])
    ready()
    xb_ref[...] = old_ref[...]
    marks = cm_ref[HALO : 2 * HALO, :]
    for low in range(0, wide, STATE):
        lanes = slice(low, low + STATE)
        window = jnp.concatenate([tail_ref[:, lanes], head_ref[:, lanes]], axis=0)
        pre = convolve(window, marks, cw_ref, lanes)
        xb_ref[:HALO, lanes] = (pre * jax.nn.sigmoid(pre)).astype(BF)
    end = aux_ref[CHUNK - 1 : CHUNK, LANES:]
    gain = jnp.exp(end - aux_ref[:HALO, LANES:]) * marks[:, 3:4] * aux_ref[:HALO, :LANES]
    gain = spread(gain, e2_ref)

    def local_state(rows):
        scaled = (gain * rows[:, :inner].astype(F32)).astype(BF)
        return dot(rows[:, inner : inner + STATE], scaled, ((0,), (0,)))

    change = local_state(xb_ref[:HALO, :]) - local_state(old_ref[:HALO, :])
    extra_ref[...] = sin_ref[...].astype(F32)

    def step_chunk(k, carry):
        base = pl.multiple_of(k * CHUNK, CHUNK)
        here = pl.ds(base, CHUNK)
        marks = cm_ref[pl.ds(base + HALO, CHUNK), :]
        incoming = (sloc_ref[k].astype(F32) + extra_ref[...]).astype(BF)
        sst_ref[k] = incoming
        b_rows = xb_ref[here, inner : inner + STATE]
        c_rows = xb_ref[here, inner + STATE : inner + 2 * STATE]
        scores = dot(c_rows, b_rows, ((1,), (1,)))
        allowed = (marks[:, 5:6] == segr_ref[0:1, here]) & lower
        scores = jnp.where(allowed, scores, 0.0)
        step = aux_ref[here, :LANES]
        cum = aux_ref[here, LANES:]
        cum_t = jnp.transpose(cum)
        step_wide = spread(step, e2_ref)
        carried = spread(jnp.exp(cum) * marks[:, 4:5], e2_ref) * dot(c_rows, incoming)
        squares = jnp.zeros((CHUNK, STATE), F32)
        for pair in range(inner // STATE):
            lanes = slice(pair * STATE, (pair + 1) * STATE)
            x_rows = xb_ref[here, lanes].astype(F32)
            scaled = step_wide[:, lanes] * x_rows
            within = carried[:, lanes] + gp_ref[1:2, lanes] * x_rows
            for half in range(2):
                head = 2 * pair + half
                decay = jnp.exp(
                    jnp.minimum(cum[:, head : head + 1] - cum_t[head : head + 1, :], 0.0)
                )
                mine = first if half == 0 else ~first
                part = jnp.where(mine, scaled, 0.0).astype(BF)
                within = within + dot((scores * decay).astype(BF), part)
            core_ref[here, lanes] = within
            z_rows = z_ref[here, lanes]
            zl_ref[here, lanes] = z_rows.astype(BF)
            gated = within * (z_rows * jax.nn.sigmoid(z_rows))
            act_ref[here, lanes] = (gated * gp_ref[0:1, lanes]).astype(BF)
            squares = squares + gated * gated
        part_ref[here, width:] = jnp.where(lane == 0, jnp.sum(squares, axis=1, keepdims=True), 0.0)
        end = cum[CHUNK - 1 :, :]
        keep = spread(jnp.exp(end) * lnk_ref[pl.ds(k * 8, 8), :], e2_ref)[0:1]
        extra_ref[...] = keep * extra_ref[...] + jnp.where(k == 0, change, 0.0)
        return carry

    chunks = count // CHUNK
    lax.fori_loop(0, chunks, step_chunk, 0)
    sst_ref[chunks] = (send_ref[...].astype(F32) + extra_ref[...]).astype(BF)
    here_refs = (xb_ref, zl_ref, core_ref, act_ref, sst_ref)
    leaving = [
        start_copy(near, far, sems.at[3 + i]) for i, (near, far) in enumerate(zip(here_refs, far_refs))
    ]
    copy_out.wait()
    for low in range(0, width, 2 * LANES):
        lanes = slice(low, low + 2 * LANES)
        part_ref[:, lanes] = dot(act_ref[...], wo_ref[lanes, :], ((1,), (1,)))
    for copy in leaving:
        copy.wait()


def sum_kernel(*refs, half_size, offset, noted, ready):
    at_ref, part_ref, came_ref = refs[:3]
    outs = refs[-half_size:] if noted else refs[-half_size - 1 : -1]
    block = outs[0].shape[0]
    width = part_ref.shape[1] - (LANES if noted else 0)
    lane = lax.broadcasted_iota(jnp.int32, (block, LANES), 1)
    for j in range(half_size):
        at = slice(j * block, (j + 1) * block)
        row = place(at_ref, j, at_ref[1], 2 * block, block) + offset
        stay = pl.ds(pl.multiple_of(row, HALO), block)
        total = part_ref[stay, :width] + came_ref[at, :width].astype(F32)
        outs[j][:, :width] = total.astype(outs[j].dtype)
        if noted:
            line = part_ref[stay, width : width + 1] + read_pair(came_ref[at, width:])
            if j == 0:
                outs[j][:, width:] = jnp.where(lane == 0, line, 0.0)
            else:
                outs[j][:, width:] = pair_lanes(line, lane)
    if offset:
        low = half_size * block
        refs[-1][...] = (part_ref[:offset, :] + came_ref[low:, :].astype(F32)).astype(BF)


def normalize(values, gain_ref):
    size = 1.0 / values.shape[1]
    inv_rms = lax.rsqrt(jnp.sum(values * values, axis=1, keepdims=True) * size + EPSILON)
    return values * inv_rms * gain_ref[0:1, :]


def grad_message(msg_ref, grad, mixed, inv_gate):
    width = grad.shape[1]
    scaled = (inv_gate * grad).astype(BF)
    msg_ref[:, :width] = scaled
    weight = jnp.sum(scaled.astype(F32) * mixed, axis=1, keepdims=True)
    lane = lax.broadcasted_iota(jnp.int32, (grad.shape[0], LANES), 1)
    msg_ref[:, width:] = pair_lanes(inv_gate * inv_gate * weight * (1.0 / INNER), lane)


def first_kernel(*refs, ready):
    x_ref, gain_ref = refs[:2]
    res_ref, normed_ref = refs[-2:]
    values = x_ref[...].astype(F32)
    res_ref[...] = values
    normed_ref[...] = normalize(values, gain_ref).astype(BF)


def own_kernel(*refs, half_size, top, ready):
    ready()
    sum_ref, others, refs = refs[0], refs[1:half_size], refs[half_size:]
    res_ref, more_ref = refs[:2]
    mixed_ref, gate_ref, new_ref, msg_ref = refs[-4:]
    width = res_ref.shape[1]
    mixed = sum_ref[:, :width]
    line = sum_ref[:, width : width + 1]
    for other in others:
        mixed = mixed + other[:, :width].astype(F32)
        line = line + read_pair(other[:, width:])
    inv_gate = lax.rsqrt(line * (1.0 / INNER) + EPSILON)
    mixed_ref[...] = mixed
    gate_ref[...] = jnp.broadcast_to(inv_gate, gate_ref.shape)
    values = res_ref[...] + inv_gate * mixed
    new_ref[...] = values
    if top:
        grad_message(msg_ref, more_ref[...], mixed, inv_gate)
    else:
        msg_ref[...] = normalize(values, more_ref).astype(BF)


def own_back_kernel(*refs, half_size, bottom, ready):
    ready()
    sum_ref, others, refs = refs[0], refs[1:half_size], refs[half_size:]
    halos, refs = refs[:half_size], refs[half_size:]
    grad_ref, res_ref, gain_ref = refs[:3]
    if bottom:
        new_ref, gnorm_ref, buf_ref = refs[-3:]
    else:
        mixed_ref, gate_ref = refs[3:5]
        new_ref, gnorm_ref, msg_ref, buf_ref = refs[-4:]
    block = sum_ref.shape[0]
    total = sum_ref[...]
    for other in others:
        total = total + other[...].astype(F32)
    buf_ref[...] = total
    for halo in halos:
        buf_ref[block - HALO :, :] += halo[...].astype(F32)
    total = buf_ref[...]
    values = res_ref[...]
    size = 1.0 / values.shape[1]
    inv_rms = lax.rsqrt(jnp.sum(values * values, axis=1, keepdims=True) * size + EPSILON)
    gnorm = jnp.sum(total * values * inv_rms, axis=0, keepdims=True)
    gnorm_ref[...] = jnp.broadcast_to(gnorm, gnorm_ref.shape)
    scaled = total * gain_ref[0:1, :]
    inner_term = jnp.sum(scaled * values, axis=1, keepdims=True) * size
    grad = grad_ref[...] + inv_rms * scaled - values * (inv_rms * inv_rms * inv_rms) * inner_term
    new_ref[...] = grad
    if not bottom:
        grad_message(msg_ref, grad, mixed_ref[...], gate_ref[:, 0:1])


def gate_back_kernel(*refs, inner, half_size, ready):
    at_ref, refs = refs[0], refs[1:]
    ours, theirs, refs = refs[:half_size], refs[half_size : 2 * half_size], refs[2 * half_size :]
    rest_ref, far_core_ref, far_z_ref, far_xb_ref, aux_ref, cm_ref, lnk_ref, gp_ref, e2_ref = refs[:9]
    (far_grows_ref, gcore_ref, gz_ref, ggain_ref, dsin_ref, state_ref, gg_ref, coef_ref,
     wo_ref, core_ref, z_ref, xb_ref, grows_ref, sems) = refs[-14:]
    copy_out = fetch_rest(rest_ref, inner, wo_ref, sems.at[0])
    count = xb_ref.shape[0]
    chunks = count // CHUNK
    width = grows_ref.shape[1]
    block = ours[0].shape[0]
    core_at = at_ref[1]
    for j in range(half_size):
        for part, side in ((ours[j], core_at), (theirs[j], 1 - core_at)):
            at = pl.ds(place(at_ref, j, side, 2 * block, block), block)
            grows_ref[at, :] = part[:, :width]
            coef_ref[at, :] = jnp.broadcast_to(read_pair(part[:, width:]), (block, LANES))
    leaving = start_copy(grows_ref, far_grows_ref, sems.at[4])
    copies = [
        start_copy(far_core_ref, core_ref, sems.at[1]),
        start_copy(far_z_ref, z_ref, sems.at[2]),
        start_copy(far_xb_ref, xb_ref, sems.at[3]),
    ]
    copy_out.wait()
    for low in range(0, inner, 2 * LANES):
        lanes = slice(low, min(low + 2 * LANES, inner))
        gg_ref[:, lanes] = dot(grows_ref[...], wo_ref[:, lanes])
    for copy in copies:
        copy.wait()
    ready()
    state_ref[...] = jnp.zeros_like(state_ref)
    ggain_ref[...] = jnp.zeros_like(ggain_ref)
    gz_ref[:HALO, :] = jnp.zeros((HALO, inner), BF)

    def step_chunk(turn, carry):
        k = chunks - 1 - turn
        base = pl.multiple_of(k * CHUNK, CHUNK)
        here = pl.ds(base, CHUNK)
        there = pl.ds(pl.multiple_of(base + HALO, HALO), CHUNK)
        marks = cm_ref[there, :]
        coef = coef_ref[here, 0:1]
        cum = aux_ref[here, LANES:]
        entry = spread(jnp.exp(cum) * marks[:, 4:5], e2_ref)
        c_rows = xb_ref[here, inner + STATE : inner + 2 * STATE]
        end = cum[CHUNK - 1 :, :]
        keep = spread(jnp.exp(end) * lnk_ref[pl.ds(k * 8, 8), :], e2_ref)[0:1]
        for pair in range(inner // STATE):
            lanes = slice(pair * STATE, (pair + 1) * STATE)
            z_rows = z_ref[here, lanes].astype(F32)
            core = core_ref[here, lanes]
            grad = gg_ref[here, lanes]
            sig = jax.nn.sigmoid(z_rows)
            act = z_rows * sig
            gated = core * act
            ggain_ref[0:1, lanes] += jnp.sum(grad * gated, axis=0, keepdims=True)
            grad_gated = gp_ref[0:1, lanes] * grad - coef * gated
            gcore = (grad_gated * act).astype(BF)
            gcore_ref[here, lanes] = gcore
            gz_ref[there, lanes] = (
                grad_gated * core * (sig * (1.0 + z_rows * (1.0 - sig)))
            ).astype(BF)
            scaled = (entry[:, lanes] * gcore.astype(F32)).astype(BF)
            state_ref[:, lanes] = keep[:, lanes] * state_ref[:, lanes] + dot(
                c_rows, scaled, ((0,), (0,))
            )
        return carry

    lax.fori_loop(0, chunks, step_chunk, 0)
    dsin_ref[...] = state_ref[...].astype(BF)
    leaving.wait()


def scan_back_kernel(*refs, inner, half_size, chips, ready):
    at_ref, refs = refs[0], refs[1:]
    pieces, refs = refs[:chips], refs[chips:]
    (rest_ref, far_gz_ref, far_raw_ref, far_xb_ref, far_core_ref, far_sst_ref, gcore_ref, aux_ref,
     dso_ref, tail_ref, cm_ref, segr_ref, lnk_ref, gp_ref, cw_ref, hp_ref, e2_ref, hm_ref) = refs[:18]
    (graw_ref, sgrad_ref, hgrad_ref, part_ref, state_ref, dpre_ref, qv_ref, xd_ref,
     raw_ref, wf_ref, wz_ref, xb_ref, core_ref, sst_ref, gz_ref, sems) = refs[-16:]
    first_copies = [
        start_copy(far_xb_ref, xb_ref, sems.at[chips + 2]),
        start_copy(far_sst_ref, sst_ref, sems.at[chips + 3]),
        start_copy(far_core_ref, core_ref, sems.at[chips + 4]),
    ]
    copy_raw = start_copy(far_raw_ref, raw_ref, sems.at[chips])
    count = xb_ref.shape[0]
    chunks = count // CHUNK
    wide = inner + 2 * STATE
    upper = triangle(CHUNK, False)
    first = lax.broadcasted_iota(jnp.int32, (CHUNK, STATE), 1) < HEADDIM
    state_ref[...] = dso_ref[...].astype(F32)
    sgrad_ref[...] = jnp.zeros_like(sgrad_ref)
    hgrad_ref[...] = jnp.zeros_like(hgrad_ref)
    dpre_ref[:HALO, :] = jnp.zeros((HALO, wide), F32)
    dpre_ref[HALO + count :, :] = jnp.zeros((HALO, wide), F32)
    graw_ref[:HALO, wide:] = jnp.zeros((HALO, LANES), BF)

    ready()
    for copy in first_copies:
        copy.wait()
    copy_raw.wait()
    copies = fetch_front(at_ref, pieces, wf_ref, sems)
    copies.append(fetch_rest(rest_ref, 0, wz_ref, sems.at[chips + 1]))
    copies.append(start_copy(far_gz_ref, gz_ref, sems.at[chips + 5]))
    raw_ref[:HALO, :wide] = jnp.concatenate(
        [jnp.zeros((HALO - 8, wide), F32), tail_ref[...]], axis=0
    ).astype(BF)

    def step_chunk(turn, carry):
        k = chunks - 1 - turn
        base = pl.multiple_of(k * CHUNK, CHUNK)
        here = pl.ds(base, CHUNK)
        there = pl.ds(pl.multiple_of(base + HALO, HALO), CHUNK)
        marks = cm_ref[there, :]
        step = aux_ref[here, :LANES]
        cum = aux_ref[here, LANES:]
        cum_t = jnp.transpose(cum)
        end = cum[CHUNK - 1 :, :]
        b_rows = xb_ref[here, inner : inner + STATE]
        c_rows = xb_ref[here, inner + STATE : wide]
        after = state_ref[...]
        after_low = after.astype(BF)
        product = jnp.sum(
            sst_ref[k + 1].astype(F32) * after_low.astype(F32), axis=0, keepdims=True
        )
        at_end = head_sum(jnp.broadcast_to(product, (8, inner)), hm_ref)[0:1]
        scores_t = dot(b_rows, c_rows, ((1,), (1,)))
        allowed = (marks[:, 5:6] == segr_ref[0:1, here]) & upper
        scores_t = jnp.where(allowed, scores_t, 0.0)
        gain = spread(jnp.exp(end - cum) * marks[:, 3:4], e2_ref)
        step_wide = spread(step, e2_ref)
        entry = spread(jnp.exp(cum) * marks[:, 4:5], e2_ref)
        keep = spread(jnp.exp(end) * lnk_ref[pl.ds(k * 8, 8), :], e2_ref)[0:1]
        outer = gain * dot(b_rows, after_low)
        scaled_grad = (entry * gcore_ref[here, :].astype(F32)).astype(BF)
        grad_c = dot(scaled_grad, sst_ref[k], ((1,), (1,)))
        scaled_x = (gain * (step_wide * xb_ref[here, :inner].astype(F32))).astype(BF)
        grad_b = dot(scaled_x, after_low, ((1,), (1,)))
        state_ref[...] = keep * after + dot(c_rows, scaled_grad, ((0,), (0,)))
        grad_scores = jnp.zeros((CHUNK, CHUNK), F32)
        for pair in range(inner // STATE):
            lanes = slice(pair * STATE, (pair + 1) * STATE)
            grad_low = gcore_ref[here, lanes]
            grad = grad_low.astype(F32)
            x_rows = xb_ref[here, lanes].astype(F32)
            wide_step = step_wide[:, lanes]
            scaled = wide_step * x_rows
            grad_u = outer[:, lanes]
            for half in range(2):
                head = 2 * pair + half
                decay = jnp.exp(
                    jnp.minimum(cum_t[head : head + 1, :] - cum[:, head : head + 1], 0.0)
                )
                mine = first if half == 0 else ~first
                part = jnp.where(mine, scaled, 0.0).astype(BF)
                grad_part = jnp.where(mine, grad, 0.0).astype(BF)
                grad_u = grad_u + dot((scores_t * decay).astype(BF), grad_part)
                grad_scores = grad_scores + dot(part, grad_low, ((1,), (1,))) * decay
            skip = gp_ref[1:2, lanes]
            qv_ref[:, lanes] = grad * (core_ref[here, lanes] - skip * x_rows) - (
                scaled.astype(BF).astype(F32) * grad_u
            )
            xd_ref[:, lanes] = x_rows * grad_u
            dpre_ref[there, lanes] = wide_step * grad_u + skip * grad
            sgrad_ref[5:6, lanes] += jnp.sum(grad * x_rows, axis=0, keepdims=True)
        grad_scores = jnp.where(allowed, grad_scores, 0.0).astype(BF)
        dpre_ref[there, inner : inner + STATE] = grad_b + dot(grad_scores, c_rows)
        dpre_ref[there, inner + STATE :] = grad_c + dot(grad_scores, b_rows, ((0,), (0,)))
        rate = hp_ref[1:2, :]
        grad_log = dot(upper.astype(F32), head_sum(qv_ref[...], hm_ref), precision=EXACT) + at_end
        grad_step = head_sum(xd_ref[...], hm_ref) - rate * grad_log
        raw_dt = raw_ref[there, wide:].astype(F32)
        grad_dt = grad_step * jax.nn.sigmoid(raw_dt + hp_ref[0:1, :])
        graw_ref[there, wide:] = grad_dt.astype(BF)
        hgrad_ref[0:1, :] += jnp.sum(grad_dt, axis=0, keepdims=True)
        hgrad_ref[1:2, :] -= rate * jnp.sum(step * grad_log, axis=0, keepdims=True)
        return carry

    lax.fori_loop(0, chunks, step_chunk, 0)

    def conv_chunk(k, carry):
        base = pl.multiple_of(k * CHUNK, CHUNK)
        there = pl.ds(pl.multiple_of(base + HALO, HALO), CHUNK)
        marks = cm_ref[there, :]
        for low in range(0, wide, STATE):
            lanes = slice(low, low + STATE)
            window = raw_ref[pl.ds(base, CHUNK + HALO), lanes].astype(F32)[HALO - 8 :]
            pre = convolve(window, marks, cw_ref, lanes)
            sig = jax.nn.sigmoid(pre)
            grad = dpre_ref[there, lanes] * (sig * (1.0 + pre * (1.0 - sig)))
            dpre_ref[there, lanes] = grad
            sgrad_ref[4:5, lanes] += jnp.sum(grad, axis=0, keepdims=True)
            sgrad_ref[3:4, lanes] += jnp.sum(grad * window[8:], axis=0, keepdims=True)
            for lag in (1, 2, 3):
                earlier = window[8 - lag : 8 - lag + CHUNK]
                sgrad_ref[3 - lag : 4 - lag, lanes] += jnp.sum(
                    grad * (earlier * marks[:, lag - 1 : lag]), axis=0, keepdims=True
                )
        return carry

    lax.fori_loop(0, chunks, conv_chunk, 0)

    def transpose_rows(start, size):
        marks = cm_ref[pl.ds(start, size + 8), :]
        for low in range(0, wide, STATE):
            lanes = slice(low, low + STATE)
            window = dpre_ref[pl.ds(start, size + 8), lanes]
            total = cw_ref[3:4, lanes] * window[:size]
            for lag in (1, 2, 3):
                masked = window[lag : lag + size] * marks[lag : lag + size, lag - 1 : lag]
                total = total + cw_ref[3 - lag : 4 - lag, lanes] * masked
            graw_ref[pl.ds(start, size), lanes] = total.astype(BF)

    transpose_rows(0, HALO)

    def back_chunk(k, carry):
        transpose_rows(pl.multiple_of(k * CHUNK + HALO, HALO), CHUNK)
        return carry

    lax.fori_loop(0, chunks, back_chunk, 0)
    width = part_ref.shape[1]
    for copy in copies:
        copy.wait()
    for low in range(0, width, 2 * LANES):
        lanes = slice(low, low + 2 * LANES)
        part_ref[:, lanes] = dot(gz_ref[...], wz_ref[lanes, :], ((1,), (1,))) + dot(
            graw_ref[...], wf_ref[lanes, :], ((1,), (1,))
        )


def weight_kernel(*refs, terms, tokens, halo, far, pieces, ready):
    refs = list(refs)
    sems = refs.pop()
    at_ref = refs.pop(0) if pieces else None
    out_ref = refs.pop()
    near = refs[-len(far) :]
    outs = refs[len(refs) - len(far) - max(2 * pieces, 1) : len(refs) - len(far)]
    leaving = []
    copies = {}
    sources = {}
    for i, (place_of, target) in enumerate(zip(far, near)):
        sources[place_of] = (refs[place_of], target, sems.at[i])
        refs[place_of] = target
        if i < 4:
            copies[place_of] = start_copy(*sources[place_of])
    ready()
    tile = 2 * LANES
    low = 0
    for term in range(terms):
        left_a, right_a, left_b, right_b = refs[4 * term : 4 * term + 4]
        size = right_a.shape[1]
        for place_of in range(4 * term, 4 * term + 4):
            copies[place_of].wait()
        for place_of in range(4 * term + 4, min(4 * term + 8, len(far))):
            copies[place_of] = start_copy(*sources[place_of])

        def step_tile(r, carry):
            at = pl.ds(pl.multiple_of(r * tile, tile), tile)
            skip_l, skip_r = left_a.shape[0] - tokens, right_a.shape[0] - tokens
            total = dot(left_a[skip_l:, at], right_a[skip_r:, :], ((0,), (0,)))
            total = total + dot(left_b[skip_l:, at], right_b[skip_r:, :], ((0,), (0,)))
            if halo:
                edges = jnp.concatenate([edge[:, at] for edge in refs[4 * terms : 4 * terms + 2]])
                heads = jnp.concatenate([right_a[:HALO, :], right_b[:HALO, :]])
                total = total + dot(edges, heads, ((0,), (0,)))
            out_ref[at, low : low + size] = total.astype(BF)
            return carry

        lax.fori_loop(0, out_ref.shape[0] // tile, step_tile, 0)
        if not pieces:
            lanes = pl.ds(low, size)
            leaving.append(
                start_copy(out_ref.at[:, lanes], outs[0].at[:, lanes], sems.at[len(far) + term])
            )
        low += size
    for copy in leaving:
        copy.wait()
    if pieces:
        for j in range(pieces):
            shared_ref, piece_ref = outs[j], outs[pieces + j]
            size, wide = piece_ref.shape
            row = pl.multiple_of((at_ref[2] ^ j) * size, size)
            rows = pl.ds(row, size)
            inner = wide - LANES
            piece_ref[:, :inner] = out_ref[rows, :inner]
            piece_ref[:, inner:] = out_ref[rows, inner + 2 * STATE :]
            shared_ref[...] = out_ref[rows, inner : inner + 2 * STATE]


def hold_kernel(*refs, ready):
    refs[-1][...] = refs[0][...]


def pick_kernel(*refs, inner, shard, layer, front, rest, ready):
    ready()
    at_ref, one_ref, two_ref = refs[:3]
    outs = refs[-(front + rest) :]
    for side in range(2):
        rows = slice(side * shard, (side + 1) * shard)
        value = jnp.where(at_ref[3] == side, one_ref[...], two_ref[...])
        low = 0
        if front:
            own_ref, other_ref = refs[3:5]
            outs[0][rows, :inner] = value[:, :inner]
            outs[0][rows, inner : inner + 2 * STATE] = jnp.where(
                at_ref[1] == side, own_ref[layer], other_ref[layer]
            )
            outs[0][rows, inner + 2 * STATE :] = value[:, inner : inner + LANES]
            low = inner + LANES
        if rest:
            outs[-1][rows, :] = value[:, low:]


def split_kernel(*refs, terms, shard, inner, front, shared, ready):
    ready()
    at_ref, refs = refs[0], refs[1:]
    buf_ref = refs[-1]
    buf_ref[...] = tree_sum([ref[...] for ref in refs[:terms]])
    half, core = at_ref[3], at_ref[1]
    outs = list(refs[-1 - 2 * (front + shared) : -1])
    if front:
        for out_ref, side in ((outs.pop(0), half), (outs.pop(0), 1 - half)):
            rows = pl.ds(pl.multiple_of(side * shard, HALO), shard)
            if front and shared:
                out_ref[:, :inner] = buf_ref[rows, :inner].astype(BF)
                out_ref[:, inner:] = buf_ref[rows, inner + 2 * STATE :].astype(BF)
            else:
                out_ref[...] = buf_ref[rows, :].astype(BF)
    if shared:
        keep_ref, away_ref = outs
        lanes = slice(inner, inner + 2 * STATE) if front else slice(0, 2 * STATE)
        rows = pl.ds(pl.multiple_of(core * shard, HALO), shard)
        keep_ref[...] = buf_ref[rows, lanes]
        rows = pl.ds(pl.multiple_of((1 - core) * shard, HALO), shard)
        away_ref[...] = buf_ref[rows, lanes].astype(BF)


def final_kernel(*refs, layers, inner, heads, tensors, chips, ready):
    (gz_ref, gx_ref, gbc_ref, gdt_ref, gout_ref, taps_ref, bias_ref, taps_bc_ref, bias_bc_ref,
     dt_ref, log_ref, skip_ref, gate_ref, norm_ref) = refs[-14:]
    low = layers * (4 + tensors)
    small = tree_sum([ref[...] for ref in refs[low : low + chips]])
    hm_ref = refs[low + chips]
    for l in range(layers):
        rest_one, rest_two, front_one, front_two = refs[4 * l : 4 * l + 4]
        total = rest_one[...].astype(F32) + rest_two[...].astype(F32)
        gz_ref[l] = total[:, :inner]
        gout_ref[l] = total[:, inner:]
        total = front_one[...].astype(F32) + front_two[...].astype(F32)
        gx_ref[l] = total[:, :inner]
        gdt_ref[l] = total[:, inner : inner + heads]
        low = 4 * layers + l * tensors
        gbc_ref[l] = tree_sum([ref[...] for ref in refs[low : low + tensors]])
        row = slice(l, l + 1)
        mine = small[l]
        taps_ref[l] = mine[0:4, :inner]
        bias_ref[row, :] = mine[4:5, :inner]
        gate_ref[row, :] = mine[5:6, :inner]
        skips = dot(mine[0:8, :inner], hm_ref[...].astype(F32), precision=EXACT)
        skip_ref[row, :] = skips[6:7, :heads]
        dt_ref[row, :] = mine[7:8, :heads]
        log_ref[row, :] = mine[7:8, LANES : LANES + heads]
        taps_bc_ref[l] = mine[8:12, : 2 * STATE]
        bias_bc_ref[row, :] = mine[12:13, : 2 * STATE]
        norm_ref[row, :] = mine[13:14, :]


def nothing_kernel(*refs):
    pass


def gate_kernel(*refs, terms, ready):
    for source, target in zip(refs[:terms], refs[-terms:]):
        target[...] = source[...]


def away_kernel(*refs, half_size, offset, noted, ready):
    at_ref, part_ref, away_ref = refs[0], refs[1], refs[-1]
    block = (part_ref.shape[0] - offset) // (2 * half_size)
    width = part_ref.shape[1] - (LANES if noted else 0)
    lane = lax.broadcasted_iota(jnp.int32, (block, LANES), 1)
    for j in range(half_size):
        to = slice(j * block, (j + 1) * block)
        row = place(at_ref, j, 1 - at_ref[1], 2 * block, block) + offset
        go = pl.ds(pl.multiple_of(row, HALO), block)
        away_ref[to, :width] = part_ref[go, :width].astype(BF)
        if noted:
            away_ref[to, width:] = pair_lanes(part_ref[go, width : width + 1], lane)
    if offset:
        away_ref[half_size * block :, :] = part_ref[:offset, :].astype(BF)


def touch_kernel(*refs, ready):
    refs[-1][...] = jnp.zeros_like(refs[-1])


def tree_sum(values):
    values = [v.astype(F32) for v in values]
    while len(values) > 1:
        values = [a + b for a, b in zip(values[::2], values[1::2])]
    return values[0]


def add_kernel(*refs, terms, ready):
    refs[-1][...] = tree_sum([ref[...] for ref in refs[:terms]]).astype(refs[-1].dtype)


def pack_kernel(*refs, inner, layers, ready):
    out_ref = refs[-1]
    out_ref[...] = jnp.zeros_like(out_ref)
    for l in range(layers):
        ggain, sgrad, hgrad, gnorm = (
            refs[8 * l + 2 * i][...] + refs[8 * l + 2 * i + 1][...] for i in range(4)
        )
        out_ref[l, 0:5, :inner] = sgrad[0:5, :inner].astype(BF)
        out_ref[l, 5:6, :inner] = ggain[0:1, :].astype(BF)
        out_ref[l, 6:7, :inner] = sgrad[5:6, :inner].astype(BF)
        out_ref[l, 7:8, :LANES] = hgrad[0:1, :].astype(BF)
        out_ref[l, 7:8, LANES : 2 * LANES] = hgrad[1:2, :].astype(BF)
        out_ref[l, 8:13, : 2 * STATE] = sgrad[0:5, inner:].astype(BF)
        out_ref[l, 13:14, :] = gnorm[0:1, :].astype(BF)


class Queue:
    def __init__(self):
        self.last = None

    def run(
        self, kernel, operands, outs, scratch=(), scalars=0, far=(), far_out=(), staged=(),
        staged_out=(), after=(), limit=10,
    ):
        near = pl.BlockSpec(memory_space=pltpu.VMEM)
        distant = pl.BlockSpec(memory_space=pltpu.HBM)
        free = pl.BlockSpec(memory_space=pl.ANY)
        extra = list(after) + ([] if self.last is None else [self.last])
        outside = set(far) | set(staged)
        outside_out = set(far_out) | set(staged_out)
        count, staged, staged_out = len(operands), list(staged), list(staged_out)

        def wrapped(*refs):
            refs = list(refs)
            sems = refs.pop()
            base = count + len(extra)
            buffers = refs[len(refs) - len(staged) - len(staged_out) :]
            refs = refs[: len(refs) - len(buffers)]
            arriving = []
            for i, position in enumerate(staged):
                arriving.append(start_copy(refs[position], buffers[i], sems.at[i]))
                refs[position] = buffers[i]
            leaving = []
            for i, position in enumerate(staged_out, len(staged)):
                leaving.append((buffers[i], refs[base + position], sems.at[i]))
                refs[base + position] = buffers[i]

            def ready():
                for copy in arriving:
                    copy.wait()

            kernel(*refs, ready=ready)
            for copy in [start_copy(*parts) for parts in leaving]:
                copy.wait()

        specs = [pl.BlockSpec(memory_space=pltpu.SMEM)] * scalars
        specs += [distant if i in outside else near for i in range(scalars, count)]
        buffers = [(operands[i].shape, operands[i].dtype) for i in staged]
        buffers += [outs[i] for i in staged_out]
        operands = [
            pltpu.with_memory_space_constraint(v, pltpu.HBM) if i in outside else v
            for i, v in enumerate(operands)
        ]
        result = pl.pallas_call(
            wrapped,
            in_specs=specs + [free] * len(extra),
            out_specs=[distant if i in outside_out else near for i in range(len(outs))],
            out_shape=[
                pltpu.HBM(s, t) if i in outside_out else jax.ShapeDtypeStruct(s, t)
                for i, (s, t) in enumerate(outs)
            ],
            scratch_shapes=[
                pltpu.SemaphoreType.DMA(s) if t is None else pltpu.VMEM(s, t)
                for s, t in [*scratch, *buffers, ((max(len(buffers), 1),), None)]
            ],
            compiler_params=pltpu.CompilerParams(vmem_limit_bytes=limit * 1024 * 1024),
            cost_estimate=pl.CostEstimate(flops=1000, bytes_accessed=1000, transcendentals=0),
        )(*operands, *extra)
        self.last = result[-1]
        return result

    def gate(self, values, after):
        return self.run(
            functools.partial(gate_kernel, terms=len(values)), values,
            [(v.shape, v.dtype) for v in values], after=after,
        )

    def pass_on(self, value, after):
        free = pl.BlockSpec(memory_space=pl.ANY)
        distant = pl.BlockSpec(memory_space=pltpu.HBM)
        extra = list(after) + ([] if self.last is value else [self.last])
        self.last = pl.pallas_call(
            nothing_kernel,
            in_specs=[distant] + [free] * len(extra),
            out_specs=distant,
            out_shape=pltpu.HBM(value.shape, value.dtype),
            input_output_aliases={0: 0},
            cost_estimate=pl.CostEstimate(flops=1000, bytes_accessed=1000, transcendentals=0),
        )(pltpu.with_memory_space_constraint(value, pltpu.HBM), *extra)
        return self.last

    def touch(self, values):
        self.run(touch_kernel, [], [((8, LANES), F32)], after=values)


def build(n_dp, n_tensor):
    axes = ("dp", "tensor")
    half_size = n_tensor // 2
    planes = [[d for d in range(n_dp) if d % 2 == c] for c in range(2)]
    plane_bits = [1 << b for b in range(1, n_dp.bit_length() - 1)]

    def pairs(route):
        found = []
        for d in range(n_dp):
            for t in range(n_tensor):
                goal = route(d, t)
                if goal is not None:
                    found.append((d * n_tensor + t, goal[0] * n_tensor + goal[1]))
        return found

    def send(value, route):
        return lax.ppermute(value, axes, pairs(route))

    def back(value, route):
        return lax.ppermute(value, axes, [(b, a) for a, b in pairs(route)])

    def to_core(d, t):
        return d ^ 1, t

    def to_plane(bits):
        return lambda d, t: (d ^ bits, t)

    def to_tensor(bits):
        return lambda d, t: (d, t ^ bits)

    def to_piece(j):
        return lambda d, t: (d, (t // half_size) * half_size + ((t % half_size) ^ j))

    def to_later(d, t):
        return (d, t + half_size) if t < half_size else None

    def to_halo(j):
        return lambda d, t: (d, half_size + j) if d % 2 == 1 and t == half_size - 1 else None

    def to_group(turn):
        def route(d, t):
            return (d & ~1) | (t % 2), t // 2 + half_size * ((d & 1) ^ turn)

        return route

    def matmul(left, right, dims=((1,), (0,))):
        return lax.dot_general(left, right, (dims, ((), ())), preferred_element_type=F32)

    def local(
        x_in, segments, norm_gain, w_z, w_x, w_bc, w_dt, conv_x, conv_x_bias, conv_bc, conv_bc_bias,
        dt_bias, a_log, d_skip, gate_gain, w_out, cotangent,
    ):
        inner = w_z.shape[2]
        heads = dt_bias.shape[1]
        piece, width = x_in.shape
        block = piece // 2
        count = half_size * piece
        rows = count + HALO
        chunks = count // CHUNK
        shard = w_z.shape[1]
        wide = inner + 2 * STATE
        place = lax.axis_index("tensor")
        dp_place = lax.axis_index("dp")
        core = dp_place % 2
        column = dp_place // 2
        half = place // half_size
        mine = place % half_size

        def cut(value, start, size):
            return lax.dynamic_slice(
                value, (start,) + (0,) * (value.ndim - 1), (size,) + value.shape[1:]
            )

        def put(value, part, start):
            return lax.dynamic_update_slice(value, part, (start,) + (0,) * (value.ndim - 1))

        def to_streams(value):
            keep, away = cut(value, core * block, block), cut(value, (1 - core) * block, block)
            came = send(away, to_core)
            return [jnp.where(core == 0, keep, came), jnp.where(core == 0, came, keep)]

        def from_streams(values):
            keep = jnp.where(core == 0, values[0], values[1])
            came = send(jnp.where(core == 0, values[1], values[0]), to_core)
            out = jnp.zeros((piece, width), F32)
            return put(put(out, keep, core * block), came, (1 - core) * block)

        def pad_lanes(value):
            return jnp.pad(value, ((0, 0), (0, LANES - value.shape[1])))

        queue = Queue()
        at = jnp.stack([mine, core, column, half]).astype(jnp.int32)
        chips = n_dp // 2

        def hold(value, after):
            return queue.run(hold_kernel, [value], [(value.shape, value.dtype)], after=after)[0]

        def regroup(value):
            return [send(value, to_group(0)), send(value, to_group(1))]

        bc_other = send(w_bc, to_core)
        def gather_plane(value):
            return lax.all_gather(value, "dp", axis=0, tiled=True, axis_index_groups=planes)

        def direct_start(values):
            return [values[0]] + [
                send(values[j % len(values)], to_plane(2 * j)) for j in range(1, chips)
            ]

        def pick(parts, l, front, rest, after=(), direct=False):
            outs = []
            if front:
                outs.append(((2 * shard, wide + LANES), BF))
            if rest:
                outs.append(((2 * shard, 2 * inner), BF))
            values = queue.run(
                functools.partial(
                    pick_kernel, inner=inner, shard=shard, layer=l, front=front, rest=rest
                ),
                [at, *parts] + ([w_bc, bc_other] if front else []),
                outs,
                scalars=1,
                after=after,
                staged_out=range(len(outs)),
            )
            if direct:
                front_w[l] = direct_start(values)
                return
            values = [gather_plane(v) for v in values]
            if front:
                front_w[l] = [values[0]]
            if rest:
                rest_w[l] = values[-1]

        def front_part(l):
            return [w_x[l], pad_lanes(w_dt[l])]

        def rest_part(l):
            return [w_z[l], w_out[l].T]

        def row(value, size):
            return jnp.pad(value, ((0, 0), (0, size - value.shape[1])))[:, None]

        head_rows = jnp.concatenate([row(v, LANES) for v in (dt_bias, a_log, d_skip)], axis=2)
        head_rows = jnp.pad(head_rows, ((0, 0), (0, 0), (0, inner - 3 * LANES)))
        packed = jnp.concatenate(
            [conv_x, conv_x_bias[:, None], gate_gain[:, None], head_rows], axis=1
        )
        packed = send(packed, to_group(0))
        taps, bias, gain_own = packed[:, :4], packed[:, 4:5], packed[:, 5:6]
        dt_own, a_own, skip_own = (packed[:, 6, i * LANES : (i + 1) * LANES] for i in range(3))
        head_ok = jnp.arange(LANES) < heads
        rate_own = jnp.where(head_ok, jnp.exp(a_own), 0.0)
        skip_wide = jnp.repeat(skip_own[:, :heads], HEADDIM, axis=1)
        conv_w = jnp.concatenate(
            [
                jnp.concatenate([taps, conv_bc], axis=2),
                jnp.concatenate([bias, conv_bc_bias[:, None]], axis=2),
                jnp.zeros((LAYERS, 3, wide), F32),
            ],
            axis=1,
        )
        gate_p = jnp.concatenate(
            [gain_own, skip_wide[:, None], jnp.zeros((LAYERS, 6, inner), F32)], axis=1
        )
        head_p = jnp.concatenate(
            [dt_own[:, None], rate_own[:, None], jnp.zeros((LAYERS, 6, LANES), F32)], axis=1
        )
        member = np.arange(inner)[None, :] // HEADDIM == np.arange(LANES)[:, None]
        e2 = jnp.asarray(np.concatenate([member, member], axis=0), BF)
        hm = jnp.asarray(member.T, BF)

        seg = jnp.concatenate([jnp.full((HALO,), -1.0, F32), segments.astype(F32)])
        seg = cut(seg, half * count, rows)
        seg_other = send(seg, to_core)
        seg = jnp.stack([jnp.where(core == 0, seg, seg_other), jnp.where(core == 0, seg_other, seg)])
        tokens = seg[:, HALO:]
        lagged = [
            (tokens == seg[:, HALO - k : HALO - k + count]).astype(F32) for k in (1, 2, 3)
        ]
        by_chunk = tokens.reshape(2, chunks, CHUNK)
        last = by_chunk[:, :, -1]
        before = jnp.concatenate([seg[:, HALO - 1 : HALO], last[:, :-1]], axis=1)
        stays = (by_chunk == last[:, :, None]).astype(F32).reshape(2, count)
        enters = (by_chunk == before[:, :, None]).astype(F32).reshape(2, count)
        marks = jnp.stack(lagged + [stays, enters, tokens, tokens, tokens], axis=-1)
        marks = jnp.pad(marks, ((0, 0), (HALO, HALO), (0, 0)))
        seg_row = jnp.broadcast_to(tokens[:, None, :], (2, 8, count))
        links = (last == before).astype(F32)
        links = jnp.broadcast_to(links[:, :, None, None], (2, chunks, 8, LANES))
        links = links.reshape(2, chunks * 8, LANES)

        def exchange(value):
            return [value] + [send(value, to_piece(j)) for j in range(1, half_size)]

        def share(ours):
            return ours + [send(part, to_core) for part in ours]

        def pieces(values):
            return [send(values[j], to_piece(j)) for j in range(1, half_size)]

        mixer = functools.partial
        sizes = dict(inner=inner, half_size=half_size)
        noted = width + LANES
        gains = [jnp.broadcast_to(norm_gain[l][None], (8, width)) for l in range(LAYERS)]

        front_w, rest_w = [None] * LAYERS, [None] * LAYERS
        parts = regroup(jnp.concatenate(front_part(0), axis=1))
        start = to_streams(x_in)
        grads = to_streams(cotangent)
        residual = [[None, None] for _ in range(LAYERS + 1)]
        normed = [None, None]
        kept = [[{}, {}] for _ in range(LAYERS)]
        arrived = [None, None]

        def spread_tokens(s):
            arrived[s] = exchange(normed[s])

        def front(l, s, after=()):
            parts = [at, *share(arrived[s]), *front_w[l]]
            chips = len(front_w[l])
            (toks, raw, head, xb, aux, sloc, tail, edge, ends) = queue.run(
                mixer(front_kernel, chips=chips, **sizes),
                [*parts, marks[s], links[s], conv_w[l], head_p[l], e2],
                [((rows, width), BF), ((rows, wide + LANES), BF), ((HALO, wide), F32),
                 ((count, wide), BF), ((count, 2 * LANES), F32), ((chunks, STATE, inner), BF),
                 ((8, wide), F32), ((HALO, width), BF), ((STATE, inner), BF)],
                [((STATE, inner), F32), ((rows, wide + LANES), F32),
                 ((n_dp * shard, wide + LANES), BF), ((rows, width), BF),
                 ((rows, wide + LANES), BF), ((chips + 2,), None)],
                scalars=1,
                far=range(len(parts) - chips, len(parts)),
                far_out=(0, 1),
                staged=range(len(parts), len(parts) + 5),
                staged_out=(2, 3, 4, 5),
                limit=20,
            )
            tail, edge, ends = queue.gate([tail, edge, ends], after)
            kept[l][s].update(
                toks=toks, raw=raw, head=head, xb=xb, aux=aux, sloc=sloc, ends=ends,
                tail=send(tail, to_later), edge=send(edge, to_later), begins=send(ends, to_later),
            )

        def states(l, s):
            return [kept[l][s][k] for k in ("begins", "tail", "edge")]

        def scan(l, s, after=()):
            v = kept[l][s]
            (xb, z, core_out, act, sst, part) = queue.run(
                mixer(scan_kernel, **sizes),
                [at, v["toks"], v["xb"], rest_w[l], v["aux"], v["sloc"], v["ends"], v["begins"],
                 v["tail"], v["head"], marks[s], seg_row[s], links[s], gate_p[l], conv_w[l], e2],
                [((count, wide), BF), ((count, inner), BF), ((count, inner), F32),
                 ((count, inner), BF), ((chunks + 1, STATE, inner), BF),
                 ((count, noted), F32)],
                [((count, wide), BF), ((count, inner), BF), ((count, inner), F32),
                 ((count, inner), BF), ((chunks + 1, STATE, inner), BF), ((rows, width), BF),
                 ((STATE, inner), F32), ((count, inner), F32), ((n_dp * shard, inner), BF),
                 ((n_dp * shard, inner), BF), ((8,), None)],
                scalars=1,
                after=[v["edge"]],
                far=(1, 3),
                far_out=range(5),
                staged=[2, 4, 5, 9, *range(10, 16)],
                limit=26,
            )
            v.update(xb=xb, z=z, core_out=core_out, act=act, sst=sst)
            send_away(v, part, 0, after)

        def send_away(v, part, offset, after):
            size = part.shape[1]
            away = queue.run(
                mixer(away_kernel, half_size=half_size, offset=offset, noted=offset == 0),
                [at, part], [((half_size * block + offset, size), BF)], scalars=1, after=after,
            )[0]
            v["sum"] = (part, send(away, to_core))

        def add_cores(l, s, has_note, after=()):
            part, came = kept[l][s]["sum"]
            size = part.shape[1]
            sums = queue.run(
                mixer(
                    sum_kernel, half_size=half_size, noted=has_note, offset=0 if has_note else HALO
                ),
                [at, part, came],
                [((block, size), F32)] + [((block, size), BF)] * (half_size - 1)
                + ([] if has_note else [((HALO, size), BF)]),
                scalars=1,
                after=after,
            )
            kept[l][s]["pieces"] = [sums[0]] + pieces(sums)
            if not has_note:
                kept[l][s]["halos"] = [back(sums[-1], to_halo(j)) for j in range(half_size)]

        def own(l, s):
            top = l == LAYERS - 1
            v = kept[l][s]
            mixed, gate, new, msg = queue.run(
                mixer(own_kernel, half_size=half_size, top=top),
                [*v["pieces"], residual[l][s], grads[s] if top else gains[l + 1]],
                [((block, width), F32), ((block, LANES), F32), ((block, width), F32),
                 ((block, noted if top else width), BF)],
                staged=(half_size, half_size + 1),
                staged_out=(0, 1, 2),
            )
            v.update(mixed=mixed, gate=gate)
            residual[l + 1][s] = new
            if top:
                arrived[s] = exchange(msg)
            else:
                normed[s] = msg
                spread_tokens(s)

        for s in range(2):
            residual[0][s], normed[s] = queue.run(
                first_kernel, [start[s], gains[0]], [((block, width), F32), ((block, width), BF)],
                staged_out=(0,),
            )
            spread_tokens(s)
        def sums_of(l, s):
            return kept[l][s]["pieces"][1:]

        pick(parts, 0, True, False)
        parts = regroup(hold(jnp.concatenate(rest_part(0), axis=1), []))
        pick(parts, 0, False, True, [*arrived[0], *arrived[1]])
        queue.touch([marks, seg_row, links, conv_w, gate_p, head_p])
        parts = [
            regroup(hold(jnp.concatenate(front_part(l) + rest_part(l), axis=1), []))
            for l in range(1, LAYERS)
        ]
        front(0, 0)
        front(0, 1, states(0, 0))
        for l in range(1, LAYERS):
            pick(parts[l - 1], l, True, True)
        for l in range(LAYERS):
            if l > 0:
                front(l, 1, states(l, 0))
            scan(l, 0, states(l, 1))
            add_cores(l, 0, True)
            scan(l, 1, sums_of(l, 0))
            own(l, 0)
            add_cores(l, 1, True)
            if l + 1 < LAYERS:
                front(l + 1, 0, sums_of(l, 1))
            own(l, 1)

        def owners(messages):
            return [back(messages[0], to_group(0)), back(messages[1], to_group(1))]

        def split_rest(l, after=()):
            messages = queue.run(
                mixer(split_kernel, terms=1, shard=shard, inner=inner, front=True, shared=False),
                [at, g_rest[l]],
                [((shard, 2 * inner), BF)] * 2,
                [(g_rest[l].shape, F32)],
                scalars=1,
                after=after,
                staged=(1,),
                limit=14,
            )
            done_rest[l] = owners(messages)

        def share_bc(l, keep, away):
            shared = (keep + send(away, to_core).astype(F32)).astype(BF)
            g_bc[l] = [shared] + [send(shared, route) for route in all_tensor]

        def split_front(l, values, front, shared, after=()):
            size = inner + LANES
            outs = [((shard, size), BF)] * 2 if front else []
            outs += [((shard, 2 * STATE), F32), ((shard, 2 * STATE), BF)] if shared else []
            outs = queue.run(
                mixer(
                    split_kernel, terms=len(values), shard=shard, inner=inner, front=front,
                    shared=shared,
                ),
                [at, *values], outs, [(values[0].shape, F32)], scalars=1, after=after, limit=14,
            )
            if front:
                done_front[l] = owners(outs[:2])
            if shared:
                share_bc(l, *outs[-2:])

        def offloaded_sum(value):
            return lax.psum_scatter(
                value, "dp", scatter_dimension=0, tiled=True, axis_index_groups=planes
            )

        def add(parts, kind):
            return queue.run(
                mixer(add_kernel, terms=len(parts)), parts, [(parts[0].shape, kind)]
            )[0]

        all_tensor = [to_tensor(j) for j in range(1, n_tensor)]
        all_plane = [to_plane(2 * j) for j in range(1, n_dp // 2)]

        def gate_back(l, s, after=(), through=None):
            v = kept[l][s]
            (grows, gcore, gz, ggain, dsin) = queue.run(
                mixer(gate_back_kernel, **sizes),
                [at, *share(arrived[s]), rest_w[l], v["core_out"], v["z"], v["xb"], v["aux"], marks[s],
                 links[s], gate_p[l], e2],
                [((count, width), BF), ((count, inner), BF), ((rows, inner), BF), ((8, inner), F32),
                 ((STATE, inner), BF)],
                [((STATE, inner), F32), ((count, inner), F32), ((count, LANES), F32),
                 ((n_dp * shard, inner), BF), ((count, inner), F32), ((count, inner), BF),
                 ((count, wide), BF), ((count, width), BF), ((5,), None)],
                scalars=1,
                far=range(1 + 2 * half_size, 5 + 2 * half_size),
                far_out=(0,),
                staged_out=(1, 2),
                staged=range(5 + 2 * half_size, 10 + 2 * half_size),
                limit=20,
            )
            moved = [] if through is None else arrived[through][1:]
            dsin, *moved = queue.gate([dsin, *moved], after)
            if through is not None:
                arrived[through] = arrived[through][:1] + moved
            v.update(grows=grows, gcore=gcore, gz=gz, ggain=ggain, dsout=back(dsin, to_later))

        def scan_back(l, s, after=()):
            v = kept[l][s]
            chips = len(front_w[l])
            (graw, sgrad, hgrad, part) = queue.run(
                mixer(scan_back_kernel, chips=chips, **sizes),
                [at, *front_w[l], rest_w[l], v["gz"], v["raw"], v["xb"], v["core_out"], v["sst"],
                 v["gcore"], v["aux"], v["dsout"], v["tail"], marks[s], seg_row[s], links[s],
                 gate_p[l], conv_w[l], head_p[l], e2, hm],
                [((rows, wide + LANES), BF), ((8, wide), F32), ((8, LANES), F32),
                 ((rows, width), F32)],
                [((STATE, inner), F32), ((count + 2 * HALO, wide), F32), ((CHUNK, inner), F32),
                 ((CHUNK, inner), F32), ((rows, wide + LANES), BF),
                 ((n_dp * shard, wide + LANES), BF), ((n_dp * shard, inner), BF),
                 ((count, wide), BF), ((count, inner), F32), ((chunks + 1, STATE, inner), BF),
                 ((rows, inner), BF), ((chips + 6,), None)],
                scalars=1,
                far=range(1, chips + 7),
                staged=[chips + 7, chips + 8, *range(chips + 10, chips + 19)],
                staged_out=(0,),
                limit=30,
            )
            send_away(v, part, HALO, after)
            v.update(graw=graw, sgrad=sgrad, hgrad=hgrad)

        def own_back(l, s, after=()):
            v = kept[l][s]
            bottom = l == 0
            before = [] if bottom else [kept[l - 1][s]["mixed"], kept[l - 1][s]["gate"]]
            result = queue.run(
                mixer(own_back_kernel, half_size=half_size, bottom=bottom),
                [*v["pieces"], *v["halos"], grads[s], residual[l][s], gains[l], *before],
                [((block, width), F32), ((8, width), F32)]
                + ([] if bottom else [((block, noted), BF)]),
                [((block, width), F32)],
                after=after,
                staged=range(2 * half_size, 2 * half_size + 3 + len(before)),
                staged_out=(0,),
            )
            grads[s], v["gnorm"] = result[:2]
            if not bottom:
                arrived[s] = exchange(result[2])

        def weights_back(l, names, pieces=0, after=()):
            one, two = kept[l]
            operands = []
            for left, right in names:
                operands += [one[left], one[right], two[left], two[right]]
            size = sum(one[right].shape[1] for _, right in names)
            halo = len(names) == 1
            if halo:
                operands += [one["edge"], two["edge"]]
            far = range(4 * len(names))
            scratch = [(operands[i].shape, BF) for i in far] + [((width, size), BF)]
            result = queue.run(
                mixer(
                    weight_kernel, terms=len(names), tokens=count, halo=halo, far=far, pieces=pieces
                ),
                ([at] if pieces else []) + operands,
                [((width // chips, 2 * STATE), BF)] * pieces
                + [((width // chips, inner + LANES), BF)] * pieces
                if pieces
                else [((width, size), BF)],
                scratch + [((len(far) + len(names),), None)],
                scalars=1 if pieces else 0,
                far=[i + 1 for i in far] if pieces else far,
                far_out=() if pieces else (0,),
                staged=[len(operands) - 2 + bool(pieces), len(operands) - 1 + bool(pieces)] if halo else (),
                limit=22,
            )
            if pieces:
                return result
            return queue.pass_on(result[0], after)

        rest_names = (("toks", "gz"), ("grows", "act"))
        front_names = (("toks", "graw"),)
        g_rest, g_front = [None] * LAYERS, [None] * LAYERS
        top = LAYERS - 1
        gate_back(top, 0, through=1)
        gate_back(top, 1, [kept[top][0]["dsout"]])
        g_rest[top] = offloaded_sum(weights_back(top, rest_names))
        done_rest, done_front, g_bc = ([None] * LAYERS for _ in range(3))
        for l in reversed(range(LAYERS)):
            ready = [kept[l][1]["dsout"]]
            if l < top:
                ready.append(done_rest[l + 1][1])
            scan_back(l, 0, ready)
            add_cores(l, 0, False)
            ready = sums_of(l, 0) + kept[l][0]["halos"]
            if l < top:
                split_front(l + 1, [g_front[l + 1]], True, True)
                ready += done_front[l + 1]
            scan_back(l, 1, ready)
            own_back(l, 0)
            add_cores(l, 1, False)
            if l == 0:
                values = weights_back(l, front_names, chips)
                direct_bc = direct_start(values[:chips])
                direct = direct_start(values[chips:])
                split_rest(l)
                own_back(l, 1, [v for k in range(1, LAYERS) for v in g_bc[k]])
                split_front(l, direct_bc, False, True)
                split_front(l, direct, True, False, done_rest[0])
            else:
                waiting = sums_of(l, 1) + kept[l][1]["halos"] + arrived[0]
                g_front[l] = offloaded_sum(weights_back(l, front_names, 0, waiting))
                split_rest(l)
                own_back(l, 1)
                gate_back(l - 1, 0, through=1)
                gate_back(l - 1, 1, [kept[l - 1][0]["dsout"]])
                g_rest[l - 1] = offloaded_sum(
                    weights_back(l - 1, rest_names, 0, [done_rest[l][0]])
                )
        grad_in = from_streams(grads)
        output = from_streams(residual[LAYERS])

        names = ("ggain", "sgrad", "hgrad", "gnorm")
        packed = queue.run(
            mixer(pack_kernel, inner=inner, layers=LAYERS),
            [kept[l][s][k] for l in range(LAYERS) for k in names for s in range(2)],
            [((LAYERS, 2 * 8, width), BF)],
        )[0]
        packed = add([back(packed, to_group(0)), back(packed, to_group(1))], F32)
        common = packed[:, 8:].astype(BF)
        common = add([common] + [send(common, route) for route in all_tensor], F32)
        packed = jnp.concatenate([packed[:, :8], common], axis=1)
        low_packed = packed.astype(BF)
        packed = [low_packed] + [send(low_packed, route) for route in all_plane]

        parts = []
        for l in range(LAYERS):
            parts += [*done_rest[l], *done_front[l]]
        smalls = queue.run(
            mixer(
                final_kernel, layers=LAYERS, inner=inner, heads=heads, tensors=n_tensor, chips=chips
            ),
            parts + [v for parts_l in g_bc for v in parts_l] + packed + [hm],
            [(shape, F32) for shape in (
                (LAYERS, shard, inner), (LAYERS, shard, inner), (LAYERS, shard, 2 * STATE),
                (LAYERS, shard, heads), (LAYERS, shard, inner), (LAYERS, 4, inner), (LAYERS, inner),
                (LAYERS, 4, 2 * STATE), (LAYERS, 2 * STATE), (LAYERS, heads), (LAYERS, heads),
                (LAYERS, heads), (LAYERS, inner), (LAYERS, width),
            )],
            limit=20,
        )
        (g_z, g_x, g_shared, g_dt, g_out, g_taps, g_bias, g_taps_bc, g_bias_bc, g_dt_bias, g_log,
         g_skip, g_gate, g_norm) = smalls
        return (
            output, grad_in, g_norm, g_z, g_x, g_shared, g_dt, g_taps, g_bias, g_taps_bc, g_bias_bc,
            g_dt_bias, g_log, g_skip, g_gate, jnp.swapaxes(g_out, 1, 2),
        )

    return local


def solution(mesh):
    n_dp, n_tensor = mesh.shape["dp"], mesh.shape["tensor"]
    tokens = P(("dp", "tensor"), None)
    columns = P(None, "dp", "tensor")
    placed = (
        tokens,
        P("dp"),
        P(),
        columns,
        columns,
        P(None, "dp", None),
        columns,
        P(None, None, "tensor"),
        P(None, "tensor"),
        P(),
        P(),
        P(None, "tensor"),
        P(None, "tensor"),
        P(None, "tensor"),
        P(None, "tensor"),
        P(None, "tensor", "dp"),
        tokens,
    )
    return jax.shard_map(
        build(n_dp, n_tensor),
        mesh=mesh,
        in_specs=placed,
        out_specs=(
            tokens,
            tokens,
            P(),
            columns,
            columns,
            P(None, "dp", None),
            columns,
            P(None, None, "tensor"),
            P(None, "tensor"),
            P(),
            P(),
            P(None, "tensor"),
            P(None, "tensor"),
            P(None, "tensor"),
            P(None, "tensor"),
            P(None, "tensor", "dp"),
        ),
        check_vma=False,
    )
```

```python
import functools

import jax
import jax.numpy as jnp
import numpy as np
from jax import lax
from jax.experimental import pallas as pl
from jax.experimental.pallas import tpu as pltpu
from jax.sharding import PartitionSpec as P

INNER = 3072
HEADDIM = 64
STATE = 128
LAYERS = 2
EPSILON = 1e-05
HALO = 16
CHUNK = 256
LANES = 128

BF = jnp.bfloat16
F32 = jnp.float32
EXACT = lax.Precision.HIGHEST


def dot(left, right, dims=((1,), (0,)), precision=None):
    return lax.dot_general(
        left, right, (dims, ((), ())), preferred_element_type=F32, precision=precision
    )


def split(values):
    high = values.astype(BF)
    return high, (values - high.astype(F32)).astype(BF)


def spread(values, e2_ref):
    return dot(jnp.concatenate(split(values), axis=1), e2_ref[...])


def head_sum(values, hm_ref):
    high, low = split(values)
    rest = (values - high.astype(F32) - low.astype(F32)).astype(BF)
    return dot(high, hm_ref[...]) + (dot(low, hm_ref[...]) + dot(rest, hm_ref[...]))


def softplus(values):
    return jnp.maximum(values, 0.0) + jnp.log1p(jnp.exp(-jnp.abs(values)))


def triangle(size, lower):
    rows = lax.broadcasted_iota(jnp.int32, (size, size), 0)
    cols = lax.broadcasted_iota(jnp.int32, (size, size), 1)
    return rows >= cols if lower else rows <= cols


def convolve(window, marks, cw, lanes):
    size = window.shape[0] - 8
    total = cw[4:5, lanes] + cw[3:4, lanes] * window[8:]
    for lag in (1, 2, 3):
        earlier = window[8 - lag : 8 - lag + size]
        total = total + cw[3 - lag : 4 - lag, lanes] * (earlier * marks[:, lag - 1 : lag])
    return total


def place(at_ref, j, side, piece, block):
    return pl.multiple_of((at_ref[0] ^ j) * piece + side * block, block)


def fetch_front(at_ref, pieces, w_ref, sems):
    size = pieces[0].shape[0]
    copies = []
    for j, piece in enumerate(pieces):
        row = pl.multiple_of((at_ref[2] ^ j) * size, size) if len(pieces) > 1 else 0
        copies.append(pltpu.make_async_copy(piece, w_ref.at[pl.ds(row, size), :], sems.at[j]))
    for copy in copies:
        copy.start()
    return copies


def start_copy(source, target, sem):
    copy = pltpu.make_async_copy(source, target, sem)
    copy.start()
    return copy


def fetch_rest(rest_ref, low, w_ref, sem):
    copy = pltpu.make_async_copy(rest_ref.at[:, pl.ds(low, w_ref.shape[1])], w_ref, sem)
    copy.start()
    return copy


def front_kernel(*refs, inner, half_size, chips, ready):
    at_ref, refs = refs[0], refs[1:]
    ours, theirs, refs = refs[:half_size], refs[half_size : 2 * half_size], refs[2 * half_size :]
    pieces, refs = refs[:chips], refs[chips:]
    cm_ref, lnk_ref, cw_ref, hp_ref, e2_ref = refs[:5]
    (far_toks_ref, far_raw_ref, head_ref, xb_ref, aux_ref, sloc_ref, tail_ref, edge_ref, send_ref,
     state_ref, raw_ref, w_ref, toks_ref, rawl_ref, sems) = refs[-15:]
    copies = fetch_front(at_ref, pieces, w_ref, sems)
    count = xb_ref.shape[0]
    wide = inner + 2 * STATE
    block = ours[0].shape[0]
    core = at_ref[1]
    toks_ref[:HALO, :] = jnp.zeros((HALO, toks_ref.shape[1]), BF)
    for j in range(half_size):
        for part, side in ((ours[j], core), (theirs[j], 1 - core)):
            row = place(at_ref, j, side, 2 * block, block) + HALO
            toks_ref[pl.ds(pl.multiple_of(row, HALO), block), :] = part[...]
    leaving = [start_copy(toks_ref, far_toks_ref, sems.at[chips])]
    for copy in copies:
        copy.wait()
    for low in range(0, wide + LANES, 2 * LANES):
        lanes = slice(low, min(low + 2 * LANES, wide + LANES))
        raw_ref[:, lanes] = dot(toks_ref[...], w_ref[:, lanes])
        rawl_ref[:, lanes] = raw_ref[:, lanes].astype(BF)
    leaving.append(start_copy(rawl_ref, far_raw_ref, sems.at[chips + 1]))
    head_ref[...] = raw_ref[HALO : 2 * HALO, :wide]
    tail_ref[...] = raw_ref[count + HALO - 8 :, :wide]
    edge_ref[...] = toks_ref[count:, :]
    ready()
    lower = triangle(CHUNK, True).astype(F32)
    state_ref[...] = jnp.zeros_like(state_ref)

    def step_chunk(k, carry):
        base = pl.multiple_of(k * CHUNK, CHUNK)
        here = pl.ds(base, CHUNK)
        marks = cm_ref[pl.ds(base + HALO, CHUNK), :]
        for low in range(0, wide, STATE):
            lanes = slice(low, low + STATE)
            window = raw_ref[pl.ds(base + HALO - 8, CHUNK + 8), lanes]
            pre = convolve(window, marks, cw_ref, lanes)
            xb_ref[here, lanes] = (pre * jax.nn.sigmoid(pre)).astype(BF)
        raw_dt = raw_ref[pl.ds(base + HALO, CHUNK), wide:]
        step = softplus(raw_dt + hp_ref[0:1, :])
        cum = dot(lower, -hp_ref[1:2, :] * step, precision=EXACT)
        aux_ref[here, :LANES] = step
        aux_ref[here, LANES:] = cum
        end = cum[CHUNK - 1 :, :]
        gain = jnp.exp(end - cum) * marks[:, 3:4] * step
        scaled = (spread(gain, e2_ref) * xb_ref[here, :inner].astype(F32)).astype(BF)
        b_rows = xb_ref[here, inner : inner + STATE]
        local = dot(b_rows, scaled, ((0,), (0,)))
        keep = spread(jnp.exp(end) * lnk_ref[pl.ds(k * 8, 8), :], e2_ref)[0:1]
        sloc_ref[k] = state_ref[...].astype(BF)
        state_ref[...] = keep * state_ref[...] + local
        return carry

    lax.fori_loop(0, count // CHUNK, step_chunk, 0)
    send_ref[...] = state_ref[...].astype(BF)
    for copy in leaving:
        copy.wait()


def pair_lanes(values, lane):
    high = values.astype(BF).astype(F32)
    return jnp.where(lane == 0, high, jnp.where(lane == 1, values - high, 0.0)).astype(BF)


def read_pair(tile):
    return tile[:, 0:1].astype(F32) + tile[:, 1:2].astype(F32)


def scan_kernel(*refs, inner, half_size, ready):
    (at_ref, far_toks_ref, old_ref, rest_ref, aux_ref, sloc_ref, send_ref, sin_ref, tail_ref,
     head_ref, cm_ref, segr_ref, lnk_ref, gp_ref, cw_ref, e2_ref) = refs[:16]
    (*far_refs, part_ref, xb_ref, zl_ref, core_ref, act_ref, sst_ref, toks_ref,
     extra_ref, z_ref, wz_ref, wo_ref, sems) = refs[-17:]
    copy_toks = start_copy(far_toks_ref, toks_ref, sems.at[2])
    copy_z = fetch_rest(rest_ref, 0, wz_ref, sems.at[0])
    count = xb_ref.shape[0]
    wide = inner + 2 * STATE
    width = toks_ref.shape[1]
    lower = triangle(CHUNK, True)
    lane = lax.broadcasted_iota(jnp.int32, (CHUNK, STATE), 1)
    first = lane < HEADDIM
    copy_toks.wait()
    copy_z.wait()
    copy_out = fetch_rest(rest_ref, inner, wo_ref, sems.at[1])
    for low in range(0, inner, 2 * LANES):
        lanes = slice(low, min(low + 2 * LANES, inner))
        z_ref[:, lanes] = dot(toks_ref[HALO:, :], wz_ref[:, lanes])
    ready()
    xb_ref[...] = old_ref[...]
    marks = cm_ref[HALO : 2 * HALO, :]
    for low in range(0, wide, STATE):
        lanes = slice(low, low + STATE)
        window = jnp.concatenate([tail_ref[:, lanes], head_ref[:, lanes]], axis=0)
        pre = convolve(window, marks, cw_ref, lanes)
        xb_ref[:HALO, lanes] = (pre * jax.nn.sigmoid(pre)).astype(BF)
    end = aux_ref[CHUNK - 1 : CHUNK, LANES:]
    gain = jnp.exp(end - aux_ref[:HALO, LANES:]) * marks[:, 3:4] * aux_ref[:HALO, :LANES]
    gain = spread(gain, e2_ref)

    def local_state(rows):
        scaled = (gain * rows[:, :inner].astype(F32)).astype(BF)
        return dot(rows[:, inner : inner + STATE], scaled, ((0,), (0,)))

    change = local_state(xb_ref[:HALO, :]) - local_state(old_ref[:HALO, :])
    extra_ref[...] = sin_ref[...].astype(F32)

    def step_chunk(k, carry):
        base = pl.multiple_of(k * CHUNK, CHUNK)
        here = pl.ds(base, CHUNK)
        marks = cm_ref[pl.ds(base + HALO, CHUNK), :]
        incoming = (sloc_ref[k].astype(F32) + extra_ref[...]).astype(BF)
        sst_ref[k] = incoming
        b_rows = xb_ref[here, inner : inner + STATE]
        c_rows = xb_ref[here, inner + STATE : inner + 2 * STATE]
        scores = dot(c_rows, b_rows, ((1,), (1,)))
        allowed = (marks[:, 5:6] == segr_ref[0:1, here]) & lower
        scores = jnp.where(allowed, scores, 0.0)
        step = aux_ref[here, :LANES]
        cum = aux_ref[here, LANES:]
        cum_t = jnp.transpose(cum)
        step_wide = spread(step, e2_ref)
        carried = spread(jnp.exp(cum) * marks[:, 4:5], e2_ref) * dot(c_rows, incoming)
        squares = jnp.zeros((CHUNK, STATE), F32)
        for pair in range(inner // STATE):
            lanes = slice(pair * STATE, (pair + 1) * STATE)
            x_rows = xb_ref[here, lanes].astype(F32)
            scaled = step_wide[:, lanes] * x_rows
            within = carried[:, lanes] + gp_ref[1:2, lanes] * x_rows
            for half in range(2):
                head = 2 * pair + half
                decay = jnp.exp(
                    jnp.minimum(cum[:, head : head + 1] - cum_t[head : head + 1, :], 0.0)
                )
                mine = first if half == 0 else ~first
                part = jnp.where(mine, scaled, 0.0).astype(BF)
                within = within + dot((scores * decay).astype(BF), part)
            core_ref[here, lanes] = within
            z_rows = z_ref[here, lanes]
            zl_ref[here, lanes] = z_rows.astype(BF)
            gated = within * (z_rows * jax.nn.sigmoid(z_rows))
            act_ref[here, lanes] = (gated * gp_ref[0:1, lanes]).astype(BF)
            squares = squares + gated * gated
        part_ref[here, width:] = jnp.where(lane == 0, jnp.sum(squares, axis=1, keepdims=True), 0.0)
        end = cum[CHUNK - 1 :, :]
        keep = spread(jnp.exp(end) * lnk_ref[pl.ds(k * 8, 8), :], e2_ref)[0:1]
        extra_ref[...] = keep * extra_ref[...] + jnp.where(k == 0, change, 0.0)
        return carry

    chunks = count // CHUNK
    lax.fori_loop(0, chunks, step_chunk, 0)
    sst_ref[chunks] = (send_ref[...].astype(F32) + extra_ref[...]).astype(BF)
    here_refs = (xb_ref, zl_ref, core_ref, act_ref, sst_ref)
    leaving = [
        start_copy(near, far, sems.at[3 + i]) for i, (near, far) in enumerate(zip(here_refs, far_refs))
    ]
    copy_out.wait()
    for low in range(0, width, 2 * LANES):
        lanes = slice(low, low + 2 * LANES)
        part_ref[:, lanes] = dot(act_ref[...], wo_ref[lanes, :], ((1,), (1,)))
    for copy in leaving:
        copy.wait()


def sum_kernel(*refs, half_size, offset, noted, ready):
    at_ref, part_ref, came_ref = refs[:3]
    outs = refs[-half_size:] if noted else refs[-half_size - 1 : -1]
    block = outs[0].shape[0]
    width = part_ref.shape[1] - (LANES if noted else 0)
    lane = lax.broadcasted_iota(jnp.int32, (block, LANES), 1)
    for j in range(half_size):
        at = slice(j * block, (j + 1) * block)
        row = place(at_ref, j, at_ref[1], 2 * block, block) + offset
        stay = pl.ds(pl.multiple_of(row, HALO), block)
        total = part_ref[stay, :width] + came_ref[at, :width].astype(F32)
        outs[j][:, :width] = total.astype(outs[j].dtype)
        if noted:
            line = part_ref[stay, width : width + 1] + read_pair(came_ref[at, width:])
            if j == 0:
                outs[j][:, width:] = jnp.where(lane == 0, line, 0.0)
            else:
                outs[j][:, width:] = pair_lanes(line, lane)
    if offset:
        low = half_size * block
        refs[-1][...] = (part_ref[:offset, :] + came_ref[low:, :].astype(F32)).astype(BF)


def normalize(values, gain_ref):
    size = 1.0 / values.shape[1]
    inv_rms = lax.rsqrt(jnp.sum(values * values, axis=1, keepdims=True) * size + EPSILON)
    return values * inv_rms * gain_ref[0:1, :]


def grad_message(msg_ref, grad, mixed, inv_gate):
    width = grad.shape[1]
    scaled = (inv_gate * grad).astype(BF)
    msg_ref[:, :width] = scaled
    weight = jnp.sum(scaled.astype(F32) * mixed, axis=1, keepdims=True)
    lane = lax.broadcasted_iota(jnp.int32, (grad.shape[0], LANES), 1)
    msg_ref[:, width:] = pair_lanes(inv_gate * inv_gate * weight * (1.0 / INNER), lane)


def first_kernel(*refs, ready):
    x_ref, gain_ref = refs[:2]
    res_ref, normed_ref = refs[-2:]
    values = x_ref[...].astype(F32)
    res_ref[...] = values
    normed_ref[...] = normalize(values, gain_ref).astype(BF)


def own_kernel(*refs, half_size, top, ready):
    ready()
    sum_ref, others, refs = refs[0], refs[1:half_size], refs[half_size:]
    res_ref, more_ref = refs[:2]
    mixed_ref, gate_ref, new_ref, msg_ref = refs[-4:]
    width = res_ref.shape[1]
    mixed = sum_ref[:, :width]
    line = sum_ref[:, width : width + 1]
    for other in others:
        mixed = mixed + other[:, :width].astype(F32)
        line = line + read_pair(other[:, width:])
    inv_gate = lax.rsqrt(line * (1.0 / INNER) + EPSILON)
    mixed_ref[...] = mixed
    gate_ref[...] = jnp.broadcast_to(inv_gate, gate_ref.shape)
    values = res_ref[...] + inv_gate * mixed
    new_ref[...] = values
    if top:
        grad_message(msg_ref, more_ref[...], mixed, inv_gate)
    else:
        msg_ref[...] = normalize(values, more_ref).astype(BF)


def own_back_kernel(*refs, half_size, bottom, ready):
    ready()
    sum_ref, others, refs = refs[0], refs[1:half_size], refs[half_size:]
    halos, refs = refs[:half_size], refs[half_size:]
    grad_ref, res_ref, gain_ref = refs[:3]
    if bottom:
        new_ref, gnorm_ref, buf_ref = refs[-3:]
    else:
        mixed_ref, gate_ref = refs[3:5]
        new_ref, gnorm_ref, msg_ref, buf_ref = refs[-4:]
    block = sum_ref.shape[0]
    total = sum_ref[...]
    for other in others:
        total = total + other[...].astype(F32)
    buf_ref[...] = total
    for halo in halos:
        buf_ref[block - HALO :, :] += halo[...].astype(F32)
    total = buf_ref[...]
    values = res_ref[...]
    size = 1.0 / values.shape[1]
    inv_rms = lax.rsqrt(jnp.sum(values * values, axis=1, keepdims=True) * size + EPSILON)
    gnorm = jnp.sum(total * values * inv_rms, axis=0, keepdims=True)
    gnorm_ref[...] = jnp.broadcast_to(gnorm, gnorm_ref.shape)
    scaled = total * gain_ref[0:1, :]
    inner_term = jnp.sum(scaled * values, axis=1, keepdims=True) * size
    grad = grad_ref[...] + inv_rms * scaled - values * (inv_rms * inv_rms * inv_rms) * inner_term
    new_ref[...] = grad
    if not bottom:
        grad_message(msg_ref, grad, mixed_ref[...], gate_ref[:, 0:1])


def gate_back_kernel(*refs, inner, half_size, ready):
    at_ref, refs = refs[0], refs[1:]
    ours, theirs, refs = refs[:half_size], refs[half_size : 2 * half_size], refs[2 * half_size :]
    rest_ref, far_core_ref, far_z_ref, far_xb_ref, aux_ref, cm_ref, lnk_ref, gp_ref, e2_ref = refs[:9]
    (far_grows_ref, gcore_ref, gz_ref, ggain_ref, dsin_ref, state_ref, gg_ref, coef_ref,
     wo_ref, core_ref, z_ref, xb_ref, grows_ref, sems) = refs[-14:]
    copy_out = fetch_rest(rest_ref, inner, wo_ref, sems.at[0])
    count = xb_ref.shape[0]
    chunks = count // CHUNK
    width = grows_ref.shape[1]
    block = ours[0].shape[0]
    core_at = at_ref[1]
    for j in range(half_size):
        for part, side in ((ours[j], core_at), (theirs[j], 1 - core_at)):
            at = pl.ds(place(at_ref, j, side, 2 * block, block), block)
            grows_ref[at, :] = part[:, :width]
            coef_ref[at, :] = jnp.broadcast_to(read_pair(part[:, width:]), (block, LANES))
    leaving = start_copy(grows_ref, far_grows_ref, sems.at[4])
    copies = [
        start_copy(far_core_ref, core_ref, sems.at[1]),
        start_copy(far_z_ref, z_ref, sems.at[2]),
        start_copy(far_xb_ref, xb_ref, sems.at[3]),
    ]
    copy_out.wait()
    for low in range(0, inner, 2 * LANES):
        lanes = slice(low, min(low + 2 * LANES, inner))
        gg_ref[:, lanes] = dot(grows_ref[...], wo_ref[:, lanes])
    for copy in copies:
        copy.wait()
    ready()
    state_ref[...] = jnp.zeros_like(state_ref)
    ggain_ref[...] = jnp.zeros_like(ggain_ref)
    gz_ref[:HALO, :] = jnp.zeros((HALO, inner), BF)

    def step_chunk(turn, carry):
        k = chunks - 1 - turn
        base = pl.multiple_of(k * CHUNK, CHUNK)
        here = pl.ds(base, CHUNK)
        there = pl.ds(pl.multiple_of(base + HALO, HALO), CHUNK)
        marks = cm_ref[there, :]
        coef = coef_ref[here, 0:1]
        cum = aux_ref[here, LANES:]
        entry = spread(jnp.exp(cum) * marks[:, 4:5], e2_ref)
        c_rows = xb_ref[here, inner + STATE : inner + 2 * STATE]
        end = cum[CHUNK - 1 :, :]
        keep = spread(jnp.exp(end) * lnk_ref[pl.ds(k * 8, 8), :], e2_ref)[0:1]
        for pair in range(inner // STATE):
            lanes = slice(pair * STATE, (pair + 1) * STATE)
            z_rows = z_ref[here, lanes].astype(F32)
            core = core_ref[here, lanes]
            grad = gg_ref[here, lanes]
            sig = jax.nn.sigmoid(z_rows)
            act = z_rows * sig
            gated = core * act
            ggain_ref[0:1, lanes] += jnp.sum(grad * gated, axis=0, keepdims=True)
            grad_gated = gp_ref[0:1, lanes] * grad - coef * gated
            gcore = (grad_gated * act).astype(BF)
            gcore_ref[here, lanes] = gcore
            gz_ref[there, lanes] = (
                grad_gated * core * (sig * (1.0 + z_rows * (1.0 - sig)))
            ).astype(BF)
            scaled = (entry[:, lanes] * gcore.astype(F32)).astype(BF)
            state_ref[:, lanes] = keep[:, lanes] * state_ref[:, lanes] + dot(
                c_rows, scaled, ((0,), (0,))
            )
        return carry

    lax.fori_loop(0, chunks, step_chunk, 0)
    dsin_ref[...] = state_ref[...].astype(BF)
    leaving.wait()


def scan_back_kernel(*refs, inner, half_size, chips, ready):
    at_ref, refs = refs[0], refs[1:]
    pieces, refs = refs[:chips], refs[chips:]
    (rest_ref, far_gz_ref, far_raw_ref, far_xb_ref, far_core_ref, far_sst_ref, gcore_ref, aux_ref,
     dso_ref, tail_ref, cm_ref, segr_ref, lnk_ref, gp_ref, cw_ref, hp_ref, e2_ref, hm_ref) = refs[:18]
    (graw_ref, sgrad_ref, hgrad_ref, part_ref, state_ref, dpre_ref, qv_ref, xd_ref,
     raw_ref, wf_ref, wz_ref, xb_ref, core_ref, sst_ref, gz_ref, sems) = refs[-16:]
    first_copies = [
        start_copy(far_xb_ref, xb_ref, sems.at[chips + 2]),
        start_copy(far_sst_ref, sst_ref, sems.at[chips + 3]),
        start_copy(far_core_ref, core_ref, sems.at[chips + 4]),
    ]
    copy_raw = start_copy(far_raw_ref, raw_ref, sems.at[chips])
    count = xb_ref.shape[0]
    chunks = count // CHUNK
    wide = inner + 2 * STATE
    upper = triangle(CHUNK, False)
    first = lax.broadcasted_iota(jnp.int32, (CHUNK, STATE), 1) < HEADDIM
    state_ref[...] = dso_ref[...].astype(F32)
    sgrad_ref[...] = jnp.zeros_like(sgrad_ref)
    hgrad_ref[...] = jnp.zeros_like(hgrad_ref)
    dpre_ref[:HALO, :] = jnp.zeros((HALO, wide), F32)
    dpre_ref[HALO + count :, :] = jnp.zeros((HALO, wide), F32)
    graw_ref[:HALO, wide:] = jnp.zeros((HALO, LANES), BF)

    ready()
    for copy in first_copies:
        copy.wait()
    copy_raw.wait()
    copies = fetch_front(at_ref, pieces, wf_ref, sems)
    copies.append(fetch_rest(rest_ref, 0, wz_ref, sems.at[chips + 1]))
    copies.append(start_copy(far_gz_ref, gz_ref, sems.at[chips + 5]))
    raw_ref[:HALO, :wide] = jnp.concatenate(
        [jnp.zeros((HALO - 8, wide), F32), tail_ref[...]], axis=0
    ).astype(BF)

    def step_chunk(turn, carry):
        k = chunks - 1 - turn
        base = pl.multiple_of(k * CHUNK, CHUNK)
        here = pl.ds(base, CHUNK)
        there = pl.ds(pl.multiple_of(base + HALO, HALO), CHUNK)
        marks = cm_ref[there, :]
        step = aux_ref[here, :LANES]
        cum = aux_ref[here, LANES:]
        cum_t = jnp.transpose(cum)
        end = cum[CHUNK - 1 :, :]
        b_rows = xb_ref[here, inner : inner + STATE]
        c_rows = xb_ref[here, inner + STATE : wide]
        after = state_ref[...]
        after_low = after.astype(BF)
        product = jnp.sum(
            sst_ref[k + 1].astype(F32) * after_low.astype(F32), axis=0, keepdims=True
        )
        at_end = head_sum(jnp.broadcast_to(product, (8, inner)), hm_ref)[0:1]
        scores_t = dot(b_rows, c_rows, ((1,), (1,)))
        allowed = (marks[:, 5:6] == segr_ref[0:1, here]) & upper
        scores_t = jnp.where(allowed, scores_t, 0.0)
        gain = spread(jnp.exp(end - cum) * marks[:, 3:4], e2_ref)
        step_wide = spread(step, e2_ref)
        entry = spread(jnp.exp(cum) * marks[:, 4:5], e2_ref)
        keep = spread(jnp.exp(end) * lnk_ref[pl.ds(k * 8, 8), :], e2_ref)[0:1]
        outer = gain * dot(b_rows, after_low)
        scaled_grad = (entry * gcore_ref[here, :].astype(F32)).astype(BF)
        grad_c = dot(scaled_grad, sst_ref[k], ((1,), (1,)))
        scaled_x = (gain * (step_wide * xb_ref[here, :inner].astype(F32))).astype(BF)
        grad_b = dot(scaled_x, after_low, ((1,), (1,)))
        state_ref[...] = keep * after + dot(c_rows, scaled_grad, ((0,), (0,)))
        grad_scores = jnp.zeros((CHUNK, CHUNK), F32)
        for pair in range(inner // STATE):
            lanes = slice(pair * STATE, (pair + 1) * STATE)
            grad_low = gcore_ref[here, lanes]
            grad = grad_low.astype(F32)
            x_rows = xb_ref[here, lanes].astype(F32)
            wide_step = step_wide[:, lanes]
            scaled = wide_step * x_rows
            grad_u = outer[:, lanes]
            for half in range(2):
                head = 2 * pair + half
                decay = jnp.exp(
                    jnp.minimum(cum_t[head : head + 1, :] - cum[:, head : head + 1], 0.0)
                )
                mine = first if half == 0 else ~first
                part = jnp.where(mine, scaled, 0.0).astype(BF)
                grad_part = jnp.where(mine, grad, 0.0).astype(BF)
                grad_u = grad_u + dot((scores_t * decay).astype(BF), grad_part)
                grad_scores = grad_scores + dot(part, grad_low, ((1,), (1,))) * decay
            skip = gp_ref[1:2, lanes]
            qv_ref[:, lanes] = grad * (core_ref[here, lanes] - skip * x_rows) - (
                scaled.astype(BF).astype(F32) * grad_u
            )
            xd_ref[:, lanes] = x_rows * grad_u
            dpre_ref[there, lanes] = wide_step * grad_u + skip * grad
            sgrad_ref[5:6, lanes] += jnp.sum(grad * x_rows, axis=0, keepdims=True)
        grad_scores = jnp.where(allowed, grad_scores, 0.0).astype(BF)
        dpre_ref[there, inner : inner + STATE] = grad_b + dot(grad_scores, c_rows)
        dpre_ref[there, inner + STATE :] = grad_c + dot(grad_scores, b_rows, ((0,), (0,)))
        rate = hp_ref[1:2, :]
        grad_log = dot(upper.astype(F32), head_sum(qv_ref[...], hm_ref), precision=EXACT) + at_end
        grad_step = head_sum(xd_ref[...], hm_ref) - rate * grad_log
        raw_dt = raw_ref[there, wide:].astype(F32)
        grad_dt = grad_step * jax.nn.sigmoid(raw_dt + hp_ref[0:1, :])
        graw_ref[there, wide:] = grad_dt.astype(BF)
        hgrad_ref[0:1, :] += jnp.sum(grad_dt, axis=0, keepdims=True)
        hgrad_ref[1:2, :] -= rate * jnp.sum(step * grad_log, axis=0, keepdims=True)
        return carry

    lax.fori_loop(0, chunks, step_chunk, 0)

    def conv_chunk(k, carry):
        base = pl.multiple_of(k * CHUNK, CHUNK)
        there = pl.ds(pl.multiple_of(base + HALO, HALO), CHUNK)
        marks = cm_ref[there, :]
        for low in range(0, wide, STATE):
            lanes = slice(low, low + STATE)
            window = raw_ref[pl.ds(base, CHUNK + HALO), lanes].astype(F32)[HALO - 8 :]
            pre = convolve(window, marks, cw_ref, lanes)
            sig = jax.nn.sigmoid(pre)
            grad = dpre_ref[there, lanes] * (sig * (1.0 + pre * (1.0 - sig)))
            dpre_ref[there, lanes] = grad
            sgrad_ref[4:5, lanes] += jnp.sum(grad, axis=0, keepdims=True)
            sgrad_ref[3:4, lanes] += jnp.sum(grad * window[8:], axis=0, keepdims=True)
            for lag in (1, 2, 3):
                earlier = window[8 - lag : 8 - lag + CHUNK]
                sgrad_ref[3 - lag : 4 - lag, lanes] += jnp.sum(
                    grad * (earlier * marks[:, lag - 1 : lag]), axis=0, keepdims=True
                )
        return carry

    lax.fori_loop(0, chunks, conv_chunk, 0)

    def transpose_rows(start, size):
        marks = cm_ref[pl.ds(start, size + 8), :]
        for low in range(0, wide, STATE):
            lanes = slice(low, low + STATE)
            window = dpre_ref[pl.ds(start, size + 8), lanes]
            total = cw_ref[3:4, lanes] * window[:size]
            for lag in (1, 2, 3):
                masked = window[lag : lag + size] * marks[lag : lag + size, lag - 1 : lag]
                total = total + cw_ref[3 - lag : 4 - lag, lanes] * masked
            graw_ref[pl.ds(start, size), lanes] = total.astype(BF)

    transpose_rows(0, HALO)

    def back_chunk(k, carry):
        transpose_rows(pl.multiple_of(k * CHUNK + HALO, HALO), CHUNK)
        return carry

    lax.fori_loop(0, chunks, back_chunk, 0)
    width = part_ref.shape[1]
    for copy in copies:
        copy.wait()
    for low in range(0, width, 2 * LANES):
        lanes = slice(low, low + 2 * LANES)
        part_ref[:, lanes] = dot(gz_ref[...], wz_ref[lanes, :], ((1,), (1,))) + dot(
            graw_ref[...], wf_ref[lanes, :], ((1,), (1,))
        )


def weight_kernel(*refs, terms, tokens, halo, far, pieces, ready):
    refs = list(refs)
    sems = refs.pop()
    at_ref = refs.pop(0) if pieces else None
    out_ref = refs.pop()
    near = refs[-len(far) :]
    outs = refs[len(refs) - len(far) - max(2 * pieces, 1) : len(refs) - len(far)]
    leaving = []
    copies = {}
    sources = {}
    for i, (place_of, target) in enumerate(zip(far, near)):
        sources[place_of] = (refs[place_of], target, sems.at[i])
        refs[place_of] = target
        if i < 4:
            copies[place_of] = start_copy(*sources[place_of])
    ready()
    tile = 2 * LANES
    low = 0
    for term in range(terms):
        left_a, right_a, left_b, right_b = refs[4 * term : 4 * term + 4]
        size = right_a.shape[1]
        for place_of in range(4 * term, 4 * term + 4):
            copies[place_of].wait()
        for place_of in range(4 * term + 4, min(4 * term + 8, len(far))):
            copies[place_of] = start_copy(*sources[place_of])

        def step_tile(r, carry):
            at = pl.ds(pl.multiple_of(r * tile, tile), tile)
            skip_l, skip_r = left_a.shape[0] - tokens, right_a.shape[0] - tokens
            total = dot(left_a[skip_l:, at], right_a[skip_r:, :], ((0,), (0,)))
            total = total + dot(left_b[skip_l:, at], right_b[skip_r:, :], ((0,), (0,)))
            if halo:
                edges = jnp.concatenate([edge[:, at] for edge in refs[4 * terms : 4 * terms + 2]])
                heads = jnp.concatenate([right_a[:HALO, :], right_b[:HALO, :]])
                total = total + dot(edges, heads, ((0,), (0,)))
            out_ref[at, low : low + size] = total.astype(BF)
            return carry

        lax.fori_loop(0, out_ref.shape[0] // tile, step_tile, 0)
        if not pieces:
            lanes = pl.ds(low, size)
            leaving.append(
                start_copy(out_ref.at[:, lanes], outs[0].at[:, lanes], sems.at[len(far) + term])
            )
        low += size
    for copy in leaving:
        copy.wait()
    if pieces:
        for j in range(pieces):
            shared_ref, piece_ref = outs[j], outs[pieces + j]
            size, wide = piece_ref.shape
            row = pl.multiple_of((at_ref[2] ^ j) * size, size)
            rows = pl.ds(row, size)
            inner = wide - LANES
            piece_ref[:, :inner] = out_ref[rows, :inner]
            piece_ref[:, inner:] = out_ref[rows, inner + 2 * STATE :]
            shared_ref[...] = out_ref[rows, inner : inner + 2 * STATE]


def hold_kernel(*refs, ready):
    refs[-1][...] = refs[0][...]


def pick_kernel(*refs, inner, shard, layer, front, rest, ready):
    ready()
    at_ref, one_ref, two_ref = refs[:3]
    outs = refs[-(front + rest) :]
    for side in range(2):
        rows = slice(side * shard, (side + 1) * shard)
        value = jnp.where(at_ref[3] == side, one_ref[...], two_ref[...])
        low = 0
        if front:
            own_ref, other_ref = refs[3:5]
            outs[0][rows, :inner] = value[:, :inner]
            outs[0][rows, inner : inner + 2 * STATE] = jnp.where(
                at_ref[1] == side, own_ref[layer], other_ref[layer]
            )
            outs[0][rows, inner + 2 * STATE :] = value[:, inner : inner + LANES]
            low = inner + LANES
        if rest:
            outs[-1][rows, :] = value[:, low:]


def split_kernel(*refs, terms, shard, inner, front, shared, ready):
    ready()
    at_ref, refs = refs[0], refs[1:]
    buf_ref = refs[-1]
    buf_ref[...] = tree_sum([ref[...] for ref in refs[:terms]])
    half, core = at_ref[3], at_ref[1]
    outs = list(refs[-1 - 2 * (front + shared) : -1])
    if front:
        for out_ref, side in ((outs.pop(0), half), (outs.pop(0), 1 - half)):
            rows = pl.ds(pl.multiple_of(side * shard, HALO), shard)
            if front and shared:
                out_ref[:, :inner] = buf_ref[rows, :inner].astype(BF)
                out_ref[:, inner:] = buf_ref[rows, inner + 2 * STATE :].astype(BF)
            else:
                out_ref[...] = buf_ref[rows, :].astype(BF)
    if shared:
        keep_ref, away_ref = outs
        lanes = slice(inner, inner + 2 * STATE) if front else slice(0, 2 * STATE)
        rows = pl.ds(pl.multiple_of(core * shard, HALO), shard)
        keep_ref[...] = buf_ref[rows, lanes]
        rows = pl.ds(pl.multiple_of((1 - core) * shard, HALO), shard)
        away_ref[...] = buf_ref[rows, lanes].astype(BF)


def final_kernel(*refs, layers, inner, heads, tensors, chips, ready):
    (gz_ref, gx_ref, gbc_ref, gdt_ref, gout_ref, taps_ref, bias_ref, taps_bc_ref, bias_bc_ref,
     dt_ref, log_ref, skip_ref, gate_ref, norm_ref) = refs[-14:]
    low = layers * (4 + tensors)
    small = tree_sum([ref[...] for ref in refs[low : low + chips]])
    hm_ref = refs[low + chips]
    for l in range(layers):
        rest_one, rest_two, front_one, front_two = refs[4 * l : 4 * l + 4]
        total = rest_one[...].astype(F32) + rest_two[...].astype(F32)
        gz_ref[l] = total[:, :inner]
        gout_ref[l] = total[:, inner:]
        total = front_one[...].astype(F32) + front_two[...].astype(F32)
        gx_ref[l] = total[:, :inner]
        gdt_ref[l] = total[:, inner : inner + heads]
        low = 4 * layers + l * tensors
        gbc_ref[l] = tree_sum([ref[...] for ref in refs[low : low + tensors]])
        row = slice(l, l + 1)
        mine = small[l]
        taps_ref[l] = mine[0:4, :inner]
        bias_ref[row, :] = mine[4:5, :inner]
        gate_ref[row, :] = mine[5:6, :inner]
        skips = dot(mine[0:8, :inner], hm_ref[...].astype(F32), precision=EXACT)
        skip_ref[row, :] = skips[6:7, :heads]
        dt_ref[row, :] = mine[7:8, :heads]
        log_ref[row, :] = mine[7:8, LANES : LANES + heads]
        taps_bc_ref[l] = mine[8:12, : 2 * STATE]
        bias_bc_ref[row, :] = mine[12:13, : 2 * STATE]
        norm_ref[row, :] = mine[13:14, :]


def nothing_kernel(*refs):
    pass


def gate_kernel(*refs, terms, ready):
    for source, target in zip(refs[:terms], refs[-terms:]):
        target[...] = source[...]


def away_kernel(*refs, half_size, offset, noted, ready):
    at_ref, part_ref, away_ref = refs[0], refs[1], refs[-1]
    block = (part_ref.shape[0] - offset) // (2 * half_size)
    width = part_ref.shape[1] - (LANES if noted else 0)
    lane = lax.broadcasted_iota(jnp.int32, (block, LANES), 1)
    for j in range(half_size):
        to = slice(j * block, (j + 1) * block)
        row = place(at_ref, j, 1 - at_ref[1], 2 * block, block) + offset
        go = pl.ds(pl.multiple_of(row, HALO), block)
        away_ref[to, :width] = part_ref[go, :width].astype(BF)
        if noted:
            away_ref[to, width:] = pair_lanes(part_ref[go, width : width + 1], lane)
    if offset:
        away_ref[half_size * block :, :] = part_ref[:offset, :].astype(BF)


def touch_kernel(*refs, ready):
    refs[-1][...] = jnp.zeros_like(refs[-1])


def tree_sum(values):
    values = [v.astype(F32) for v in values]
    while len(values) > 1:
        values = [a + b for a, b in zip(values[::2], values[1::2])]
    return values[0]


def add_kernel(*refs, terms, ready):
    refs[-1][...] = tree_sum([ref[...] for ref in refs[:terms]]).astype(refs[-1].dtype)


def pack_kernel(*refs, inner, layers, ready):
    out_ref = refs[-1]
    out_ref[...] = jnp.zeros_like(out_ref)
    for l in range(layers):
        ggain, sgrad, hgrad, gnorm = (
            refs[8 * l + 2 * i][...] + refs[8 * l + 2 * i + 1][...] for i in range(4)
        )
        out_ref[l, 0:5, :inner] = sgrad[0:5, :inner].astype(BF)
        out_ref[l, 5:6, :inner] = ggain[0:1, :].astype(BF)
        out_ref[l, 6:7, :inner] = sgrad[5:6, :inner].astype(BF)
        out_ref[l, 7:8, :LANES] = hgrad[0:1, :].astype(BF)
        out_ref[l, 7:8, LANES : 2 * LANES] = hgrad[1:2, :].astype(BF)
        out_ref[l, 8:13, : 2 * STATE] = sgrad[0:5, inner:].astype(BF)
        out_ref[l, 13:14, :] = gnorm[0:1, :].astype(BF)


class Queue:
    def __init__(self):
        self.last = None

    def run(
        self, kernel, operands, outs, scratch=(), scalars=0, far=(), far_out=(), staged=(),
        staged_out=(), after=(), limit=10,
    ):
        near = pl.BlockSpec(memory_space=pltpu.VMEM)
        distant = pl.BlockSpec(memory_space=pltpu.HBM)
        free = pl.BlockSpec(memory_space=pl.ANY)
        extra = list(after) + ([] if self.last is None else [self.last])
        outside = set(far) | set(staged)
        outside_out = set(far_out) | set(staged_out)
        count, staged, staged_out = len(operands), list(staged), list(staged_out)

        def wrapped(*refs):
            refs = list(refs)
            sems = refs.pop()
            base = count + len(extra)
            buffers = refs[len(refs) - len(staged) - len(staged_out) :]
            refs = refs[: len(refs) - len(buffers)]
            arriving = []
            for i, position in enumerate(staged):
                arriving.append(start_copy(refs[position], buffers[i], sems.at[i]))
                refs[position] = buffers[i]
            leaving = []
            for i, position in enumerate(staged_out, len(staged)):
                leaving.append((buffers[i], refs[base + position], sems.at[i]))
                refs[base + position] = buffers[i]

            def ready():
                for copy in arriving:
                    copy.wait()

            kernel(*refs, ready=ready)
            for copy in [start_copy(*parts) for parts in leaving]:
                copy.wait()

        specs = [pl.BlockSpec(memory_space=pltpu.SMEM)] * scalars
        specs += [distant if i in outside else near for i in range(scalars, count)]
        buffers = [(operands[i].shape, operands[i].dtype) for i in staged]
        buffers += [outs[i] for i in staged_out]
        operands = [
            pltpu.with_memory_space_constraint(v, pltpu.HBM) if i in outside else v
            for i, v in enumerate(operands)
        ]
        result = pl.pallas_call(
            wrapped,
            in_specs=specs + [free] * len(extra),
            out_specs=[distant if i in outside_out else near for i in range(len(outs))],
            out_shape=[
                pltpu.HBM(s, t) if i in outside_out else jax.ShapeDtypeStruct(s, t)
                for i, (s, t) in enumerate(outs)
            ],
            scratch_shapes=[
                pltpu.SemaphoreType.DMA(s) if t is None else pltpu.VMEM(s, t)
                for s, t in [*scratch, *buffers, ((max(len(buffers), 1),), None)]
            ],
            compiler_params=pltpu.CompilerParams(vmem_limit_bytes=limit * 1024 * 1024),
            cost_estimate=pl.CostEstimate(flops=1000, bytes_accessed=1000, transcendentals=0),
        )(*operands, *extra)
        self.last = result[-1]
        return result

    def gate(self, values, after):
        return self.run(
            functools.partial(gate_kernel, terms=len(values)), values,
            [(v.shape, v.dtype) for v in values], after=after,
        )

    def pass_on(self, value, after):
        free = pl.BlockSpec(memory_space=pl.ANY)
        distant = pl.BlockSpec(memory_space=pltpu.HBM)
        extra = list(after) + ([] if self.last is value else [self.last])
        self.last = pl.pallas_call(
            nothing_kernel,
            in_specs=[distant] + [free] * len(extra),
            out_specs=distant,
            out_shape=pltpu.HBM(value.shape, value.dtype),
            input_output_aliases={0: 0},
            cost_estimate=pl.CostEstimate(flops=1000, bytes_accessed=1000, transcendentals=0),
        )(pltpu.with_memory_space_constraint(value, pltpu.HBM), *extra)
        return self.last

    def touch(self, values):
        self.run(touch_kernel, [], [((8, LANES), F32)], after=values)


def build(n_dp, n_tensor):
    axes = ("dp", "tensor")
    half_size = n_tensor // 2
    planes = [[d for d in range(n_dp) if d % 2 == c] for c in range(2)]
    plane_bits = [1 << b for b in range(1, n_dp.bit_length() - 1)]

    def pairs(route):
        found = []
        for d in range(n_dp):
            for t in range(n_tensor):
                goal = route(d, t)
                if goal is not None:
                    found.append((d * n_tensor + t, goal[0] * n_tensor + goal[1]))
        return found

    def send(value, route):
        return lax.ppermute(value, axes, pairs(route))

    def back(value, route):
        return lax.ppermute(value, axes, [(b, a) for a, b in pairs(route)])

    def to_core(d, t):
        return d ^ 1, t

    def to_plane(bits):
        return lambda d, t: (d ^ bits, t)

    def to_tensor(bits):
        return lambda d, t: (d, t ^ bits)

    def to_piece(j):
        return lambda d, t: (d, (t // half_size) * half_size + ((t % half_size) ^ j))

    def to_later(d, t):
        return (d, t + half_size) if t < half_size else None

    def to_halo(j):
        return lambda d, t: (d, half_size + j) if d % 2 == 1 and t == half_size - 1 else None

    def to_group(turn):
        def route(d, t):
            return (d & ~1) | (t % 2), t // 2 + half_size * ((d & 1) ^ turn)

        return route

    def matmul(left, right, dims=((1,), (0,))):
        return lax.dot_general(left, right, (dims, ((), ())), preferred_element_type=F32)

    def local(
        x_in, segments, norm_gain, w_z, w_x, w_bc, w_dt, conv_x, conv_x_bias, conv_bc, conv_bc_bias,
        dt_bias, a_log, d_skip, gate_gain, w_out, cotangent,
    ):
        inner = w_z.shape[2]
        heads = dt_bias.shape[1]
        piece, width = x_in.shape
        block = piece // 2
        count = half_size * piece
        rows = count + HALO
        chunks = count // CHUNK
        shard = w_z.shape[1]
        wide = inner + 2 * STATE
        place = lax.axis_index("tensor")
        dp_place = lax.axis_index("dp")
        core = dp_place % 2
        column = dp_place // 2
        half = place // half_size
        mine = place % half_size

        def cut(value, start, size):
            return lax.dynamic_slice(
                value, (start,) + (0,) * (value.ndim - 1), (size,) + value.shape[1:]
            )

        def put(value, part, start):
            return lax.dynamic_update_slice(value, part, (start,) + (0,) * (value.ndim - 1))

        def to_streams(value):
            keep, away = cut(value, core * block, block), cut(value, (1 - core) * block, block)
            came = send(away, to_core)
            return [jnp.where(core == 0, keep, came), jnp.where(core == 0, came, keep)]

        def from_streams(values):
            keep = jnp.where(core == 0, values[0], values[1])
            came = send(jnp.where(core == 0, values[1], values[0]), to_core)
            out = jnp.zeros((piece, width), F32)
            return put(put(out, keep, core * block), came, (1 - core) * block)

        def pad_lanes(value):
            return jnp.pad(value, ((0, 0), (0, LANES - value.shape[1])))

        queue = Queue()
        at = jnp.stack([mine, core, column, half]).astype(jnp.int32)
        chips = n_dp // 2

        def hold(value, after):
            return queue.run(hold_kernel, [value], [(value.shape, value.dtype)], after=after)[0]

        def regroup(value):
            return [send(value, to_group(0)), send(value, to_group(1))]

        bc_other = send(w_bc, to_core)
        def gather_plane(value):
            return lax.all_gather(value, "dp", axis=0, tiled=True, axis_index_groups=planes)

        def direct_start(values):
            return [values[0]] + [
                send(values[j % len(values)], to_plane(2 * j)) for j in range(1, chips)
            ]

        def pick(parts, l, front, rest, after=(), direct=False):
            outs = []
            if front:
                outs.append(((2 * shard, wide + LANES), BF))
            if rest:
                outs.append(((2 * shard, 2 * inner), BF))
            values = queue.run(
                functools.partial(
                    pick_kernel, inner=inner, shard=shard, layer=l, front=front, rest=rest
                ),
                [at, *parts] + ([w_bc, bc_other] if front else []),
                outs,
                scalars=1,
                after=after,
                staged_out=range(len(outs)),
            )
            if direct:
                front_w[l] = direct_start(values)
                return
            values = [gather_plane(v) for v in values]
            if front:
                front_w[l] = [values[0]]
            if rest:
                rest_w[l] = values[-1]

        def front_part(l):
            return [w_x[l], pad_lanes(w_dt[l])]

        def rest_part(l):
            return [w_z[l], w_out[l].T]

        def row(value, size):
            return jnp.pad(value, ((0, 0), (0, size - value.shape[1])))[:, None]

        head_rows = jnp.concatenate([row(v, LANES) for v in (dt_bias, a_log, d_skip)], axis=2)
        head_rows = jnp.pad(head_rows, ((0, 0), (0, 0), (0, inner - 3 * LANES)))
        packed = jnp.concatenate(
            [conv_x, conv_x_bias[:, None], gate_gain[:, None], head_rows], axis=1
        )
        packed = send(packed, to_group(0))
        taps, bias, gain_own = packed[:, :4], packed[:, 4:5], packed[:, 5:6]
        dt_own, a_own, skip_own = (packed[:, 6, i * LANES : (i + 1) * LANES] for i in range(3))
        head_ok = jnp.arange(LANES) < heads
        rate_own = jnp.where(head_ok, jnp.exp(a_own), 0.0)
        skip_wide = jnp.repeat(skip_own[:, :heads], HEADDIM, axis=1)
        conv_w = jnp.concatenate(
            [
                jnp.concatenate([taps, conv_bc], axis=2),
                jnp.concatenate([bias, conv_bc_bias[:, None]], axis=2),
                jnp.zeros((LAYERS, 3, wide), F32),
            ],
            axis=1,
        )
        gate_p = jnp.concatenate(
            [gain_own, skip_wide[:, None], jnp.zeros((LAYERS, 6, inner), F32)], axis=1
        )
        head_p = jnp.concatenate(
            [dt_own[:, None], rate_own[:, None], jnp.zeros((LAYERS, 6, LANES), F32)], axis=1
        )
        member = np.arange(inner)[None, :] // HEADDIM == np.arange(LANES)[:, None]
        e2 = jnp.asarray(np.concatenate([member, member], axis=0), BF)
        hm = jnp.asarray(member.T, BF)

        seg = jnp.concatenate([jnp.full((HALO,), -1.0, F32), segments.astype(F32)])
        seg = cut(seg, half * count, rows)
        seg_other = send(seg, to_core)
        seg = jnp.stack([jnp.where(core == 0, seg, seg_other), jnp.where(core == 0, seg_other, seg)])
        tokens = seg[:, HALO:]
        lagged = [
            (tokens == seg[:, HALO - k : HALO - k + count]).astype(F32) for k in (1, 2, 3)
        ]
        by_chunk = tokens.reshape(2, chunks, CHUNK)
        last = by_chunk[:, :, -1]
        before = jnp.concatenate([seg[:, HALO - 1 : HALO], last[:, :-1]], axis=1)
        stays = (by_chunk == last[:, :, None]).astype(F32).reshape(2, count)
        enters = (by_chunk == before[:, :, None]).astype(F32).reshape(2, count)
        marks = jnp.stack(lagged + [stays, enters, tokens, tokens, tokens], axis=-1)
        marks = jnp.pad(marks, ((0, 0), (HALO, HALO), (0, 0)))
        seg_row = jnp.broadcast_to(tokens[:, None, :], (2, 8, count))
        links = (last == before).astype(F32)
        links = jnp.broadcast_to(links[:, :, None, None], (2, chunks, 8, LANES))
        links = links.reshape(2, chunks * 8, LANES)

        def exchange(value):
            return [value] + [send(value, to_piece(j)) for j in range(1, half_size)]

        def share(ours):
            return ours + [send(part, to_core) for part in ours]

        def pieces(values):
            return [send(values[j], to_piece(j)) for j in range(1, half_size)]

        mixer = functools.partial
        sizes = dict(inner=inner, half_size=half_size)
        noted = width + LANES
        gains = [jnp.broadcast_to(norm_gain[l][None], (8, width)) for l in range(LAYERS)]

        front_w, rest_w = [None] * LAYERS, [None] * LAYERS
        parts = regroup(jnp.concatenate(front_part(0), axis=1))
        start = to_streams(x_in)
        grads = to_streams(cotangent)
        residual = [[None, None] for _ in range(LAYERS + 1)]
        normed = [None, None]
        kept = [[{}, {}] for _ in range(LAYERS)]
        arrived = [None, None]

        def spread_tokens(s):
            arrived[s] = exchange(normed[s])

        def front(l, s, after=()):
            parts = [at, *share(arrived[s]), *front_w[l]]
            chips = len(front_w[l])
            (toks, raw, head, xb, aux, sloc, tail, edge, ends) = queue.run(
                mixer(front_kernel, chips=chips, **sizes),
                [*parts, marks[s], links[s], conv_w[l], head_p[l], e2],
                [((rows, width), BF), ((rows, wide + LANES), BF), ((HALO, wide), F32),
                 ((count, wide), BF), ((count, 2 * LANES), F32), ((chunks, STATE, inner), BF),
                 ((8, wide), F32), ((HALO, width), BF), ((STATE, inner), BF)],
                [((STATE, inner), F32), ((rows, wide + LANES), F32),
                 ((n_dp * shard, wide + LANES), BF), ((rows, width), BF),
                 ((rows, wide + LANES), BF), ((chips + 2,), None)],
                scalars=1,
                far=range(len(parts) - chips, len(parts)),
                far_out=(0, 1),
                staged=range(len(parts), len(parts) + 5),
                staged_out=(2, 3, 4, 5),
                limit=20,
            )
            tail, edge, ends = queue.gate([tail, edge, ends], after)
            kept[l][s].update(
                toks=toks, raw=raw, head=head, xb=xb, aux=aux, sloc=sloc, ends=ends,
                tail=send(tail, to_later), edge=send(edge, to_later), begins=send(ends, to_later),
            )

        def states(l, s):
            return [kept[l][s][k] for k in ("begins", "tail", "edge")]

        def scan(l, s, after=()):
            v = kept[l][s]
            (xb, z, core_out, act, sst, part) = queue.run(
                mixer(scan_kernel, **sizes),
                [at, v["toks"], v["xb"], rest_w[l], v["aux"], v["sloc"], v["ends"], v["begins"],
                 v["tail"], v["head"], marks[s], seg_row[s], links[s], gate_p[l], conv_w[l], e2],
                [((count, wide), BF), ((count, inner), BF), ((count, inner), F32),
                 ((count, inner), BF), ((chunks + 1, STATE, inner), BF),
                 ((count, noted), F32)],
                [((count, wide), BF), ((count, inner), BF), ((count, inner), F32),
                 ((count, inner), BF), ((chunks + 1, STATE, inner), BF), ((rows, width), BF),
                 ((STATE, inner), F32), ((count, inner), F32), ((n_dp * shard, inner), BF),
                 ((n_dp * shard, inner), BF), ((8,), None)],
                scalars=1,
                after=[v["edge"]],
                far=(1, 3),
                far_out=range(5),
                staged=[2, 4, 5, 9, *range(10, 16)],
                limit=26,
            )
            v.update(xb=xb, z=z, core_out=core_out, act=act, sst=sst)
            send_away(v, part, 0, after)

        def send_away(v, part, offset, after):
            size = part.shape[1]
            away = queue.run(
                mixer(away_kernel, half_size=half_size, offset=offset, noted=offset == 0),
                [at, part], [((half_size * block + offset, size), BF)], scalars=1, after=after,
            )[0]
            v["sum"] = (part, send(away, to_core))

        def add_cores(l, s, has_note, after=()):
            part, came = kept[l][s]["sum"]
            size = part.shape[1]
            sums = queue.run(
                mixer(
                    sum_kernel, half_size=half_size, noted=has_note, offset=0 if has_note else HALO
                ),
                [at, part, came],
                [((block, size), F32)] + [((block, size), BF)] * (half_size - 1)
                + ([] if has_note else [((HALO, size), BF)]),
                scalars=1,
                after=after,
            )
            kept[l][s]["pieces"] = [sums[0]] + pieces(sums)
            if not has_note:
                kept[l][s]["halos"] = [back(sums[-1], to_halo(j)) for j in range(half_size)]

        def own(l, s):
            top = l == LAYERS - 1
            v = kept[l][s]
            mixed, gate, new, msg = queue.run(
                mixer(own_kernel, half_size=half_size, top=top),
                [*v["pieces"], residual[l][s], grads[s] if top else gains[l + 1]],
                [((block, width), F32), ((block, LANES), F32), ((block, width), F32),
                 ((block, noted if top else width), BF)],
                staged=(half_size, half_size + 1),
                staged_out=(0, 1, 2),
            )
            v.update(mixed=mixed, gate=gate)
            residual[l + 1][s] = new
            if top:
                arrived[s] = exchange(msg)
            else:
                normed[s] = msg
                spread_tokens(s)

        for s in range(2):
            residual[0][s], normed[s] = queue.run(
                first_kernel, [start[s], gains[0]], [((block, width), F32), ((block, width), BF)],
                staged_out=(0,),
            )
            spread_tokens(s)
        def sums_of(l, s):
            return kept[l][s]["pieces"][1:]

        pick(parts, 0, True, False)
        parts = regroup(hold(jnp.concatenate(rest_part(0), axis=1), []))
        pick(parts, 0, False, True, [*arrived[0], *arrived[1]])
        queue.touch([marks, seg_row, links, conv_w, gate_p, head_p])
        parts = [
            regroup(hold(jnp.concatenate(front_part(l) + rest_part(l), axis=1), []))
            for l in range(1, LAYERS)
        ]
        front(0, 0)
        front(0, 1, states(0, 0))
        for l in range(1, LAYERS):
            pick(parts[l - 1], l, True, True)
        for l in range(LAYERS):
            if l > 0:
                front(l, 1, states(l, 0))
            scan(l, 0, states(l, 1))
            add_cores(l, 0, True)
            scan(l, 1, sums_of(l, 0))
            own(l, 0)
            add_cores(l, 1, True)
            if l + 1 < LAYERS:
                front(l + 1, 0, sums_of(l, 1))
            own(l, 1)

        def owners(messages):
            return [back(messages[0], to_group(0)), back(messages[1], to_group(1))]

        def split_rest(l, after=()):
            messages = queue.run(
                mixer(split_kernel, terms=1, shard=shard, inner=inner, front=True, shared=False),
                [at, g_rest[l]],
                [((shard, 2 * inner), BF)] * 2,
                [(g_rest[l].shape, F32)],
                scalars=1,
                after=after,
                staged=(1,),
                limit=14,
            )
            done_rest[l] = owners(messages)

        def share_bc(l, keep, away):
            shared = (keep + send(away, to_core).astype(F32)).astype(BF)
            g_bc[l] = [shared] + [send(shared, route) for route in all_tensor]

        def split_front(l, values, front, shared, after=()):
            size = inner + LANES
            outs = [((shard, size), BF)] * 2 if front else []
            outs += [((shard, 2 * STATE), F32), ((shard, 2 * STATE), BF)] if shared else []
            outs = queue.run(
                mixer(
                    split_kernel, terms=len(values), shard=shard, inner=inner, front=front,
                    shared=shared,
                ),
                [at, *values], outs, [(values[0].shape, F32)], scalars=1, after=after, limit=14,
            )
            if front:
                done_front[l] = owners(outs[:2])
            if shared:
                share_bc(l, *outs[-2:])

        def offloaded_sum(value):
            return lax.psum_scatter(
                value, "dp", scatter_dimension=0, tiled=True, axis_index_groups=planes
            )

        def add(parts, kind):
            return queue.run(
                mixer(add_kernel, terms=len(parts)), parts, [(parts[0].shape, kind)]
            )[0]

        all_tensor = [to_tensor(j) for j in range(1, n_tensor)]
        all_plane = [to_plane(2 * j) for j in range(1, n_dp // 2)]

        def gate_back(l, s, after=(), through=None):
            v = kept[l][s]
            (grows, gcore, gz, ggain, dsin) = queue.run(
                mixer(gate_back_kernel, **sizes),
                [at, *share(arrived[s]), rest_w[l], v["core_out"], v["z"], v["xb"], v["aux"], marks[s],
                 links[s], gate_p[l], e2],
                [((count, width), BF), ((count, inner), BF), ((rows, inner), BF), ((8, inner), F32),
                 ((STATE, inner), BF)],
                [((STATE, inner), F32), ((count, inner), F32), ((count, LANES), F32),
                 ((n_dp * shard, inner), BF), ((count, inner), F32), ((count, inner), BF),
                 ((count, wide), BF), ((count, width), BF), ((5,), None)],
                scalars=1,
                far=range(1 + 2 * half_size, 5 + 2 * half_size),
                far_out=(0,),
                staged_out=(1, 2),
                staged=range(5 + 2 * half_size, 10 + 2 * half_size),
                limit=20,
            )
            moved = [] if through is None else arrived[through][1:]
            dsin, *moved = queue.gate([dsin, *moved], after)
            if through is not None:
                arrived[through] = arrived[through][:1] + moved
            v.update(grows=grows, gcore=gcore, gz=gz, ggain=ggain, dsout=back(dsin, to_later))

        def scan_back(l, s, after=()):
            v = kept[l][s]
            chips = len(front_w[l])
            (graw, sgrad, hgrad, part) = queue.run(
                mixer(scan_back_kernel, chips=chips, **sizes),
                [at, *front_w[l], rest_w[l], v["gz"], v["raw"], v["xb"], v["core_out"], v["sst"],
                 v["gcore"], v["aux"], v["dsout"], v["tail"], marks[s], seg_row[s], links[s],
                 gate_p[l], conv_w[l], head_p[l], e2, hm],
                [((rows, wide + LANES), BF), ((8, wide), F32), ((8, LANES), F32),
                 ((rows, width), F32)],
                [((STATE, inner), F32), ((count + 2 * HALO, wide), F32), ((CHUNK, inner), F32),
                 ((CHUNK, inner), F32), ((rows, wide + LANES), BF),
                 ((n_dp * shard, wide + LANES), BF), ((n_dp * shard, inner), BF),
                 ((count, wide), BF), ((count, inner), F32), ((chunks + 1, STATE, inner), BF),
                 ((rows, inner), BF), ((chips + 6,), None)],
                scalars=1,
                far=range(1, chips + 7),
                staged=[chips + 7, chips + 8, *range(chips + 10, chips + 19)],
                staged_out=(0,),
                limit=30,
            )
            send_away(v, part, HALO, after)
            v.update(graw=graw, sgrad=sgrad, hgrad=hgrad)

        def own_back(l, s, after=()):
            v = kept[l][s]
            bottom = l == 0
            before = [] if bottom else [kept[l - 1][s]["mixed"], kept[l - 1][s]["gate"]]
            result = queue.run(
                mixer(own_back_kernel, half_size=half_size, bottom=bottom),
                [*v["pieces"], *v["halos"], grads[s], residual[l][s], gains[l], *before],
                [((block, width), F32), ((8, width), F32)]
                + ([] if bottom else [((block, noted), BF)]),
                [((block, width), F32)],
                after=after,
                staged=range(2 * half_size, 2 * half_size + 3 + len(before)),
                staged_out=(0,),
            )
            grads[s], v["gnorm"] = result[:2]
            if not bottom:
                arrived[s] = exchange(result[2])

        def weights_back(l, names, pieces=0, after=()):
            one, two = kept[l]
            operands = []
            for left, right in names:
                operands += [one[left], one[right], two[left], two[right]]
            size = sum(one[right].shape[1] for _, right in names)
            halo = len(names) == 1
            if halo:
                operands += [one["edge"], two["edge"]]
            far = range(4 * len(names))
            scratch = [(operands[i].shape, BF) for i in far] + [((width, size), BF)]
            result = queue.run(
                mixer(
                    weight_kernel, terms=len(names), tokens=count, halo=halo, far=far, pieces=pieces
                ),
                ([at] if pieces else []) + operands,
                [((width // chips, 2 * STATE), BF)] * pieces
                + [((width // chips, inner + LANES), BF)] * pieces
                if pieces
                else [((width, size), BF)],
                scratch + [((len(far) + len(names),), None)],
                scalars=1 if pieces else 0,
                far=[i + 1 for i in far] if pieces else far,
                far_out=() if pieces else (0,),
                staged=[len(operands) - 2 + bool(pieces), len(operands) - 1 + bool(pieces)] if halo else (),
                limit=22,
            )
            if pieces:
                return result
            return queue.pass_on(result[0], after)

        rest_names = (("toks", "gz"), ("grows", "act"))
        front_names = (("toks", "graw"),)
        g_rest, g_front = [None] * LAYERS, [None] * LAYERS
        top = LAYERS - 1
        gate_back(top, 0, through=1)
        gate_back(top, 1, [kept[top][0]["dsout"]])
        g_rest[top] = offloaded_sum(weights_back(top, rest_names))
        done_rest, done_front, g_bc = ([None] * LAYERS for _ in range(3))
        for l in reversed(range(LAYERS)):
            ready = [kept[l][1]["dsout"]]
            if l < top:
                ready.append(done_rest[l + 1][1])
            scan_back(l, 0, ready)
            add_cores(l, 0, False)
            ready = sums_of(l, 0) + kept[l][0]["halos"]
            if l < top:
                split_front(l + 1, [g_front[l + 1]], True, True)
                ready += done_front[l + 1]
            scan_back(l, 1, ready)
            own_back(l, 0)
            add_cores(l, 1, False)
            if l == 0:
                values = weights_back(l, front_names, chips)
                direct_bc = direct_start(values[:chips])
                direct = direct_start(values[chips:])
                split_rest(l)
                own_back(l, 1, [v for k in range(1, LAYERS) for v in g_bc[k]])
                split_front(l, direct_bc, False, True)
                split_front(l, direct, True, False, done_rest[0])
            else:
                waiting = sums_of(l, 1) + kept[l][1]["halos"] + arrived[0]
                g_front[l] = offloaded_sum(weights_back(l, front_names, 0, waiting))
                split_rest(l)
                own_back(l, 1)
                gate_back(l - 1, 0, through=1)
                gate_back(l - 1, 1, [kept[l - 1][0]["dsout"]])
                g_rest[l - 1] = offloaded_sum(
                    weights_back(l - 1, rest_names, 0, [done_rest[l][0]])
                )
        grad_in = from_streams(grads)
        output = from_streams(residual[LAYERS])

        names = ("ggain", "sgrad", "hgrad", "gnorm")
        packed = queue.run(
            mixer(pack_kernel, inner=inner, layers=LAYERS),
            [kept[l][s][k] for l in range(LAYERS) for k in names for s in range(2)],
            [((LAYERS, 2 * 8, width), BF)],
        )[0]
        packed = add([back(packed, to_group(0)), back(packed, to_group(1))], F32)
        common = packed[:, 8:].astype(BF)
        common = add([common] + [send(common, route) for route in all_tensor], F32)
        packed = jnp.concatenate([packed[:, :8], common], axis=1)
        low_packed = packed.astype(BF)
        packed = [low_packed] + [send(low_packed, route) for route in all_plane]

        parts = []
        for l in range(LAYERS):
            parts += [*done_rest[l], *done_front[l]]
        smalls = queue.run(
            mixer(
                final_kernel, layers=LAYERS, inner=inner, heads=heads, tensors=n_tensor, chips=chips
            ),
            parts + [v for parts_l in g_bc for v in parts_l] + packed + [hm],
            [(shape, F32) for shape in (
                (LAYERS, shard, inner), (LAYERS, shard, inner), (LAYERS, shard, 2 * STATE),
                (LAYERS, shard, heads), (LAYERS, shard, inner), (LAYERS, 4, inner), (LAYERS, inner),
                (LAYERS, 4, 2 * STATE), (LAYERS, 2 * STATE), (LAYERS, heads), (LAYERS, heads),
                (LAYERS, heads), (LAYERS, inner), (LAYERS, width),
            )],
            limit=20,
        )
        (g_z, g_x, g_shared, g_dt, g_out, g_taps, g_bias, g_taps_bc, g_bias_bc, g_dt_bias, g_log,
         g_skip, g_gate, g_norm) = smalls
        return (
            output, grad_in, g_norm, g_z, g_x, g_shared, g_dt, g_taps, g_bias, g_taps_bc, g_bias_bc,
            g_dt_bias, g_log, g_skip, g_gate, jnp.swapaxes(g_out, 1, 2),
        )

    return local


def solution(mesh):
    n_dp, n_tensor = mesh.shape["dp"], mesh.shape["tensor"]
    tokens = P(("dp", "tensor"), None)
    columns = P(None, "dp", "tensor")
    placed = (
        tokens,
        P("dp"),
        P(),
        columns,
        columns,
        P(None, "dp", None),
        columns,
        P(None, None, "tensor"),
        P(None, "tensor"),
        P(),
        P(),
        P(None, "tensor"),
        P(None, "tensor"),
        P(None, "tensor"),
        P(None, "tensor"),
        P(None, "tensor", "dp"),
        tokens,
    )
    return jax.shard_map(
        build(n_dp, n_tensor),
        mesh=mesh,
        in_specs=placed,
        out_specs=(
            tokens,
            tokens,
            P(),
            columns,
            columns,
            P(None, "dp", None),
            columns,
            P(None, None, "tensor"),
            P(None, "tensor"),
            P(),
            P(),
            P(None, "tensor"),
            P(None, "tensor"),
            P(None, "tensor"),
            P(None, "tensor"),
            P(None, "tensor", "dp"),
        ),
        check_vma=False,
    )
```

```python
import functools

import jax
import jax.numpy as jnp
import numpy as np
from jax import lax
from jax.experimental import pallas as pl
from jax.experimental.pallas import tpu as pltpu
from jax.sharding import PartitionSpec as P

INNER = 3072
HEADDIM = 64
STATE = 128
LAYERS = 2
EPSILON = 1e-05
HALO = 16
CHUNK = 128
LANES = 128

BF = jnp.bfloat16
F32 = jnp.float32
EXACT = lax.Precision.HIGHEST


def dot(left, right, dims=((1,), (0,)), precision=None):
    return lax.dot_general(
        left, right, (dims, ((), ())), preferred_element_type=F32, precision=precision
    )


def split(values):
    high = values.astype(BF)
    return high, (values - high.astype(F32)).astype(BF)


def spread(values, e2_ref):
    return dot(jnp.concatenate(split(values), axis=1), e2_ref[...])


def head_sum(values, hm_ref):
    high, low = split(values)
    return dot(high, hm_ref[...]) + dot(low, hm_ref[...])


def softplus(values):
    return jnp.maximum(values, 0.0) + jnp.log1p(jnp.exp(-jnp.abs(values)))


def triangle(size, lower):
    rows = lax.broadcasted_iota(jnp.int32, (size, size), 0)
    cols = lax.broadcasted_iota(jnp.int32, (size, size), 1)
    return rows >= cols if lower else rows <= cols


def convolve(window, marks, cw, lanes):
    size = window.shape[0] - 8
    total = cw[4:5, lanes] + cw[3:4, lanes] * window[8:]
    for lag in (1, 2, 3):
        earlier = window[8 - lag : 8 - lag + size]
        total = total + cw[3 - lag : 4 - lag, lanes] * (earlier * marks[:, lag - 1 : lag])
    return total


def place(at_ref, j, side, piece, block):
    return pl.multiple_of((at_ref[0] ^ j) * piece + side * block, block)


def fetch_front(at_ref, pieces, w_ref, sems):
    size = pieces[0].shape[0]
    copies = []
    for j, piece in enumerate(pieces):
        row = pl.multiple_of((at_ref[2] ^ j) * size, size) if len(pieces) > 1 else 0
        copies.append(pltpu.make_async_copy(piece, w_ref.at[pl.ds(row, size), :], sems.at[j]))
    for copy in copies:
        copy.start()
    return copies


def start_copy(source, target, sem):
    copy = pltpu.make_async_copy(source, target, sem)
    copy.start()
    return copy


def fetch_rest(rest_ref, low, w_ref, sem):
    copy = pltpu.make_async_copy(rest_ref.at[:, pl.ds(low, w_ref.shape[1])], w_ref, sem)
    copy.start()
    return copy


def front_kernel(*refs, inner, half_size, chips, ready):
    at_ref, refs = refs[0], refs[1:]
    ours, theirs, refs = refs[:half_size], refs[half_size : 2 * half_size], refs[2 * half_size :]
    pieces, refs = refs[:chips], refs[chips:]
    cm_ref, lnk_ref, cw_ref, hp_ref, e2_ref = refs[:5]
    (far_toks_ref, far_raw_ref, head_ref, xb_ref, aux_ref, sloc_ref, tail_ref, edge_ref, send_ref,
     state_ref, raw_ref, w_ref, toks_ref, rawl_ref, sems) = refs[-15:]
    copies = fetch_front(at_ref, pieces, w_ref, sems)
    count = xb_ref.shape[0]
    wide = inner + 2 * STATE
    block = ours[0].shape[0]
    core = at_ref[1]
    toks_ref[:HALO, :] = jnp.zeros((HALO, toks_ref.shape[1]), BF)
    for j in range(half_size):
        for part, side in ((ours[j], core), (theirs[j], 1 - core)):
            row = place(at_ref, j, side, 2 * block, block) + HALO
            toks_ref[pl.ds(pl.multiple_of(row, HALO), block), :] = part[...]
    leaving = [start_copy(toks_ref, far_toks_ref, sems.at[chips])]
    for copy in copies:
        copy.wait()
    for low in range(0, wide + LANES, 2 * LANES):
        lanes = slice(low, min(low + 2 * LANES, wide + LANES))
        raw_ref[:, lanes] = dot(toks_ref[...], w_ref[:, lanes])
        rawl_ref[:, lanes] = raw_ref[:, lanes].astype(BF)
    leaving.append(start_copy(rawl_ref, far_raw_ref, sems.at[chips + 1]))
    head_ref[...] = raw_ref[HALO : 2 * HALO, :wide]
    tail_ref[...] = raw_ref[count + HALO - 8 :, :wide]
    edge_ref[...] = toks_ref[count:, :]
    ready()
    lower = triangle(CHUNK, True).astype(F32)
    state_ref[...] = jnp.zeros_like(state_ref)

    def step_chunk(k, carry):
        base = pl.multiple_of(k * CHUNK, CHUNK)
        here = pl.ds(base, CHUNK)
        marks = cm_ref[pl.ds(base + HALO, CHUNK), :]
        for low in range(0, wide, STATE):
            lanes = slice(low, low + STATE)
            window = raw_ref[pl.ds(base + HALO - 8, CHUNK + 8), lanes]
            pre = convolve(window, marks, cw_ref, lanes)
            xb_ref[here, lanes] = (pre * jax.nn.sigmoid(pre)).astype(BF)
        raw_dt = raw_ref[pl.ds(base + HALO, CHUNK), wide:]
        step = softplus(raw_dt + hp_ref[0:1, :])
        cum = dot(lower, -hp_ref[1:2, :] * step, precision=EXACT)
        aux_ref[here, :LANES] = step
        aux_ref[here, LANES:] = cum
        end = cum[CHUNK - 1 :, :]
        gain = jnp.exp(end - cum) * marks[:, 3:4] * step
        scaled = (spread(gain, e2_ref) * xb_ref[here, :inner].astype(F32)).astype(BF)
        b_rows = xb_ref[here, inner : inner + STATE]
        local = dot(b_rows, scaled, ((0,), (0,)))
        keep = spread(jnp.exp(end) * lnk_ref[pl.ds(k * 8, 8), :], e2_ref)[0:1]
        sloc_ref[k] = state_ref[...].astype(BF)
        state_ref[...] = keep * state_ref[...] + local
        return carry

    lax.fori_loop(0, count // CHUNK, step_chunk, 0)
    send_ref[...] = state_ref[...].astype(BF)
    for copy in leaving:
        copy.wait()


def pair_lanes(values, lane):
    high = values.astype(BF).astype(F32)
    return jnp.where(lane == 0, high, jnp.where(lane == 1, values - high, 0.0)).astype(BF)


def read_pair(tile):
    return tile[:, 0:1].astype(F32) + tile[:, 1:2].astype(F32)


def scan_kernel(*refs, inner, half_size, ready):
    (at_ref, far_toks_ref, old_ref, rest_ref, aux_ref, sloc_ref, send_ref, sin_ref, tail_ref,
     head_ref, cm_ref, segr_ref, lnk_ref, gp_ref, cw_ref, e2_ref) = refs[:16]
    (*far_refs, part_ref, xb_ref, zl_ref, core_ref, act_ref, sst_ref, toks_ref,
     extra_ref, z_ref, wz_ref, wo_ref, sems) = refs[-17:]
    copy_toks = start_copy(far_toks_ref, toks_ref, sems.at[2])
    copy_z = fetch_rest(rest_ref, 0, wz_ref, sems.at[0])
    count = xb_ref.shape[0]
    wide = inner + 2 * STATE
    width = toks_ref.shape[1]
    lower = triangle(CHUNK, True)
    lane = lax.broadcasted_iota(jnp.int32, (CHUNK, STATE), 1)
    first = lane < HEADDIM
    copy_toks.wait()
    copy_z.wait()
    copy_out = fetch_rest(rest_ref, inner, wo_ref, sems.at[1])
    for low in range(0, inner, 2 * LANES):
        lanes = slice(low, min(low + 2 * LANES, inner))
        z_ref[:, lanes] = dot(toks_ref[HALO:, :], wz_ref[:, lanes])
    ready()
    xb_ref[...] = old_ref[...]
    marks = cm_ref[HALO : 2 * HALO, :]
    for low in range(0, wide, STATE):
        lanes = slice(low, low + STATE)
        window = jnp.concatenate([tail_ref[:, lanes], head_ref[:, lanes]], axis=0)
        pre = convolve(window, marks, cw_ref, lanes)
        xb_ref[:HALO, lanes] = (pre * jax.nn.sigmoid(pre)).astype(BF)
    end = aux_ref[CHUNK - 1 : CHUNK, LANES:]
    gain = jnp.exp(end - aux_ref[:HALO, LANES:]) * marks[:, 3:4] * aux_ref[:HALO, :LANES]
    gain = spread(gain, e2_ref)

    def local_state(rows):
        scaled = (gain * rows[:, :inner].astype(F32)).astype(BF)
        return dot(rows[:, inner : inner + STATE], scaled, ((0,), (0,)))

    change = local_state(xb_ref[:HALO, :]) - local_state(old_ref[:HALO, :])
    extra_ref[...] = sin_ref[...].astype(F32)

    def step_chunk(k, carry):
        base = pl.multiple_of(k * CHUNK, CHUNK)
        here = pl.ds(base, CHUNK)
        marks = cm_ref[pl.ds(base + HALO, CHUNK), :]
        incoming = (sloc_ref[k].astype(F32) + extra_ref[...]).astype(BF)
        sst_ref[k] = incoming
        b_rows = xb_ref[here, inner : inner + STATE]
        c_rows = xb_ref[here, inner + STATE : inner + 2 * STATE]
        scores = dot(c_rows, b_rows, ((1,), (1,)))
        allowed = (marks[:, 5:6] == segr_ref[0:1, here]) & lower
        scores = jnp.where(allowed, scores, 0.0)
        step = aux_ref[here, :LANES]
        cum = aux_ref[here, LANES:]
        cum_t = jnp.transpose(cum)
        step_wide = spread(step, e2_ref)
        carried = spread(jnp.exp(cum) * marks[:, 4:5], e2_ref) * dot(c_rows, incoming)
        squares = jnp.zeros((CHUNK, STATE), F32)
        for pair in range(inner // STATE):
            lanes = slice(pair * STATE, (pair + 1) * STATE)
            x_rows = xb_ref[here, lanes].astype(F32)
            scaled = step_wide[:, lanes] * x_rows
            within = carried[:, lanes] + gp_ref[1:2, lanes] * x_rows
            for half in range(2):
                head = 2 * pair + half
                decay = jnp.exp(
                    jnp.minimum(cum[:, head : head + 1] - cum_t[head : head + 1, :], 0.0)
                )
                mine = first if half == 0 else ~first
                part = jnp.where(mine, scaled, 0.0).astype(BF)
                within = within + dot((scores * decay).astype(BF), part)
            core_ref[here, lanes] = within
            z_rows = z_ref[here, lanes]
            zl_ref[here, lanes] = z_rows.astype(BF)
            gated = within * (z_rows * jax.nn.sigmoid(z_rows))
            act_ref[here, lanes] = (gated * gp_ref[0:1, lanes]).astype(BF)
            squares = squares + gated * gated
        part_ref[here, width:] = jnp.where(lane == 0, jnp.sum(squares, axis=1, keepdims=True), 0.0)
        end = cum[CHUNK - 1 :, :]
        keep = spread(jnp.exp(end) * lnk_ref[pl.ds(k * 8, 8), :], e2_ref)[0:1]
        extra_ref[...] = keep * extra_ref[...] + jnp.where(k == 0, change, 0.0)
        return carry

    chunks = count // CHUNK
    lax.fori_loop(0, chunks, step_chunk, 0)
    sst_ref[chunks] = (send_ref[...].astype(F32) + extra_ref[...]).astype(BF)
    here_refs = (xb_ref, zl_ref, core_ref, act_ref, sst_ref)
    leaving = [
        start_copy(near, far, sems.at[3 + i]) for i, (near, far) in enumerate(zip(here_refs, far_refs))
    ]
    copy_out.wait()
    for low in range(0, width, 2 * LANES):
        lanes = slice(low, low + 2 * LANES)
        part_ref[:, lanes] = dot(act_ref[...], wo_ref[lanes, :], ((1,), (1,)))
    for copy in leaving:
        copy.wait()


def sum_kernel(*refs, half_size, offset, noted, ready):
    at_ref, part_ref, came_ref = refs[:3]
    outs = refs[-half_size:] if noted else refs[-half_size - 1 : -1]
    block = outs[0].shape[0]
    width = part_ref.shape[1] - (LANES if noted else 0)
    lane = lax.broadcasted_iota(jnp.int32, (block, LANES), 1)
    for j in range(half_size):
        at = slice(j * block, (j + 1) * block)
        row = place(at_ref, j, at_ref[1], 2 * block, block) + offset
        stay = pl.ds(pl.multiple_of(row, HALO), block)
        total = part_ref[stay, :width] + came_ref[at, :width].astype(F32)
        outs[j][:, :width] = total.astype(outs[j].dtype)
        if noted:
            line = part_ref[stay, width : width + 1] + read_pair(came_ref[at, width:])
            if j == 0:
                outs[j][:, width:] = jnp.where(lane == 0, line, 0.0)
            else:
                outs[j][:, width:] = pair_lanes(line, lane)
    if offset:
        low = half_size * block
        refs[-1][...] = (part_ref[:offset, :] + came_ref[low:, :].astype(F32)).astype(BF)


def normalize(values, gain_ref):
    size = 1.0 / values.shape[1]
    inv_rms = lax.rsqrt(jnp.sum(values * values, axis=1, keepdims=True) * size + EPSILON)
    return values * inv_rms * gain_ref[0:1, :]


def grad_message(msg_ref, grad, mixed, inv_gate):
    width = grad.shape[1]
    scaled = (inv_gate * grad).astype(BF)
    msg_ref[:, :width] = scaled
    weight = jnp.sum(scaled.astype(F32) * mixed, axis=1, keepdims=True)
    lane = lax.broadcasted_iota(jnp.int32, (grad.shape[0], LANES), 1)
    msg_ref[:, width:] = pair_lanes(inv_gate * inv_gate * weight * (1.0 / INNER), lane)


def first_kernel(*refs, ready):
    x_ref, gain_ref = refs[:2]
    res_ref, normed_ref = refs[-2:]
    values = x_ref[...].astype(F32)
    res_ref[...] = values
    normed_ref[...] = normalize(values, gain_ref).astype(BF)


def own_kernel(*refs, half_size, top, ready):
    ready()
    sum_ref, others, refs = refs[0], refs[1:half_size], refs[half_size:]
    res_ref, more_ref = refs[:2]
    mixed_ref, gate_ref, new_ref, msg_ref = refs[-4:]
    width = res_ref.shape[1]
    mixed = sum_ref[:, :width]
    line = sum_ref[:, width : width + 1]
    for other in others:
        mixed = mixed + other[:, :width].astype(F32)
        line = line + read_pair(other[:, width:])
    inv_gate = lax.rsqrt(line * (1.0 / INNER) + EPSILON)
    mixed_ref[...] = mixed
    gate_ref[...] = jnp.broadcast_to(inv_gate, gate_ref.shape)
    values = res_ref[...] + inv_gate * mixed
    new_ref[...] = values
    if top:
        grad_message(msg_ref, more_ref[...], mixed, inv_gate)
    else:
        msg_ref[...] = normalize(values, more_ref).astype(BF)


def own_back_kernel(*refs, half_size, bottom, ready):
    ready()
    sum_ref, others, refs = refs[0], refs[1:half_size], refs[half_size:]
    halos, refs = refs[:half_size], refs[half_size:]
    grad_ref, res_ref, gain_ref = refs[:3]
    if bottom:
        new_ref, gnorm_ref, buf_ref = refs[-3:]
    else:
        mixed_ref, gate_ref = refs[3:5]
        new_ref, gnorm_ref, msg_ref, buf_ref = refs[-4:]
    block = sum_ref.shape[0]
    total = sum_ref[...]
    for other in others:
        total = total + other[...].astype(F32)
    buf_ref[...] = total
    for halo in halos:
        buf_ref[block - HALO :, :] += halo[...].astype(F32)
    total = buf_ref[...]
    values = res_ref[...]
    size = 1.0 / values.shape[1]
    inv_rms = lax.rsqrt(jnp.sum(values * values, axis=1, keepdims=True) * size + EPSILON)
    gnorm = jnp.sum(total * values * inv_rms, axis=0, keepdims=True)
    gnorm_ref[...] = jnp.broadcast_to(gnorm, gnorm_ref.shape)
    scaled = total * gain_ref[0:1, :]
    inner_term = jnp.sum(scaled * values, axis=1, keepdims=True) * size
    grad = grad_ref[...] + inv_rms * scaled - values * (inv_rms * inv_rms * inv_rms) * inner_term
    new_ref[...] = grad
    if not bottom:
        grad_message(msg_ref, grad, mixed_ref[...], gate_ref[:, 0:1])


def gate_back_kernel(*refs, inner, half_size, ready):
    at_ref, refs = refs[0], refs[1:]
    ours, theirs, refs = refs[:half_size], refs[half_size : 2 * half_size], refs[2 * half_size :]
    rest_ref, far_core_ref, far_z_ref, far_xb_ref, aux_ref, cm_ref, lnk_ref, gp_ref, e2_ref = refs[:9]
    (far_grows_ref, gcore_ref, gz_ref, ggain_ref, dsin_ref, state_ref, gg_ref, coef_ref,
     wo_ref, core_ref, z_ref, xb_ref, grows_ref, sems) = refs[-14:]
    copy_out = fetch_rest(rest_ref, inner, wo_ref, sems.at[0])
    count = xb_ref.shape[0]
    chunks = count // CHUNK
    width = grows_ref.shape[1]
    block = ours[0].shape[0]
    core_at = at_ref[1]
    for j in range(half_size):
        for part, side in ((ours[j], core_at), (theirs[j], 1 - core_at)):
            at = pl.ds(place(at_ref, j, side, 2 * block, block), block)
            grows_ref[at, :] = part[:, :width]
            coef_ref[at, :] = jnp.broadcast_to(read_pair(part[:, width:]), (block, LANES))
    leaving = start_copy(grows_ref, far_grows_ref, sems.at[4])
    copies = [
        start_copy(far_core_ref, core_ref, sems.at[1]),
        start_copy(far_z_ref, z_ref, sems.at[2]),
        start_copy(far_xb_ref, xb_ref, sems.at[3]),
    ]
    copy_out.wait()
    for low in range(0, inner, 2 * LANES):
        lanes = slice(low, min(low + 2 * LANES, inner))
        gg_ref[:, lanes] = dot(grows_ref[...], wo_ref[:, lanes])
    for copy in copies:
        copy.wait()
    ready()
    state_ref[...] = jnp.zeros_like(state_ref)
    ggain_ref[...] = jnp.zeros_like(ggain_ref)
    gz_ref[:HALO, :] = jnp.zeros((HALO, inner), BF)

    def step_chunk(turn, carry):
        k = chunks - 1 - turn
        base = pl.multiple_of(k * CHUNK, CHUNK)
        here = pl.ds(base, CHUNK)
        there = pl.ds(pl.multiple_of(base + HALO, HALO), CHUNK)
        marks = cm_ref[there, :]
        coef = coef_ref[here, 0:1]
        cum = aux_ref[here, LANES:]
        entry = spread(jnp.exp(cum) * marks[:, 4:5], e2_ref)
        c_rows = xb_ref[here, inner + STATE : inner + 2 * STATE]
        end = cum[CHUNK - 1 :, :]
        keep = spread(jnp.exp(end) * lnk_ref[pl.ds(k * 8, 8), :], e2_ref)[0:1]
        for pair in range(inner // STATE):
            lanes = slice(pair * STATE, (pair + 1) * STATE)
            z_rows = z_ref[here, lanes].astype(F32)
            core = core_ref[here, lanes]
            grad = gg_ref[here, lanes]
            sig = jax.nn.sigmoid(z_rows)
            act = z_rows * sig
            gated = core * act
            ggain_ref[0:1, lanes] += jnp.sum(grad * gated, axis=0, keepdims=True)
            grad_gated = gp_ref[0:1, lanes] * grad - coef * gated
            gcore = (grad_gated * act).astype(BF)
            gcore_ref[here, lanes] = gcore
            gz_ref[there, lanes] = (
                grad_gated * core * (sig * (1.0 + z_rows * (1.0 - sig)))
            ).astype(BF)
            scaled = (entry[:, lanes] * gcore.astype(F32)).astype(BF)
            state_ref[:, lanes] = keep[:, lanes] * state_ref[:, lanes] + dot(
                c_rows, scaled, ((0,), (0,))
            )
        return carry

    lax.fori_loop(0, chunks, step_chunk, 0)
    dsin_ref[...] = state_ref[...].astype(BF)
    leaving.wait()


def scan_back_kernel(*refs, inner, half_size, chips, ready):
    at_ref, refs = refs[0], refs[1:]
    pieces, refs = refs[:chips], refs[chips:]
    (rest_ref, far_gz_ref, far_raw_ref, far_xb_ref, far_core_ref, far_sst_ref, gcore_ref, aux_ref,
     dso_ref, tail_ref, cm_ref, segr_ref, lnk_ref, gp_ref, cw_ref, hp_ref, e2_ref, hm_ref) = refs[:18]
    (graw_ref, sgrad_ref, hgrad_ref, part_ref, state_ref, dpre_ref, qv_ref, xd_ref,
     raw_ref, wf_ref, wz_ref, xb_ref, core_ref, sst_ref, gz_ref, sems) = refs[-16:]
    first_copies = [
        start_copy(far_xb_ref, xb_ref, sems.at[chips + 2]),
        start_copy(far_sst_ref, sst_ref, sems.at[chips + 3]),
        start_copy(far_core_ref, core_ref, sems.at[chips + 4]),
    ]
    copy_raw = start_copy(far_raw_ref, raw_ref, sems.at[chips])
    count = xb_ref.shape[0]
    chunks = count // CHUNK
    wide = inner + 2 * STATE
    upper = triangle(CHUNK, False)
    first = lax.broadcasted_iota(jnp.int32, (CHUNK, STATE), 1) < HEADDIM
    state_ref[...] = dso_ref[...].astype(F32)
    sgrad_ref[...] = jnp.zeros_like(sgrad_ref)
    hgrad_ref[...] = jnp.zeros_like(hgrad_ref)
    dpre_ref[:HALO, :] = jnp.zeros((HALO, wide), F32)
    dpre_ref[HALO + count :, :] = jnp.zeros((HALO, wide), F32)
    graw_ref[:HALO, wide:] = jnp.zeros((HALO, LANES), BF)

    ready()
    for copy in first_copies:
        copy.wait()
    copy_raw.wait()
    copies = fetch_front(at_ref, pieces, wf_ref, sems)
    copies.append(fetch_rest(rest_ref, 0, wz_ref, sems.at[chips + 1]))
    copies.append(start_copy(far_gz_ref, gz_ref, sems.at[chips + 5]))
    raw_ref[:HALO, :wide] = jnp.concatenate(
        [jnp.zeros((HALO - 8, wide), F32), tail_ref[...]], axis=0
    ).astype(BF)

    def step_chunk(turn, carry):
        k = chunks - 1 - turn
        base = pl.multiple_of(k * CHUNK, CHUNK)
        here = pl.ds(base, CHUNK)
        there = pl.ds(pl.multiple_of(base + HALO, HALO), CHUNK)
        marks = cm_ref[there, :]
        step = aux_ref[here, :LANES]
        cum = aux_ref[here, LANES:]
        cum_t = jnp.transpose(cum)
        end = cum[CHUNK - 1 :, :]
        b_rows = xb_ref[here, inner : inner + STATE]
        c_rows = xb_ref[here, inner + STATE : wide]
        after = state_ref[...]
        after_low = after.astype(BF)
        product = jnp.sum(
            sst_ref[k + 1].astype(F32) * after_low.astype(F32), axis=0, keepdims=True
        )
        at_end = head_sum(jnp.broadcast_to(product, (8, inner)), hm_ref)[0:1]
        scores_t = dot(b_rows, c_rows, ((1,), (1,)))
        allowed = (marks[:, 5:6] == segr_ref[0:1, here]) & upper
        scores_t = jnp.where(allowed, scores_t, 0.0)
        gain = spread(jnp.exp(end - cum) * marks[:, 3:4], e2_ref)
        step_wide = spread(step, e2_ref)
        entry = spread(jnp.exp(cum) * marks[:, 4:5], e2_ref)
        keep = spread(jnp.exp(end) * lnk_ref[pl.ds(k * 8, 8), :], e2_ref)[0:1]
        outer = gain * dot(b_rows, after_low)
        scaled_grad = (entry * gcore_ref[here, :].astype(F32)).astype(BF)
        grad_c = dot(scaled_grad, sst_ref[k], ((1,), (1,)))
        scaled_x = (gain * (step_wide * xb_ref[here, :inner].astype(F32))).astype(BF)
        grad_b = dot(scaled_x, after_low, ((1,), (1,)))
        state_ref[...] = keep * after + dot(c_rows, scaled_grad, ((0,), (0,)))
        grad_scores = jnp.zeros((CHUNK, CHUNK), F32)
        for pair in range(inner // STATE):
            lanes = slice(pair * STATE, (pair + 1) * STATE)
            grad_low = gcore_ref[here, lanes]
            grad = grad_low.astype(F32)
            x_rows = xb_ref[here, lanes].astype(F32)
            wide_step = step_wide[:, lanes]
            scaled = wide_step * x_rows
            grad_u = outer[:, lanes]
            for half in range(2):
                head = 2 * pair + half
                decay = jnp.exp(
                    jnp.minimum(cum_t[head : head + 1, :] - cum[:, head : head + 1], 0.0)
                )
                mine = first if half == 0 else ~first
                part = jnp.where(mine, scaled, 0.0).astype(BF)
                grad_part = jnp.where(mine, grad, 0.0).astype(BF)
                grad_u = grad_u + dot((scores_t * decay).astype(BF), grad_part)
                grad_scores = grad_scores + dot(part, grad_low, ((1,), (1,))) * decay
            skip = gp_ref[1:2, lanes]
            qv_ref[:, lanes] = grad * (core_ref[here, lanes] - skip * x_rows) - (
                scaled.astype(BF).astype(F32) * grad_u
            )
            xd_ref[:, lanes] = x_rows * grad_u
            dpre_ref[there, lanes] = wide_step * grad_u + skip * grad
            sgrad_ref[5:6, lanes] += jnp.sum(grad * x_rows, axis=0, keepdims=True)
        grad_scores = jnp.where(allowed, grad_scores, 0.0).astype(BF)
        dpre_ref[there, inner : inner + STATE] = grad_b + dot(grad_scores, c_rows)
        dpre_ref[there, inner + STATE :] = grad_c + dot(grad_scores, b_rows, ((0,), (0,)))
        rate = hp_ref[1:2, :]
        grad_log = dot(upper.astype(F32), head_sum(qv_ref[...], hm_ref), precision=EXACT) + at_end
        grad_step = head_sum(xd_ref[...], hm_ref) - rate * grad_log
        raw_dt = raw_ref[there, wide:].astype(F32)
        grad_dt = grad_step * jax.nn.sigmoid(raw_dt + hp_ref[0:1, :])
        graw_ref[there, wide:] = grad_dt.astype(BF)
        hgrad_ref[0:1, :] += jnp.sum(grad_dt, axis=0, keepdims=True)
        hgrad_ref[1:2, :] -= rate * jnp.sum(step * grad_log, axis=0, keepdims=True)
        return carry

    lax.fori_loop(0, chunks, step_chunk, 0)

    def conv_chunk(k, carry):
        base = pl.multiple_of(k * CHUNK, CHUNK)
        there = pl.ds(pl.multiple_of(base + HALO, HALO), CHUNK)
        marks = cm_ref[there, :]
        for low in range(0, wide, STATE):
            lanes = slice(low, low + STATE)
            window = raw_ref[pl.ds(base, CHUNK + HALO), lanes].astype(F32)[HALO - 8 :]
            pre = convolve(window, marks, cw_ref, lanes)
            sig = jax.nn.sigmoid(pre)
            grad = dpre_ref[there, lanes] * (sig * (1.0 + pre * (1.0 - sig)))
            dpre_ref[there, lanes] = grad
            sgrad_ref[4:5, lanes] += jnp.sum(grad, axis=0, keepdims=True)
            sgrad_ref[3:4, lanes] += jnp.sum(grad * window[8:], axis=0, keepdims=True)
            for lag in (1, 2, 3):
                earlier = window[8 - lag : 8 - lag + CHUNK]
                sgrad_ref[3 - lag : 4 - lag, lanes] += jnp.sum(
                    grad * (earlier * marks[:, lag - 1 : lag]), axis=0, keepdims=True
                )
        return carry

    lax.fori_loop(0, chunks, conv_chunk, 0)

    def transpose_rows(start, size):
        marks = cm_ref[pl.ds(start, size + 8), :]
        for low in range(0, wide, STATE):
            lanes = slice(low, low + STATE)
            window = dpre_ref[pl.ds(start, size + 8), lanes]
            total = cw_ref[3:4, lanes] * window[:size]
            for lag in (1, 2, 3):
                masked = window[lag : lag + size] * marks[lag : lag + size, lag - 1 : lag]
                total = total + cw_ref[3 - lag : 4 - lag, lanes] * masked
            graw_ref[pl.ds(start, size), lanes] = total.astype(BF)

    transpose_rows(0, HALO)

    def back_chunk(k, carry):
        transpose_rows(pl.multiple_of(k * CHUNK + HALO, HALO), CHUNK)
        return carry

    lax.fori_loop(0, chunks, back_chunk, 0)
    width = part_ref.shape[1]
    for copy in copies:
        copy.wait()
    for low in range(0, width, 2 * LANES):
        lanes = slice(low, low + 2 * LANES)
        part_ref[:, lanes] = dot(gz_ref[...], wz_ref[lanes, :], ((1,), (1,))) + dot(
            graw_ref[...], wf_ref[lanes, :], ((1,), (1,))
        )


def weight_kernel(*refs, terms, tokens, halo, far, pieces, ready):
    refs = list(refs)
    sems = refs.pop()
    at_ref = refs.pop(0) if pieces else None
    out_ref = refs.pop()
    near = refs[-len(far) :]
    outs = refs[len(refs) - len(far) - max(2 * pieces, 1) : len(refs) - len(far)]
    leaving = []
    copies = {}
    sources = {}
    for i, (place_of, target) in enumerate(zip(far, near)):
        sources[place_of] = (refs[place_of], target, sems.at[i])
        refs[place_of] = target
        if i < 4:
            copies[place_of] = start_copy(*sources[place_of])
    ready()
    tile = 2 * LANES
    low = 0
    for term in range(terms):
        left_a, right_a, left_b, right_b = refs[4 * term : 4 * term + 4]
        size = right_a.shape[1]
        for place_of in range(4 * term, 4 * term + 4):
            copies[place_of].wait()
        for place_of in range(4 * term + 4, min(4 * term + 8, len(far))):
            copies[place_of] = start_copy(*sources[place_of])

        def step_tile(r, carry):
            at = pl.ds(pl.multiple_of(r * tile, tile), tile)
            skip_l, skip_r = left_a.shape[0] - tokens, right_a.shape[0] - tokens
            total = dot(left_a[skip_l:, at], right_a[skip_r:, :], ((0,), (0,)))
            total = total + dot(left_b[skip_l:, at], right_b[skip_r:, :], ((0,), (0,)))
            if halo:
                edges = jnp.concatenate([edge[:, at] for edge in refs[4 * terms : 4 * terms + 2]])
                heads = jnp.concatenate([right_a[:HALO, :], right_b[:HALO, :]])
                total = total + dot(edges, heads, ((0,), (0,)))
            out_ref[at, low : low + size] = total.astype(BF)
            return carry

        lax.fori_loop(0, out_ref.shape[0] // tile, step_tile, 0)
        if not pieces:
            lanes = pl.ds(low, size)
            leaving.append(
                start_copy(out_ref.at[:, lanes], outs[0].at[:, lanes], sems.at[len(far) + term])
            )
        low += size
    for copy in leaving:
        copy.wait()
    if pieces:
        for j in range(pieces):
            shared_ref, piece_ref = outs[j], outs[pieces + j]
            size, wide = piece_ref.shape
            row = pl.multiple_of((at_ref[2] ^ j) * size, size)
            rows = pl.ds(row, size)
            inner = wide - LANES
            piece_ref[:, :inner] = out_ref[rows, :inner]
            piece_ref[:, inner:] = out_ref[rows, inner + 2 * STATE :]
            shared_ref[...] = out_ref[rows, inner : inner + 2 * STATE]


def hold_kernel(*refs, ready):
    refs[-1][...] = refs[0][...]


def pick_kernel(*refs, inner, shard, layer, front, rest, ready):
    ready()
    at_ref, one_ref, two_ref = refs[:3]
    outs = refs[-(front + rest) :]
    for side in range(2):
        rows = slice(side * shard, (side + 1) * shard)
        value = jnp.where(at_ref[3] == side, one_ref[...], two_ref[...])
        low = 0
        if front:
            own_ref, other_ref = refs[3:5]
            outs[0][rows, :inner] = value[:, :inner]
            outs[0][rows, inner : inner + 2 * STATE] = jnp.where(
                at_ref[1] == side, own_ref[layer], other_ref[layer]
            )
            outs[0][rows, inner + 2 * STATE :] = value[:, inner : inner + LANES]
            low = inner + LANES
        if rest:
            outs[-1][rows, :] = value[:, low:]


def split_kernel(*refs, terms, shard, inner, front, shared, ready):
    ready()
    at_ref, refs = refs[0], refs[1:]
    buf_ref = refs[-1]
    buf_ref[...] = tree_sum([ref[...] for ref in refs[:terms]])
    half, core = at_ref[3], at_ref[1]
    outs = list(refs[-1 - 2 * (front + shared) : -1])
    if front:
        for out_ref, side in ((outs.pop(0), half), (outs.pop(0), 1 - half)):
            rows = pl.ds(pl.multiple_of(side * shard, HALO), shard)
            if front and shared:
                out_ref[:, :inner] = buf_ref[rows, :inner].astype(BF)
                out_ref[:, inner:] = buf_ref[rows, inner + 2 * STATE :].astype(BF)
            else:
                out_ref[...] = buf_ref[rows, :].astype(BF)
    if shared:
        keep_ref, away_ref = outs
        lanes = slice(inner, inner + 2 * STATE) if front else slice(0, 2 * STATE)
        rows = pl.ds(pl.multiple_of(core * shard, HALO), shard)
        keep_ref[...] = buf_ref[rows, lanes]
        rows = pl.ds(pl.multiple_of((1 - core) * shard, HALO), shard)
        away_ref[...] = buf_ref[rows, lanes].astype(BF)


def final_kernel(*refs, layers, inner, heads, tensors, chips, ready):
    (gz_ref, gx_ref, gbc_ref, gdt_ref, gout_ref, taps_ref, bias_ref, taps_bc_ref, bias_bc_ref,
     dt_ref, log_ref, skip_ref, gate_ref, norm_ref) = refs[-14:]
    low = layers * (4 + tensors)
    small = tree_sum([ref[...] for ref in refs[low : low + chips]])
    hm_ref = refs[low + chips]
    for l in range(layers):
        rest_one, rest_two, front_one, front_two = refs[4 * l : 4 * l + 4]
        total = rest_one[...].astype(F32) + rest_two[...].astype(F32)
        gz_ref[l] = total[:, :inner]
        gout_ref[l] = total[:, inner:]
        total = front_one[...].astype(F32) + front_two[...].astype(F32)
        gx_ref[l] = total[:, :inner]
        gdt_ref[l] = total[:, inner : inner + heads]
        low = 4 * layers + l * tensors
        gbc_ref[l] = tree_sum([ref[...] for ref in refs[low : low + tensors]])
        row = slice(l, l + 1)
        mine = small[l]
        taps_ref[l] = mine[0:4, :inner]
        bias_ref[row, :] = mine[4:5, :inner]
        gate_ref[row, :] = mine[5:6, :inner]
        skips = dot(mine[0:8, :inner], hm_ref[...].astype(F32), precision=EXACT)
        skip_ref[row, :] = skips[6:7, :heads]
        dt_ref[row, :] = mine[7:8, :heads]
        log_ref[row, :] = mine[7:8, LANES : LANES + heads]
        taps_bc_ref[l] = mine[8:12, : 2 * STATE]
        bias_bc_ref[row, :] = mine[12:13, : 2 * STATE]
        norm_ref[row, :] = mine[13:14, :]


def nothing_kernel(*refs):
    pass


def gate_kernel(*refs, terms, ready):
    for source, target in zip(refs[:terms], refs[-terms:]):
        target[...] = source[...]


def away_kernel(*refs, half_size, offset, noted, ready):
    at_ref, part_ref, away_ref = refs[0], refs[1], refs[-1]
    block = (part_ref.shape[0] - offset) // (2 * half_size)
    width = part_ref.shape[1] - (LANES if noted else 0)
    lane = lax.broadcasted_iota(jnp.int32, (block, LANES), 1)
    for j in range(half_size):
        to = slice(j * block, (j + 1) * block)
        row = place(at_ref, j, 1 - at_ref[1], 2 * block, block) + offset
        go = pl.ds(pl.multiple_of(row, HALO), block)
        away_ref[to, :width] = part_ref[go, :width].astype(BF)
        if noted:
            away_ref[to, width:] = pair_lanes(part_ref[go, width : width + 1], lane)
    if offset:
        away_ref[half_size * block :, :] = part_ref[:offset, :].astype(BF)


def touch_kernel(*refs, ready):
    refs[-1][...] = jnp.zeros_like(refs[-1])


def tree_sum(values):
    values = [v.astype(F32) for v in values]
    while len(values) > 1:
        values = [a + b for a, b in zip(values[::2], values[1::2])]
    return values[0]


def add_kernel(*refs, terms, ready):
    refs[-1][...] = tree_sum([ref[...] for ref in refs[:terms]]).astype(refs[-1].dtype)


def pack_kernel(*refs, inner, layers, ready):
    out_ref = refs[-1]
    out_ref[...] = jnp.zeros_like(out_ref)
    for l in range(layers):
        ggain, sgrad, hgrad, gnorm = (
            refs[8 * l + 2 * i][...] + refs[8 * l + 2 * i + 1][...] for i in range(4)
        )
        out_ref[l, 0:5, :inner] = sgrad[0:5, :inner].astype(BF)
        out_ref[l, 5:6, :inner] = ggain[0:1, :].astype(BF)
        out_ref[l, 6:7, :inner] = sgrad[5:6, :inner].astype(BF)
        out_ref[l, 7:8, :LANES] = hgrad[0:1, :].astype(BF)
        out_ref[l, 7:8, LANES : 2 * LANES] = hgrad[1:2, :].astype(BF)
        out_ref[l, 8:13, : 2 * STATE] = sgrad[0:5, inner:].astype(BF)
        out_ref[l, 13:14, :] = gnorm[0:1, :].astype(BF)


class Queue:
    def __init__(self):
        self.last = None

    def run(
        self, kernel, operands, outs, scratch=(), scalars=0, far=(), far_out=(), staged=(),
        staged_out=(), after=(), limit=10,
    ):
        near = pl.BlockSpec(memory_space=pltpu.VMEM)
        distant = pl.BlockSpec(memory_space=pltpu.HBM)
        free = pl.BlockSpec(memory_space=pl.ANY)
        extra = list(after) + ([] if self.last is None else [self.last])
        outside = set(far) | set(staged)
        outside_out = set(far_out) | set(staged_out)
        count, staged, staged_out = len(operands), list(staged), list(staged_out)

        def wrapped(*refs):
            refs = list(refs)
            sems = refs.pop()
            base = count + len(extra)
            buffers = refs[len(refs) - len(staged) - len(staged_out) :]
            refs = refs[: len(refs) - len(buffers)]
            arriving = []
            for i, position in enumerate(staged):
                arriving.append(start_copy(refs[position], buffers[i], sems.at[i]))
                refs[position] = buffers[i]
            leaving = []
            for i, position in enumerate(staged_out, len(staged)):
                leaving.append((buffers[i], refs[base + position], sems.at[i]))
                refs[base + position] = buffers[i]

            def ready():
                for copy in arriving:
                    copy.wait()

            kernel(*refs, ready=ready)
            for copy in [start_copy(*parts) for parts in leaving]:
                copy.wait()

        specs = [pl.BlockSpec(memory_space=pltpu.SMEM)] * scalars
        specs += [distant if i in outside else near for i in range(scalars, count)]
        buffers = [(operands[i].shape, operands[i].dtype) for i in staged]
        buffers += [outs[i] for i in staged_out]
        operands = [
            pltpu.with_memory_space_constraint(v, pltpu.HBM) if i in outside else v
            for i, v in enumerate(operands)
        ]
        result = pl.pallas_call(
            wrapped,
            in_specs=specs + [free] * len(extra),
            out_specs=[distant if i in outside_out else near for i in range(len(outs))],
            out_shape=[
                pltpu.HBM(s, t) if i in outside_out else jax.ShapeDtypeStruct(s, t)
                for i, (s, t) in enumerate(outs)
            ],
            scratch_shapes=[
                pltpu.SemaphoreType.DMA(s) if t is None else pltpu.VMEM(s, t)
                for s, t in [*scratch, *buffers, ((max(len(buffers), 1),), None)]
            ],
            compiler_params=pltpu.CompilerParams(vmem_limit_bytes=limit * 1024 * 1024),
            cost_estimate=pl.CostEstimate(flops=1000, bytes_accessed=1000, transcendentals=0),
        )(*operands, *extra)
        self.last = result[-1]
        return result

    def gate(self, values, after):
        return self.run(
            functools.partial(gate_kernel, terms=len(values)), values,
            [(v.shape, v.dtype) for v in values], after=after,
        )

    def pass_on(self, value, after):
        free = pl.BlockSpec(memory_space=pl.ANY)
        distant = pl.BlockSpec(memory_space=pltpu.HBM)
        extra = list(after) + ([] if self.last is value else [self.last])
        self.last = pl.pallas_call(
            nothing_kernel,
            in_specs=[distant] + [free] * len(extra),
            out_specs=distant,
            out_shape=pltpu.HBM(value.shape, value.dtype),
            input_output_aliases={0: 0},
            cost_estimate=pl.CostEstimate(flops=1000, bytes_accessed=1000, transcendentals=0),
        )(pltpu.with_memory_space_constraint(value, pltpu.HBM), *extra)
        return self.last

    def touch(self, values):
        self.run(touch_kernel, [], [((8, LANES), F32)], after=values)


def build(n_dp, n_tensor):
    axes = ("dp", "tensor")
    half_size = n_tensor // 2
    planes = [[d for d in range(n_dp) if d % 2 == c] for c in range(2)]
    plane_bits = [1 << b for b in range(1, n_dp.bit_length() - 1)]

    def pairs(route):
        found = []
        for d in range(n_dp):
            for t in range(n_tensor):
                goal = route(d, t)
                if goal is not None:
                    found.append((d * n_tensor + t, goal[0] * n_tensor + goal[1]))
        return found

    def send(value, route):
        return lax.ppermute(value, axes, pairs(route))

    def back(value, route):
        return lax.ppermute(value, axes, [(b, a) for a, b in pairs(route)])

    def to_core(d, t):
        return d ^ 1, t

    def to_plane(bits):
        return lambda d, t: (d ^ bits, t)

    def to_tensor(bits):
        return lambda d, t: (d, t ^ bits)

    def to_piece(j):
        return lambda d, t: (d, (t // half_size) * half_size + ((t % half_size) ^ j))

    def to_later(d, t):
        return (d, t + half_size) if t < half_size else None

    def to_halo(j):
        return lambda d, t: (d, half_size + j) if d % 2 == 1 and t == half_size - 1 else None

    def to_group(turn):
        def route(d, t):
            return (d & ~1) | (t % 2), t // 2 + half_size * ((d & 1) ^ turn)

        return route

    def matmul(left, right, dims=((1,), (0,))):
        return lax.dot_general(left, right, (dims, ((), ())), preferred_element_type=F32)

    def local(
        x_in, segments, norm_gain, w_z, w_x, w_bc, w_dt, conv_x, conv_x_bias, conv_bc, conv_bc_bias,
        dt_bias, a_log, d_skip, gate_gain, w_out, cotangent,
    ):
        inner = w_z.shape[2]
        heads = dt_bias.shape[1]
        piece, width = x_in.shape
        block = piece // 2
        count = half_size * piece
        rows = count + HALO
        chunks = count // CHUNK
        shard = w_z.shape[1]
        wide = inner + 2 * STATE
        place = lax.axis_index("tensor")
        dp_place = lax.axis_index("dp")
        core = dp_place % 2
        column = dp_place // 2
        half = place // half_size
        mine = place % half_size

        def cut(value, start, size):
            return lax.dynamic_slice(
                value, (start,) + (0,) * (value.ndim - 1), (size,) + value.shape[1:]
            )

        def put(value, part, start):
            return lax.dynamic_update_slice(value, part, (start,) + (0,) * (value.ndim - 1))

        def to_streams(value):
            keep, away = cut(value, core * block, block), cut(value, (1 - core) * block, block)
            came = send(away, to_core)
            return [jnp.where(core == 0, keep, came), jnp.where(core == 0, came, keep)]

        def from_streams(values):
            keep = jnp.where(core == 0, values[0], values[1])
            came = send(jnp.where(core == 0, values[1], values[0]), to_core)
            out = jnp.zeros((piece, width), F32)
            return put(put(out, keep, core * block), came, (1 - core) * block)

        def pad_lanes(value):
            return jnp.pad(value, ((0, 0), (0, LANES - value.shape[1])))

        queue = Queue()
        at = jnp.stack([mine, core, column, half]).astype(jnp.int32)
        chips = n_dp // 2

        def hold(value, after):
            return queue.run(hold_kernel, [value], [(value.shape, value.dtype)], after=after)[0]

        def regroup(value):
            return [send(value, to_group(0)), send(value, to_group(1))]

        bc_other = send(w_bc, to_core)
        def gather_plane(value):
            return lax.all_gather(value, "dp", axis=0, tiled=True, axis_index_groups=planes)

        def direct_start(values):
            return [values[0]] + [
                send(values[j % len(values)], to_plane(2 * j)) for j in range(1, chips)
            ]

        def pick(parts, l, front, rest, after=(), direct=False):
            outs = []
            if front:
                outs.append(((2 * shard, wide + LANES), BF))
            if rest:
                outs.append(((2 * shard, 2 * inner), BF))
            values = queue.run(
                functools.partial(
                    pick_kernel, inner=inner, shard=shard, layer=l, front=front, rest=rest
                ),
                [at, *parts] + ([w_bc, bc_other] if front else []),
                outs,
                scalars=1,
                after=after,
                staged_out=range(len(outs)),
            )
            if direct:
                front_w[l] = direct_start(values)
                return
            values = [gather_plane(v) for v in values]
            if front:
                front_w[l] = [values[0]]
            if rest:
                rest_w[l] = values[-1]

        def front_part(l):
            return [w_x[l], pad_lanes(w_dt[l])]

        def rest_part(l):
            return [w_z[l], w_out[l].T]

        def row(value, size):
            return jnp.pad(value, ((0, 0), (0, size - value.shape[1])))[:, None]

        head_rows = jnp.concatenate([row(v, LANES) for v in (dt_bias, a_log, d_skip)], axis=2)
        head_rows = jnp.pad(head_rows, ((0, 0), (0, 0), (0, inner - 3 * LANES)))
        packed = jnp.concatenate(
            [conv_x, conv_x_bias[:, None], gate_gain[:, None], head_rows], axis=1
        )
        packed = send(packed, to_group(0))
        taps, bias, gain_own = packed[:, :4], packed[:, 4:5], packed[:, 5:6]
        dt_own, a_own, skip_own = (packed[:, 6, i * LANES : (i + 1) * LANES] for i in range(3))
        head_ok = jnp.arange(LANES) < heads
        rate_own = jnp.where(head_ok, jnp.exp(a_own), 0.0)
        skip_wide = jnp.repeat(skip_own[:, :heads], HEADDIM, axis=1)
        conv_w = jnp.concatenate(
            [
                jnp.concatenate([taps, conv_bc], axis=2),
                jnp.concatenate([bias, conv_bc_bias[:, None]], axis=2),
                jnp.zeros((LAYERS, 3, wide), F32),
            ],
            axis=1,
        )
        gate_p = jnp.concatenate(
            [gain_own, skip_wide[:, None], jnp.zeros((LAYERS, 6, inner), F32)], axis=1
        )
        head_p = jnp.concatenate(
            [dt_own[:, None], rate_own[:, None], jnp.zeros((LAYERS, 6, LANES), F32)], axis=1
        )
        member = np.arange(inner)[None, :] // HEADDIM == np.arange(LANES)[:, None]
        e2 = jnp.asarray(np.concatenate([member, member], axis=0), BF)
        hm = jnp.asarray(member.T, BF)

        seg = jnp.concatenate([jnp.full((HALO,), -1.0, F32), segments.astype(F32)])
        seg = cut(seg, half * count, rows)
        seg_other = send(seg, to_core)
        seg = jnp.stack([jnp.where(core == 0, seg, seg_other), jnp.where(core == 0, seg_other, seg)])
        tokens = seg[:, HALO:]
        lagged = [
            (tokens == seg[:, HALO - k : HALO - k + count]).astype(F32) for k in (1, 2, 3)
        ]
        by_chunk = tokens.reshape(2, chunks, CHUNK)
        last = by_chunk[:, :, -1]
        before = jnp.concatenate([seg[:, HALO - 1 : HALO], last[:, :-1]], axis=1)
        stays = (by_chunk == last[:, :, None]).astype(F32).reshape(2, count)
        enters = (by_chunk == before[:, :, None]).astype(F32).reshape(2, count)
        marks = jnp.stack(lagged + [stays, enters, tokens, tokens, tokens], axis=-1)
        marks = jnp.pad(marks, ((0, 0), (HALO, HALO), (0, 0)))
        seg_row = jnp.broadcast_to(tokens[:, None, :], (2, 8, count))
        links = (last == before).astype(F32)
        links = jnp.broadcast_to(links[:, :, None, None], (2, chunks, 8, LANES))
        links = links.reshape(2, chunks * 8, LANES)

        def exchange(value):
            return [value] + [send(value, to_piece(j)) for j in range(1, half_size)]

        def share(ours):
            return ours + [send(part, to_core) for part in ours]

        def pieces(values):
            return [send(values[j], to_piece(j)) for j in range(1, half_size)]

        mixer = functools.partial
        sizes = dict(inner=inner, half_size=half_size)
        noted = width + LANES
        gains = [jnp.broadcast_to(norm_gain[l][None], (8, width)) for l in range(LAYERS)]

        front_w, rest_w = [None] * LAYERS, [None] * LAYERS
        parts = regroup(jnp.concatenate(front_part(0), axis=1))
        start = to_streams(x_in)
        grads = to_streams(cotangent)
        residual = [[None, None] for _ in range(LAYERS + 1)]
        normed = [None, None]
        kept = [[{}, {}] for _ in range(LAYERS)]
        arrived = [None, None]

        def spread_tokens(s):
            arrived[s] = exchange(normed[s])

        def front(l, s, after=()):
            parts = [at, *share(arrived[s]), *front_w[l]]
            chips = len(front_w[l])
            (toks, raw, head, xb, aux, sloc, tail, edge, ends) = queue.run(
                mixer(front_kernel, chips=chips, **sizes),
                [*parts, marks[s], links[s], conv_w[l], head_p[l], e2],
                [((rows, width), BF), ((rows, wide + LANES), BF), ((HALO, wide), F32),
                 ((count, wide), BF), ((count, 2 * LANES), F32), ((chunks, STATE, inner), BF),
                 ((8, wide), F32), ((HALO, width), BF), ((STATE, inner), BF)],
                [((STATE, inner), F32), ((rows, wide + LANES), F32),
                 ((n_dp * shard, wide + LANES), BF), ((rows, width), BF),
                 ((rows, wide + LANES), BF), ((chips + 2,), None)],
                scalars=1,
                far=range(len(parts) - chips, len(parts)),
                far_out=(0, 1),
                staged=range(len(parts), len(parts) + 5),
                staged_out=(2, 3, 4, 5),
                limit=20,
            )
            tail, edge, ends = queue.gate([tail, edge, ends], after)
            kept[l][s].update(
                toks=toks, raw=raw, head=head, xb=xb, aux=aux, sloc=sloc, ends=ends,
                tail=send(tail, to_later), edge=send(edge, to_later), begins=send(ends, to_later),
            )

        def states(l, s):
            return [kept[l][s][k] for k in ("begins", "tail", "edge")]

        def scan(l, s, after=()):
            v = kept[l][s]
            (xb, z, core_out, act, sst, part) = queue.run(
                mixer(scan_kernel, **sizes),
                [at, v["toks"], v["xb"], rest_w[l], v["aux"], v["sloc"], v["ends"], v["begins"],
                 v["tail"], v["head"], marks[s], seg_row[s], links[s], gate_p[l], conv_w[l], e2],
                [((count, wide), BF), ((count, inner), BF), ((count, inner), F32),
                 ((count, inner), BF), ((chunks + 1, STATE, inner), BF),
                 ((count, noted), F32)],
                [((count, wide), BF), ((count, inner), BF), ((count, inner), F32),
                 ((count, inner), BF), ((chunks + 1, STATE, inner), BF), ((rows, width), BF),
                 ((STATE, inner), F32), ((count, inner), F32), ((n_dp * shard, inner), BF),
                 ((n_dp * shard, inner), BF), ((8,), None)],
                scalars=1,
                after=[v["edge"]],
                far=(1, 3),
                far_out=range(5),
                staged=[2, 4, 5, 9, *range(10, 16)],
                limit=26,
            )
            v.update(xb=xb, z=z, core_out=core_out, act=act, sst=sst)
            send_away(v, part, 0, after)

        def send_away(v, part, offset, after):
            size = part.shape[1]
            away = queue.run(
                mixer(away_kernel, half_size=half_size, offset=offset, noted=offset == 0),
                [at, part], [((half_size * block + offset, size), BF)], scalars=1, after=after,
            )[0]
            v["sum"] = (part, send(away, to_core))

        def add_cores(l, s, has_note, after=()):
            part, came = kept[l][s]["sum"]
            size = part.shape[1]
            sums = queue.run(
                mixer(
                    sum_kernel, half_size=half_size, noted=has_note, offset=0 if has_note else HALO
                ),
                [at, part, came],
                [((block, size), F32)] + [((block, size), BF)] * (half_size - 1)
                + ([] if has_note else [((HALO, size), BF)]),
                scalars=1,
                after=after,
            )
            kept[l][s]["pieces"] = [sums[0]] + pieces(sums)
            if not has_note:
                kept[l][s]["halos"] = [back(sums[-1], to_halo(j)) for j in range(half_size)]

        def own(l, s):
            top = l == LAYERS - 1
            v = kept[l][s]
            mixed, gate, new, msg = queue.run(
                mixer(own_kernel, half_size=half_size, top=top),
                [*v["pieces"], residual[l][s], grads[s] if top else gains[l + 1]],
                [((block, width), F32), ((block, LANES), F32), ((block, width), F32),
                 ((block, noted if top else width), BF)],
                staged=(half_size, half_size + 1),
                staged_out=(0, 1, 2),
            )
            v.update(mixed=mixed, gate=gate)
            residual[l + 1][s] = new
            if top:
                arrived[s] = exchange(msg)
            else:
                normed[s] = msg
                spread_tokens(s)

        for s in range(2):
            residual[0][s], normed[s] = queue.run(
                first_kernel, [start[s], gains[0]], [((block, width), F32), ((block, width), BF)],
                staged_out=(0,),
            )
            spread_tokens(s)
        def sums_of(l, s):
            return kept[l][s]["pieces"][1:]

        pick(parts, 0, True, False)
        parts = regroup(hold(jnp.concatenate(rest_part(0), axis=1), []))
        pick(parts, 0, False, True, [*arrived[0], *arrived[1]])
        parts = [
            regroup(hold(jnp.concatenate(front_part(l) + rest_part(l), axis=1), []))
            for l in range(1, LAYERS)
        ]
        queue.touch([marks, seg_row, links, conv_w, gate_p, head_p])
        front(0, 0)
        front(0, 1, states(0, 0))
        for l in range(1, LAYERS):
            pick(parts[l - 1], l, True, True)
        for l in range(LAYERS):
            if l > 0:
                front(l, 1, states(l, 0))
            scan(l, 0, states(l, 1))
            add_cores(l, 0, True)
            scan(l, 1, sums_of(l, 0))
            own(l, 0)
            add_cores(l, 1, True)
            if l + 1 < LAYERS:
                front(l + 1, 0, sums_of(l, 1))
            own(l, 1)

        def owners(messages):
            return [back(messages[0], to_group(0)), back(messages[1], to_group(1))]

        def split_rest(l, after=()):
            messages = queue.run(
                mixer(split_kernel, terms=1, shard=shard, inner=inner, front=True, shared=False),
                [at, g_rest[l]],
                [((shard, 2 * inner), BF)] * 2,
                [(g_rest[l].shape, F32)],
                scalars=1,
                after=after,
                staged=(1,),
                limit=14,
            )
            done_rest[l] = owners(messages)

        def share_bc(l, keep, away):
            shared = (keep + send(away, to_core).astype(F32)).astype(BF)
            g_bc[l] = [shared] + [send(shared, route) for route in all_tensor]

        def split_front(l, values, front, shared, after=()):
            size = inner + LANES
            outs = [((shard, size), BF)] * 2 if front else []
            outs += [((shard, 2 * STATE), F32), ((shard, 2 * STATE), BF)] if shared else []
            outs = queue.run(
                mixer(
                    split_kernel, terms=len(values), shard=shard, inner=inner, front=front,
                    shared=shared,
                ),
                [at, *values], outs, [(values[0].shape, F32)], scalars=1, after=after, limit=14,
            )
            if front:
                done_front[l] = owners(outs[:2])
            if shared:
                share_bc(l, *outs[-2:])

        def offloaded_sum(value):
            return lax.psum_scatter(
                value, "dp", scatter_dimension=0, tiled=True, axis_index_groups=planes
            )

        def add(parts, kind):
            return queue.run(
                mixer(add_kernel, terms=len(parts)), parts, [(parts[0].shape, kind)]
            )[0]

        all_tensor = [to_tensor(j) for j in range(1, n_tensor)]
        all_plane = [to_plane(2 * j) for j in range(1, n_dp // 2)]

        def gate_back(l, s, after=(), through=None):
            v = kept[l][s]
            (grows, gcore, gz, ggain, dsin) = queue.run(
                mixer(gate_back_kernel, **sizes),
                [at, *share(arrived[s]), rest_w[l], v["core_out"], v["z"], v["xb"], v["aux"], marks[s],
                 links[s], gate_p[l], e2],
                [((count, width), BF), ((count, inner), BF), ((rows, inner), BF), ((8, inner), F32),
                 ((STATE, inner), BF)],
                [((STATE, inner), F32), ((count, inner), F32), ((count, LANES), F32),
                 ((n_dp * shard, inner), BF), ((count, inner), F32), ((count, inner), BF),
                 ((count, wide), BF), ((count, width), BF), ((5,), None)],
                scalars=1,
                far=range(1 + 2 * half_size, 5 + 2 * half_size),
                far_out=(0,),
                staged_out=(1, 2),
                staged=range(5 + 2 * half_size, 10 + 2 * half_size),
                limit=20,
            )
            moved = [] if through is None else arrived[through][1:]
            dsin, *moved = queue.gate([dsin, *moved], after)
            if through is not None:
                arrived[through] = arrived[through][:1] + moved
            v.update(grows=grows, gcore=gcore, gz=gz, ggain=ggain, dsout=back(dsin, to_later))

        def scan_back(l, s, after=()):
            v = kept[l][s]
            chips = len(front_w[l])
            (graw, sgrad, hgrad, part) = queue.run(
                mixer(scan_back_kernel, chips=chips, **sizes),
                [at, *front_w[l], rest_w[l], v["gz"], v["raw"], v["xb"], v["core_out"], v["sst"],
                 v["gcore"], v["aux"], v["dsout"], v["tail"], marks[s], seg_row[s], links[s],
                 gate_p[l], conv_w[l], head_p[l], e2, hm],
                [((rows, wide + LANES), BF), ((8, wide), F32), ((8, LANES), F32),
                 ((rows, width), F32)],
                [((STATE, inner), F32), ((count + 2 * HALO, wide), F32), ((CHUNK, inner), F32),
                 ((CHUNK, inner), F32), ((rows, wide + LANES), BF),
                 ((n_dp * shard, wide + LANES), BF), ((n_dp * shard, inner), BF),
                 ((count, wide), BF), ((count, inner), F32), ((chunks + 1, STATE, inner), BF),
                 ((rows, inner), BF), ((chips + 6,), None)],
                scalars=1,
                far=range(1, chips + 7),
                staged=[chips + 7, chips + 8, *range(chips + 10, chips + 19)],
                staged_out=(0,),
                limit=30,
            )
            send_away(v, part, HALO, after)
            v.update(graw=graw, sgrad=sgrad, hgrad=hgrad)

        def own_back(l, s, after=()):
            v = kept[l][s]
            bottom = l == 0
            before = [] if bottom else [kept[l - 1][s]["mixed"], kept[l - 1][s]["gate"]]
            result = queue.run(
                mixer(own_back_kernel, half_size=half_size, bottom=bottom),
                [*v["pieces"], *v["halos"], grads[s], residual[l][s], gains[l], *before],
                [((block, width), F32), ((8, width), F32)]
                + ([] if bottom else [((block, noted), BF)]),
                [((block, width), F32)],
                after=after,
                staged=range(2 * half_size, 2 * half_size + 3 + len(before)),
                staged_out=(0,),
            )
            grads[s], v["gnorm"] = result[:2]
            if not bottom:
                arrived[s] = exchange(result[2])

        def weights_back(l, names, pieces=0, after=()):
            one, two = kept[l]
            operands = []
            for left, right in names:
                operands += [one[left], one[right], two[left], two[right]]
            size = sum(one[right].shape[1] for _, right in names)
            halo = len(names) == 1
            if halo:
                operands += [one["edge"], two["edge"]]
            far = range(4 * len(names))
            scratch = [(operands[i].shape, BF) for i in far] + [((width, size), BF)]
            result = queue.run(
                mixer(
                    weight_kernel, terms=len(names), tokens=count, halo=halo, far=far, pieces=pieces
                ),
                ([at] if pieces else []) + operands,
                [((width // chips, 2 * STATE), BF)] * pieces
                + [((width // chips, inner + LANES), BF)] * pieces
                if pieces
                else [((width, size), BF)],
                scratch + [((len(far) + len(names),), None)],
                scalars=1 if pieces else 0,
                far=[i + 1 for i in far] if pieces else far,
                far_out=() if pieces else (0,),
                staged=[len(operands) - 2 + bool(pieces), len(operands) - 1 + bool(pieces)] if halo else (),
                limit=22,
            )
            if pieces:
                return result
            return queue.pass_on(result[0], after)

        rest_names = (("toks", "gz"), ("grows", "act"))
        front_names = (("toks", "graw"),)
        g_rest, g_front = [None] * LAYERS, [None] * LAYERS
        top = LAYERS - 1
        gate_back(top, 0, through=1)
        gate_back(top, 1, [kept[top][0]["dsout"]])
        g_rest[top] = offloaded_sum(weights_back(top, rest_names))
        done_rest, done_front, g_bc = ([None] * LAYERS for _ in range(3))
        for l in reversed(range(LAYERS)):
            ready = [kept[l][1]["dsout"]]
            if l < top:
                ready.append(done_rest[l + 1][1])
            scan_back(l, 0, ready)
            add_cores(l, 0, False)
            ready = sums_of(l, 0) + kept[l][0]["halos"]
            if l < top:
                split_front(l + 1, [g_front[l + 1]], True, True)
                ready += done_front[l + 1]
            scan_back(l, 1, ready)
            own_back(l, 0)
            add_cores(l, 1, False)
            if l == 0:
                values = weights_back(l, front_names, chips)
                direct_bc = direct_start(values[:chips])
                direct = direct_start(values[chips:])
                split_rest(l)
                own_back(l, 1, [v for k in range(1, LAYERS) for v in g_bc[k]])
                split_front(l, direct_bc, False, True)
                split_front(l, direct, True, False, done_rest[0])
            else:
                waiting = sums_of(l, 1) + kept[l][1]["halos"] + arrived[0]
                g_front[l] = offloaded_sum(weights_back(l, front_names, 0, waiting))
                split_rest(l)
                own_back(l, 1)
                gate_back(l - 1, 0, through=1)
                gate_back(l - 1, 1, [kept[l - 1][0]["dsout"]])
                g_rest[l - 1] = offloaded_sum(
                    weights_back(l - 1, rest_names, 0, [done_rest[l][0]])
                )
        grad_in = from_streams(grads)
        output = from_streams(residual[LAYERS])

        names = ("ggain", "sgrad", "hgrad", "gnorm")
        packed = queue.run(
            mixer(pack_kernel, inner=inner, layers=LAYERS),
            [kept[l][s][k] for l in range(LAYERS) for k in names for s in range(2)],
            [((LAYERS, 2 * 8, width), BF)],
        )[0]
        packed = add([back(packed, to_group(0)), back(packed, to_group(1))], F32)
        common = packed[:, 8:].astype(BF)
        common = add([common] + [send(common, route) for route in all_tensor], F32)
        packed = jnp.concatenate([packed[:, :8], common], axis=1)
        low_packed = packed.astype(BF)
        packed = [low_packed] + [send(low_packed, route) for route in all_plane]

        parts = []
        for l in range(LAYERS):
            parts += [*done_rest[l], *done_front[l]]
        smalls = queue.run(
            mixer(
                final_kernel, layers=LAYERS, inner=inner, heads=heads, tensors=n_tensor, chips=chips
            ),
            parts + [v for parts_l in g_bc for v in parts_l] + packed + [hm],
            [(shape, F32) for shape in (
                (LAYERS, shard, inner), (LAYERS, shard, inner), (LAYERS, shard, 2 * STATE),
                (LAYERS, shard, heads), (LAYERS, shard, inner), (LAYERS, 4, inner), (LAYERS, inner),
                (LAYERS, 4, 2 * STATE), (LAYERS, 2 * STATE), (LAYERS, heads), (LAYERS, heads),
                (LAYERS, heads), (LAYERS, inner), (LAYERS, width),
            )],
            limit=20,
        )
        (g_z, g_x, g_shared, g_dt, g_out, g_taps, g_bias, g_taps_bc, g_bias_bc, g_dt_bias, g_log,
         g_skip, g_gate, g_norm) = smalls
        return (
            output, grad_in, g_norm, g_z, g_x, g_shared, g_dt, g_taps, g_bias, g_taps_bc, g_bias_bc,
            g_dt_bias, g_log, g_skip, g_gate, jnp.swapaxes(g_out, 1, 2),
        )

    return local


def solution(mesh):
    n_dp, n_tensor = mesh.shape["dp"], mesh.shape["tensor"]
    tokens = P(("dp", "tensor"), None)
    columns = P(None, "dp", "tensor")
    placed = (
        tokens,
        P("dp"),
        P(),
        columns,
        columns,
        P(None, "dp", None),
        columns,
        P(None, None, "tensor"),
        P(None, "tensor"),
        P(),
        P(),
        P(None, "tensor"),
        P(None, "tensor"),
        P(None, "tensor"),
        P(None, "tensor"),
        P(None, "tensor", "dp"),
        tokens,
    )
    return jax.shard_map(
        build(n_dp, n_tensor),
        mesh=mesh,
        in_specs=placed,
        out_specs=(
            tokens,
            tokens,
            P(),
            columns,
            columns,
            P(None, "dp", None),
            columns,
            P(None, None, "tensor"),
            P(None, "tensor"),
            P(),
            P(),
            P(None, "tensor"),
            P(None, "tensor"),
            P(None, "tensor"),
            P(None, "tensor"),
            P(None, "tensor", "dp"),
        ),
        check_vma=False,
    )
```
